32 devices in a mesh: node: 16 (over z, x, core), term: 2 (over y).
Axes of the slice: x: 2, y: 2, z: 4, core: 2. Of those that a mesh axis runs over, the one named last changes fastest.
Arguments:
- node_tensors: bfloat16 [16, 64, 4096], P('node'), may hold values from -0.046875 to 1.046875
- prim_ops: bfloat16 [16, 8, 2, 64, 64], P('node', 'term'), may hold values from -3.8 to 3.8, as said below
- active: int32 [16, 8, 2], P('node', 'term'), may hold values 0 or 1
- top_field: bfloat16 [8, 64, 64], P('term'), may hold values from -0.95 to 0.95, as said below
- node_map: int32 [16], replicated, may hold values from 0 to 15, as said below
Outputs:
- derivative: bfloat16 [16, 64, 4096], P('node', 'term')
The draws below stay inside these ranges and needn't reach their ends.
Inputs may be any that keep to these rules, and one draw needn't show every extreme that they name: node_map holds every position 0 to 15 once; position 15 is no node; the slot of position 1 is the slot of position 0 plus 16 // 2, counted round. `prim_ops`: each operator is symmetric. `top_field`: each matrix is symmetric.
All inputs are finite; a program needn't handle non-finite values. No bound on the sum of `active` on one device may be relied on, other than what follows from the above.
Results may differ from the reference program's by a relative error of at most 0.025.
The reference program's roundings to bfloat16 on the way count: a program that leaves them out, or rounds other values in their place, can miss the bound.
Values may be sent and summed in bfloat16 or wider, within the bound.
No kernel may reach another device: no remote copies, remote signals or barrier semaphores. Data moves between devices by JAX's collectives and lax.ppermute only.
A program may use at most 64 MiB of HBM per device.

```python
import jax
import jax.numpy as jnp
from jax import lax

B = 64
TERM_DEV = 4
TERMS = 8
SLOTS = 16


def draw_node_tensors(key, part):
    key_noise = jax.random.fold_in(key, 11)
    key_place = jax.random.fold_in(key, 12)
    noise = jax.random.truncated_normal(key_noise, -4.0, 4.0, (SLOTS, B * B, B), jnp.float32) * (0.7 / B)
    place_keys = jax.random.split(key_place, SLOTS)
    chosen = jax.vmap(lambda single: jax.random.permutation(single, B * B)[:B])(place_keys)
    cells = jnp.arange(B * B, dtype=jnp.int32)
    aligned = (cells[None, :, None] == chosen[:, None, :]).astype(jnp.float32)
    return (aligned + noise).reshape(SLOTS, B, B * B).astype(jnp.bfloat16)


def draw_prim_ops(key, part):
    key_main = jax.random.fold_in(key, 21)
    raw = jax.random.truncated_normal(key_main, -4.0, 4.0, (SLOTS, TERMS, 2, B, B), jnp.float32)
    return ((raw + jnp.swapaxes(raw, -1, -2)) * (0.67 / 1.4143)).astype(jnp.bfloat16)


def draw_top_field(key, part):
    key_main = jax.random.fold_in(key, 31)
    raw = jax.random.truncated_normal(key_main, -4.0, 4.0, (TERMS, B, B), jnp.float32)
    return ((raw + jnp.swapaxes(raw, -1, -2)) * (0.16 / 1.4143)).astype(jnp.bfloat16)


def draw_node_map(key, part):
    key_main = jax.random.fold_in(key, 41)
    shuffled = jax.random.permutation(key_main, SLOTS).astype(jnp.int32)
    slot_ids = jnp.arange(SLOTS, dtype=jnp.int32)
    root_slot = jnp.sum(jnp.where(shuffled == 0, slot_ids, 0))
    target = (root_slot + SLOTS // 2) % SLOTS
    displaced = jnp.sum(jnp.where(slot_ids == target, shuffled, 0))
    moved = jnp.where(shuffled == 1, displaced, shuffled)
    return jnp.where(slot_ids == target, 1, moved).astype(jnp.int32)


def plant(entries, key, least, top_value):
    longest = entries.shape.index(max(entries.shape))
    spots = []
    for shift in (0, 1):
        where = [jax.random.randint(jax.random.fold_in(key, axis), (), 0, length) for axis, length in enumerate(entries.shape)]
        where[longest] = (where[longest] + shift) % entries.shape[longest]
        spots.append(tuple(where))
    return entries.at[spots[0]].set(least).at[spots[1]].set(top_value)


def setup_inputs(seed: int = 0) -> dict:
    splits = jax.random.split(jax.random.key(seed), 6)
    return {
        "node_tensors": draw_node_tensors(jax.random.fold_in(splits[5], 71), 0),
        "prim_ops": draw_prim_ops(jax.random.fold_in(splits[5], 71), 0),
        "active": plant((jax.random.randint(splits[2], (SLOTS, TERMS, 2), 0, 4) < 3).astype(jnp.int32), jax.random.fold_in(splits[2], 1), 0, 1),
        "top_field": draw_top_field(jax.random.fold_in(splits[5], 71), 0),
        "node_map": draw_node_map(jax.random.fold_in(splits[5], 71), 0),
    }


def mode_one(matrix, tensor):
    extent = tensor.shape[0]
    return jnp.dot(matrix, tensor.reshape(extent, -1), preferred_element_type=jnp.float32).reshape(tensor.shape)


def mode_two(matrix, tensor):
    return jnp.einsum("ij,ajc->aic", matrix.astype(jnp.float32), tensor.astype(jnp.float32))


def mode_three(matrix, tensor):
    extent = tensor.shape[2]
    return jnp.dot(tensor.reshape(-1, extent), matrix.T, preferred_element_type=jnp.float32).reshape(tensor.shape)


def up_term(tensor, left_term, right_term):
    extent = tensor.shape[2]
    partial_one = mode_two(right_term, tensor).astype(jnp.bfloat16)
    weighted = mode_one(left_term, partial_one).astype(jnp.bfloat16)
    return jnp.dot(tensor.reshape(-1, extent).T, weighted.reshape(-1, extent), preferred_element_type=jnp.float32).astype(jnp.bfloat16)


def down_term(tensor, left_term, right_term, field_now):
    extent = tensor.shape[0]
    reduced = mode_three(field_now, tensor).astype(jnp.bfloat16)
    side_left = mode_two(right_term, reduced).astype(jnp.bfloat16)
    side_right = mode_one(left_term, reduced).astype(jnp.bfloat16)
    field_left = jnp.dot(tensor.reshape(extent, -1), side_left.reshape(extent, -1).T, preferred_element_type=jnp.float32).astype(jnp.bfloat16)
    field_right = jnp.einsum("abc,adc->bd", tensor.astype(jnp.float32), side_right.astype(jnp.float32)).astype(jnp.bfloat16)
    deriv_term = mode_one(left_term, side_left)
    return field_left, field_right, deriv_term


def reference(node_tensors, prim_ops, active, top_field, node_map):
    slots = node_map.shape[0]
    count = slots - 1
    first_leaf = count // 2
    extent = node_tensors.shape[1]
    terms_all = top_field.shape[0]
    groups = terms_all // TERM_DEV
    inverse = jnp.zeros((slots,), jnp.int32).at[node_map].set(jnp.arange(slots, dtype=jnp.int32))
    identity = jnp.eye(extent, dtype=jnp.bfloat16)

    def tensor_at(place):
        return node_tensors[inverse[place]].reshape(extent, extent, extent)

    def children_of(place, term_mats):
        if place >= first_leaf:
            slot_here = inverse[place]
            operators = jnp.where(active[slot_here][..., None, None] == 1, prim_ops[slot_here], identity)
            return operators[:, 0], operators[:, 1]
        return term_mats[2 * place + 1], term_mats[2 * place + 2]

    term_mats = {}
    for place in range(count - 1, 0, -1):
        tensor_here = tensor_at(place)
        left_terms, right_terms = children_of(place, term_mats)
        term_mats[place] = lax.map(lambda pair: up_term(tensor_here, pair[0], pair[1]), (left_terms, right_terms))

    fields = {0: top_field}
    result = jnp.zeros((slots, extent, extent * extent), jnp.bfloat16)
    for place in range(count):
        tensor_here = tensor_at(place)
        left_terms, right_terms = children_of(place, term_mats)
        field_here = fields[place]

        def group_step(total, items):
            parts = jnp.zeros((extent, extent, extent), jnp.float32)
            lefts = []
            rights = []
            for inner in range(TERM_DEV):
                field_left, field_right, deriv_term = down_term(tensor_here, items[0][inner], items[1][inner], items[2][inner])
                parts = parts + deriv_term
                lefts.append(field_left)
                rights.append(field_right)
            rounded = lax.optimization_barrier(parts.astype(jnp.bfloat16))
            return total + rounded.astype(jnp.float32), (jnp.stack(lefts), jnp.stack(rights))

        shaped = (left_terms.reshape(groups, TERM_DEV, extent, extent),
                  right_terms.reshape(groups, TERM_DEV, extent, extent),
                  field_here.reshape(groups, TERM_DEV, extent, extent))
        total, (lefts_all, rights_all) = lax.scan(group_step, jnp.zeros((extent, extent, extent), jnp.float32), shaped)
        if place < first_leaf:
            fields[2 * place + 1] = lefts_all.reshape(terms_all, extent, extent)
            fields[2 * place + 2] = rights_all.reshape(terms_all, extent, extent)
        result = result.at[inverse[place]].set(total.astype(jnp.bfloat16).reshape(extent, extent * extent))
    return result
```

```python
import jax
import jax.numpy as jnp
from jax import lax
from jax.experimental import pallas as pl
from jax.experimental.pallas import tpu as pltpu
from jax.sharding import PartitionSpec as P

LANES = 128
WIDE = 256


def dot(left, right):
    return jnp.dot(left, right, preferred_element_type=jnp.float32)


def iota(shape, dim):
    return lax.broadcasted_iota(jnp.int32, shape, dim)


def split_terms(packed, extent):
    per = LANES // extent
    wide = packed.astype(jnp.float32)
    out = []
    for term in range(per * packed.shape[0] // extent):
        block = wide[(term // per) * extent : (term // per + 1) * extent]
        mine = lax.div(iota(block.shape, 1), extent) == term % per
        out.append(jnp.where(mine, block, 0.0).astype(jnp.bfloat16))
    return out


def rows_apply(tensor_ref, mats, spread_ref, extent):
    per = LANES // extent
    half = extent // per
    stack = jnp.concatenate(mats, axis=0)
    for chunk in range(extent * extent // WIDE):
        piece = tensor_ref[:, chunk * WIDE : (chunk + 1) * WIDE]
        result = dot(stack, jnp.concatenate([piece] * per, axis=0))
        for part in range(WIDE // LANES):
            i = chunk * (WIDE // LANES) + part
            for term in range(len(mats)):
                spread_ref[term, pl.ds(i, extent, stride=half), :] = result[
                    term * extent : (term + 1) * extent, part * LANES : (part + 1) * LANES
                ]


def block_diagonals(mats, extent):
    per = LANES // extent
    half = extent // per
    quads = WIDE // extent
    rows = lax.rem(iota((LANES, WIDE), 0), extent)
    lanes = iota((LANES, WIDE), 1)
    wanted = per * lax.rem(lanes, half) + lax.div(lanes, WIDE // per)
    pick = jnp.where(rows == wanted, 1.0, 0.0).astype(jnp.bfloat16)
    spread = dot(jnp.concatenate(mats, axis=0), pick)
    lanes = iota((WIDE, WIDE), 1)
    same = lax.div(iota((WIDE, WIDE), 0), extent) == lax.rem(lax.div(lanes, half), quads)
    out = []
    for term in range(len(mats)):
        block = spread[term * extent : (term + 1) * extent]
        out.append(jnp.where(same, jnp.concatenate([block] * quads, axis=0), 0.0).astype(jnp.bfloat16))
    return out


def tall(tensor_ref):
    width = tensor_ref.shape[1]
    return jnp.concatenate([tensor_ref[:, j : j + WIDE] for j in range(0, width, WIDE)], axis=0)


def pair_up(accs, extent):
    per = LANES // extent
    out = []
    for first in range(0, len(accs), per):
        packed = None
        for lo in range(per):
            acc = accs[first + lo]
            group = lax.div(iota((extent, LANES), 1), extent)
            kept = jnp.zeros((extent, LANES), jnp.float32)
            for p in range(per):
                kept = jnp.where(group == p, acc[p * extent : (p + 1) * extent], kept)
            total = kept
            for p in range(1, per):
                total = total + pltpu.roll(kept, p * extent, 1)
            packed = total if packed is None else jnp.where(group == lo, total, packed)
        out.append(packed.astype(jnp.bfloat16))
    return jnp.concatenate(out, axis=0)


def contract(stacked, diagonals, spread, extent):
    per = LANES // extent
    groups = stacked.shape[0] // extent
    accs = []
    for term, diagonal in enumerate(diagonals):
        moved = dot(stacked, diagonal).astype(jnp.bfloat16)
        left = jnp.concatenate(
            [
                jnp.concatenate(
                    [
                        moved[j * extent : (j + 1) * extent, p * (WIDE // per) : (p + 1) * (WIDE // per)]
                        for j in range(groups)
                    ],
                    axis=1,
                )
                for p in range(per)
            ],
            axis=0,
        )
        accs.append(dot(left, spread[term].astype(jnp.bfloat16)))
    return pair_up(accs, extent)


def up_kernel(rows_ref, lanes_ref, left_ref, right_ref, out_ref, spread_ref):
    extent = rows_ref.shape[0]
    rows_apply(rows_ref, split_terms(right_ref[...], extent), spread_ref, extent)
    diagonals = block_diagonals(split_terms(left_ref[...], extent), extent)
    out_ref[...] = contract(tall(lanes_ref), diagonals, spread_ref, extent)


def prepare_kernel(bca_ref, acb_ref, left_ref, right_ref, for_left_ref, for_right_ref, spread_ref):
    extent = bca_ref.shape[0]
    rows_apply(bca_ref, split_terms(right_ref[...], extent), spread_ref, extent)
    for_left_ref[...] = spread_ref[...].astype(jnp.bfloat16)
    rows_apply(acb_ref, split_terms(left_ref[...], extent), spread_ref, extent)
    for_right_ref[...] = spread_ref[...].astype(jnp.bfloat16)


def down_kernel(abc_ref, bac_ref, field_ref, for_left_ref, for_right_ref, out_ref):
    extent = abc_ref.shape[0]
    diagonals = block_diagonals(split_terms(field_ref[...], extent), extent)
    out_ref[0] = contract(tall(abc_ref), diagonals, for_left_ref, extent)
    out_ref[1] = contract(tall(bac_ref), diagonals, for_right_ref, extent)


def weigh_kernel(bac_ref, left_ref, right_ref, out_ref, spread_ref):
    extent = bac_ref.shape[0]
    per = LANES // extent
    half = extent // per
    rows_apply(bac_ref, split_terms(right_ref[...], extent), spread_ref, extent)
    rows = lax.rem(iota((LANES, extent), 0), extent)
    lanes = iota((LANES, extent), 1)
    wanted = per * lax.rem(lanes, half) + lax.div(lanes, half)
    pick = jnp.where(rows == wanted, 1.0, 0.0).astype(jnp.bfloat16)
    group = lax.div(iota((half, LANES), 1), extent)
    for term, mat in enumerate(split_terms(left_ref[...], extent)):
        permuted = dot(mat, pick).astype(jnp.bfloat16)
        tiles = []
        for j in range(extent // per):
            given = [spread_ref[term, (per * j + q) * half : (per * j + q + 1) * half, :] for q in range(per)]
            stacked = []
            for p in range(per):
                row = None
                for q in range(per):
                    shift = (q - p) * extent % LANES
                    moved = pltpu.roll(given[q], shift, 1) if shift else given[q]
                    row = moved if row is None else jnp.where(group == q, moved, row)
                stacked.append(row)
            tiles.append(jnp.concatenate(stacked, axis=0).astype(jnp.bfloat16))
        for j in range(0, len(tiles), WIDE // LANES):
            wide = jnp.concatenate(tiles[j : j + WIDE // LANES], axis=1)
            out_ref[term, :, j * LANES : j * LANES + WIDE] = dot(permuted, wide).astype(jnp.bfloat16)


def finish_kernel(weighed_ref, field_ref, out_ref):
    terms, extent, width = weighed_ref.shape
    quads = WIDE // extent
    copies = pick_rows(extent, WIDE)
    same = lax.div(iota((WIDE, WIDE), 0), extent) == lax.div(iota((WIDE, WIDE), 1), extent)
    total = None
    for term, mat in enumerate(split_terms(field_ref[...], extent)):
        narrow = dot(mat, pick_rows(extent, LANES).T)
        block = dot(narrow.T.astype(jnp.bfloat16), copies)
        diagonal = jnp.where(same, jnp.concatenate([block] * quads, axis=0), 0.0).astype(jnp.bfloat16)
        stacked = jnp.concatenate([weighed_ref[term, :, j : j + WIDE] for j in range(0, width, WIDE)], axis=0)
        part = dot(stacked, diagonal)
        total = part if total is None else total + part
    for j in range(width // WIDE):
        out_ref[:, j * WIDE : (j + 1) * WIDE] = total[j * extent : (j + 1) * extent].astype(jnp.bfloat16)


def pick_rows(extent, width):
    rows = iota((extent, width), 0)
    return jnp.where(rows == lax.rem(iota((extent, width), 1), extent), 1.0, 0.0).astype(jnp.bfloat16)


def call(kernel, out_shape, *operands, scratch=()):
    vmem = pl.BlockSpec(memory_space=pltpu.VMEM)
    return pl.pallas_call(
        kernel,
        out_shape=out_shape,
        in_specs=[vmem] * len(operands),
        out_specs=jax.tree.map(lambda _: vmem, out_shape),
        scratch_shapes=list(scratch),
        compiler_params=pltpu.CompilerParams(vmem_limit_bytes=48 * 2**20),
    )(*operands)


LOW = 4


def z_exchange(value, nodes):
    parts = [value]
    for high in range(1, nodes // LOW):
        parts.append(lax.ppermute(value, "node", [(i, i ^ (high * LOW)) for i in range(nodes)]))
    return parts


def low_gather(value, nodes):
    groups = [[base + low for low in range(LOW)] for base in range(0, nodes, LOW)]
    return lax.all_gather(value, "node", axis=0, tiled=False, axis_index_groups=groups)


def pick(stack, index):
    return lax.dynamic_index_in_dim(stack, index, 0, keepdims=False)


def per_device(node_tensors, prim_ops, active, top_field, node_map):
    nodes = lax.axis_size("node")
    groups = lax.axis_size("term")
    depths = nodes.bit_length() - 1
    me = lax.axis_index("node")
    my_high = me // LOW
    position = node_map[me]
    slot_ids = jnp.arange(nodes, dtype=jnp.int32)
    slots = jnp.sum(jnp.where(node_map[None, :] == slot_ids[:, None], slot_ids[None, :], 0), axis=1)

    def slot_of(target):
        return jnp.sum(jnp.where(node_map == target, slot_ids, 0))

    my_depth = jnp.zeros((), jnp.int32)
    for power in range(1, depths):
        my_depth = my_depth + jnp.where(position + 1 >= 2**power, 1, 0)
    my_depth = jnp.where(position >= nodes - 1, -1, my_depth)
    left_slot = slot_of(2 * position + 1)
    right_slot = slot_of(2 * position + 2)

    extent = node_tensors.shape[1]
    terms = prim_ops.shape[1]
    per = LANES // extent
    pairs = terms // per
    flat = node_tensors[0]
    cube = flat.reshape(extent, extent, extent)

    def turned(*order):
        return jnp.transpose(cube, order).reshape(extent, extent * extent)

    bac = turned(1, 0, 2)
    cba = turned(2, 1, 0)
    bca = turned(1, 2, 0)
    acb = turned(0, 2, 1)

    def packed(mats):
        return mats.reshape(pairs, per, extent, extent).transpose(0, 2, 1, 3).reshape(pairs * extent, LANES)

    identity = jnp.eye(extent, dtype=jnp.bfloat16)
    leaf_terms = jnp.where(active[0][..., None, None] == 1, prim_ops[0], identity)
    left = packed(leaf_terms[:, 0])
    right = packed(leaf_terms[:, 1])
    field = packed(top_field)

    mats = jax.ShapeDtypeStruct((pairs * extent, LANES), jnp.bfloat16)
    spread = jax.ShapeDtypeStruct((terms, extent * extent * extent // LANES, LANES), jnp.bfloat16)
    space = pltpu.VMEM(spread.shape, jnp.float32)

    for depth in range(depths - 2, -1, -1):
        mine = call(up_kernel, mats, bac, cba, left, right, scratch=[space])
        sent = jnp.stack(z_exchange(mine, nodes))
        gathered = low_gather(sent, nodes).reshape((-1,) + mine.shape)
        now = my_depth == depth

        def from_slot(slot):
            return pick(gathered, (slot % LOW) * (nodes // LOW) + ((slot // LOW) ^ my_high))

        left = jnp.where(now, from_slot(left_slot), left)
        right = jnp.where(now, from_slot(right_slot), right)

    for_left, for_right = call(prepare_kernel, (spread, spread), bca, acb, left, right, scratch=[space])
    weighed = call(
        weigh_kernel,
        jax.ShapeDtypeStruct((terms,) + flat.shape, jnp.bfloat16),
        bac,
        left,
        right,
        scratch=[space],
    )
    sons = jax.ShapeDtypeStruct((2,) + mats.shape, jnp.bfloat16)
    for depth in range(depths - 1):
        fields = call(down_kernel, sons, flat, bac, field, for_left, for_right)
        parts = jnp.stack(z_exchange(fields, nodes))
        parts = parts.reshape((-1,) + mats.shape)
        relayed = []
        for low in range(LOW):
            target = node_map[my_high * LOW + low]
            source = slots[jnp.maximum((target - 1) // 2, 0)]
            relayed.append(pick(parts, 2 * ((source // LOW) ^ my_high) + (target + 1) % 2))
        gathered = low_gather(jnp.stack(relayed), nodes).reshape((-1,) + mats.shape)
        parent_slot = slots[jnp.maximum((position - 1) // 2, 0)]
        arrived = pick(gathered, (parent_slot % LOW) * LOW + me % LOW)
        field = jnp.where(my_depth == depth + 1, arrived, field)

    partial = call(finish_kernel, jax.ShapeDtypeStruct(flat.shape, jnp.bfloat16), weighed, field)
    partial = jnp.where(my_depth >= 0, partial, jnp.zeros((), jnp.bfloat16))
    mine = lax.axis_index("term")
    rows = extent // groups
    pieces = partial.reshape(groups, rows, extent * extent)
    total = pick(pieces, mine).astype(jnp.float32)
    for shift in range(1, groups):
        sent = pick(pieces, (mine + shift) % groups)
        total = total + lax.ppermute(sent, "term", [(i, (i + shift) % groups) for i in range(groups)]).astype(
            jnp.float32
        )
    return total.astype(jnp.bfloat16)[None]


def solution(mesh):
    placed = (
        P("node", None, None),
        P("node", "term", None, None, None),
        P("node", "term", None),
        P("term", None, None),
        P(),
    )
    return jax.shard_map(
        per_device, mesh=mesh, in_specs=placed, out_specs=P("node", "term", None), check_vma=False
    )
```

```python
import functools

import jax
import jax.numpy as jnp
from jax import lax
from jax.experimental import pallas as pl
from jax.experimental.pallas import tpu as pltpu
from jax.sharding import PartitionSpec as P

LANES = 128
WIDE = 256


def dot(left, right):
    return jnp.dot(left, right, preferred_element_type=jnp.float32)


def iota(shape, dim):
    return lax.broadcasted_iota(jnp.int32, shape, dim)


def split_terms(packed, extent):
    per = LANES // extent
    wide = packed.astype(jnp.float32)
    out = []
    for term in range(per * packed.shape[0] // extent):
        block = wide[(term // per) * extent : (term // per + 1) * extent]
        mine = lax.div(iota(block.shape, 1), extent) == term % per
        out.append(jnp.where(mine, block, 0.0).astype(jnp.bfloat16))
    return out


def rows_apply(tensor_ref, mats, spread_ref, extent):
    per = LANES // extent
    half = extent // per
    stack = jnp.concatenate(mats, axis=0)
    for chunk in range(extent * extent // WIDE):
        piece = tensor_ref[:, chunk * WIDE : (chunk + 1) * WIDE]
        result = dot(stack, jnp.concatenate([piece] * per, axis=0))
        for part in range(WIDE // LANES):
            i = chunk * (WIDE // LANES) + part
            for term in range(len(mats)):
                spread_ref[term, pl.ds(i, extent, stride=half), :] = result[
                    term * extent : (term + 1) * extent, part * LANES : (part + 1) * LANES
                ]


def block_diagonals(mats, extent):
    per = LANES // extent
    half = extent // per
    quads = WIDE // extent
    rows = lax.rem(iota((LANES, WIDE), 0), extent)
    lanes = iota((LANES, WIDE), 1)
    wanted = per * lax.rem(lanes, half) + lax.div(lanes, WIDE // per)
    pick = jnp.where(rows == wanted, 1.0, 0.0).astype(jnp.bfloat16)
    spread = dot(jnp.concatenate(mats, axis=0), pick)
    lanes = iota((WIDE, WIDE), 1)
    same = lax.div(iota((WIDE, WIDE), 0), extent) == lax.rem(lax.div(lanes, half), quads)
    out = []
    for term in range(len(mats)):
        block = spread[term * extent : (term + 1) * extent]
        out.append(jnp.where(same, jnp.concatenate([block] * quads, axis=0), 0.0).astype(jnp.bfloat16))
    return out


def tall(tensor_ref):
    width = tensor_ref.shape[1]
    return jnp.concatenate([tensor_ref[:, j : j + WIDE] for j in range(0, width, WIDE)], axis=0)


def pair_up(accs, extent):
    per = LANES // extent
    out = []
    for first in range(0, len(accs), per):
        packed = None
        for lo in range(per):
            acc = accs[first + lo]
            group = lax.div(iota((extent, LANES), 1), extent)
            kept = jnp.zeros((extent, LANES), jnp.float32)
            for p in range(per):
                kept = jnp.where(group == p, acc[p * extent : (p + 1) * extent], kept)
            total = kept
            for p in range(1, per):
                total = total + pltpu.roll(kept, p * extent, 1)
            packed = total if packed is None else jnp.where(group == lo, total, packed)
        out.append(packed.astype(jnp.bfloat16))
    return jnp.concatenate(out, axis=0)


def contract(stacked, diagonals, spread, extent):
    per = LANES // extent
    groups = stacked.shape[0] // extent
    accs = []
    for term, diagonal in enumerate(diagonals):
        moved = dot(stacked, diagonal).astype(jnp.bfloat16)
        left = jnp.concatenate(
            [
                jnp.concatenate(
                    [
                        moved[j * extent : (j + 1) * extent, p * (WIDE // per) : (p + 1) * (WIDE // per)]
                        for j in range(groups)
                    ],
                    axis=1,
                )
                for p in range(per)
            ],
            axis=0,
        )
        accs.append(dot(left, spread[term].astype(jnp.bfloat16)))
    return pair_up(accs, extent)


def swap(value, turn_ref, out_ref, extent):
    per = LANES // extent
    half = extent // per
    rows = iota((extent, extent), 0)
    wanted = per * lax.rem(rows, half) + lax.div(rows, half)
    order = jnp.where(iota((extent, extent), 1) == wanted, 1.0, 0.0).astype(jnp.bfloat16)
    sorted_rows = dot(order, value)
    group = lax.div(iota((half, LANES), 1), extent)
    for j in range(extent // per):
        given = [sorted_rows[p * half : (p + 1) * half, j * LANES : (j + 1) * LANES] for p in range(per)]
        for q in range(per):
            row = None
            for p in range(per):
                shift = (p - q) * extent % LANES
                moved = pltpu.roll(given[p], shift, 1) if shift else given[p]
                row = moved if row is None else jnp.where(group == p, moved, row)
            turn_ref[pl.ds(per * j + q, half, stride=extent), :] = row
    for i in range(half):
        out_ref[:, i * LANES : (i + 1) * LANES] = turn_ref[i * extent : (i + 1) * extent, :].astype(jnp.bfloat16)


def flip(value, extent):
    per = LANES // extent
    wide = value.astype(jnp.float32)
    tiles = []
    for j in range(extent // per):
        turned = wide[:, j * LANES : (j + 1) * LANES].T
        tiles.append(jnp.concatenate([turned[p * extent : (p + 1) * extent] for p in range(per)], axis=1))
    return jnp.concatenate(tiles, axis=1).astype(jnp.bfloat16)


DEPTH, FROM_LEFT, FROM_RIGHT, FROM_PARENT, UP_RELAY, DOWN_RELAY, TABLE = 0, 1, 2, 3, 8, 16, 24
LOW = 4


def fill_table(map_ref, me, inverse_ref, table_ref):
    nodes = map_ref.shape[0]

    def note(slot, carry):
        inverse_ref[map_ref[slot]] = slot
        return carry

    lax.fori_loop(0, nodes, note, 0)
    low = lax.rem(me, LOW)
    high = lax.div(me, LOW)

    def routes(slot):
        position = map_ref[slot]
        last = jnp.int32(nodes - 1)
        left = inverse_ref[jnp.minimum(2 * position + 1, last)]
        right = inverse_ref[jnp.minimum(2 * position + 2, last)]
        parent = inverse_ref[lax.div(jnp.maximum(position - 1, 0), 2)]
        return position, left, right, parent

    position, left, right, parent = routes(me)
    depth = jnp.int32(0)
    for power in range(1, nodes.bit_length() - 1):
        depth = depth + jnp.where(position + 1 >= 2**power, 1, 0)
    table_ref[DEPTH] = jnp.where(position >= nodes - 1, -1, depth)
    table_ref[FROM_LEFT] = lax.rem(left, LOW) ^ low
    table_ref[FROM_RIGHT] = lax.rem(right, LOW) ^ low
    table_ref[FROM_PARENT] = lax.rem(parent, LOW) ^ low
    for j in range(LOW):
        position, left, right, parent = routes(high * LOW + (low ^ j))
        table_ref[UP_RELAY + 2 * j] = lax.div(left, LOW) ^ high
        table_ref[UP_RELAY + 2 * j + 1] = lax.div(right, LOW) ^ high
        table_ref[DOWN_RELAY + j] = 2 * (lax.div(parent, LOW) ^ high) + lax.rem(position + 1, 2)


def choose(index, choices):
    out = choices[0]().astype(jnp.float32)
    for k in range(1, len(choices)):
        out = jnp.where(index == k, choices[k]().astype(jnp.float32), out)
    return out.astype(jnp.bfloat16)


def loads(refs, *where):
    return [lambda ref=ref: ref[where] if where else ref[...] for ref in refs]


def start_kernel(
    tensor_ref, prim_ref, active_ref, top_ref, map_ref, me_ref,
    bac_ref, cba_ref, left_ref, right_ref, field_ref, out_ref, table_ref,
    spread_ref, turn_ref, inverse_ref,
):
    extent = tensor_ref.shape[1]
    per = LANES // extent
    terms = prim_ref.shape[1]
    fill_table(map_ref, me_ref[0], inverse_ref, table_ref)
    eye = jnp.where(iota((extent, extent), 0) == iota((extent, extent), 1), 1.0, 0.0)

    def operator(term, side):
        return jnp.where(active_ref[0, term, side] == 1, prim_ref[0, term, side].astype(jnp.float32), eye)

    for first in range(0, terms, per):
        rows = pl.ds(first // per * extent, extent)
        for side, ref in ((0, left_ref), (1, right_ref)):
            side_by_side = [operator(first + lo, side) for lo in range(per)]
            ref[rows, :] = jnp.concatenate(side_by_side, axis=1).astype(jnp.bfloat16)
        fields = [top_ref[first + lo].astype(jnp.float32) for lo in range(per)]
        field_ref[rows, :] = jnp.concatenate(fields, axis=1).astype(jnp.bfloat16)
    swap(tensor_ref[0], turn_ref, bac_ref, extent)
    cba_ref[...] = flip(tensor_ref[0], extent)
    rows_apply(bac_ref, split_terms(right_ref[...], extent), spread_ref, extent)
    diagonals = block_diagonals(split_terms(left_ref[...], extent), extent)
    out_ref[...] = contract(tall(cba_ref), diagonals, spread_ref, extent)


def turn_kernel(bac_ref, cba_ref, bca_ref, acb_ref, cab_ref, turn_ref):
    extent = bac_ref.shape[0]
    swap(cba_ref[...], turn_ref, bca_ref, extent)
    cab_ref[...] = flip(bac_ref[...], extent)
    swap(cab_ref[...], turn_ref, acb_ref, extent)


def relay_up_kernel(*refs):
    parts, table_ref, outs = refs[:-5], refs[-5], refs[-4:]
    for j, out in enumerate(outs):
        for side in range(2):
            out[side] = choose(table_ref[UP_RELAY + 2 * j + side], loads(parts))


def relay_down_kernel(*refs):
    parts, table_ref, outs = refs[:-5], refs[-5], refs[-4:]
    choices = [f for part in parts for side in range(2) for f in loads([part], side)]
    for j, out in enumerate(outs):
        out[...] = choose(table_ref[DOWN_RELAY + j], choices)


def up_kernel(depth, *refs):
    came, (bac_ref, cba_ref, old_left_ref, old_right_ref, table_ref) = refs[:LOW], refs[LOW : LOW + 5]
    left_ref, right_ref, out_ref, spread_ref = refs[LOW + 5 :]
    extent = bac_ref.shape[0]
    now = table_ref[DEPTH] == depth
    left = choose(table_ref[FROM_LEFT], loads(came, 0))
    right = choose(table_ref[FROM_RIGHT], loads(came, 1))
    left_ref[...] = choose(now, [lambda: old_left_ref[...], lambda: left])
    right_ref[...] = choose(now, [lambda: old_right_ref[...], lambda: right])
    rows_apply(bac_ref, split_terms(right_ref[...], extent), spread_ref, extent)
    diagonals = block_diagonals(split_terms(left_ref[...], extent), extent)
    out_ref[...] = contract(tall(cba_ref), diagonals, spread_ref, extent)


def prepare_kernel(first_ref, second_ref, left_ref, right_ref, for_left_ref, for_right_ref, spread_ref):
    extent = first_ref.shape[0]
    rows_apply(first_ref, split_terms(left_ref[...], extent), spread_ref, extent)
    for_left_ref[...] = spread_ref[...].astype(jnp.bfloat16)
    rows_apply(second_ref, split_terms(right_ref[...], extent), spread_ref, extent)
    for_right_ref[...] = spread_ref[...].astype(jnp.bfloat16)


def top_kernel(
    acb_ref, bca_ref, old_left_ref, old_right_ref, came_left_ref, came_right_ref, for_left_ref, for_right_ref, table_ref,
    left_ref, right_ref, to_left_ref, to_right_ref,
):
    extent = acb_ref.shape[0]
    now = table_ref[DEPTH] == 0
    left_ref[...] = choose(now, loads([old_left_ref, came_left_ref]))
    right_ref[...] = choose(now, loads([old_right_ref, came_right_ref]))
    diagonals = block_diagonals(split_terms(right_ref[...], extent), extent)
    to_left_ref[...] = contract(tall(acb_ref), diagonals, for_left_ref, extent)
    diagonals = block_diagonals(split_terms(left_ref[...], extent), extent)
    to_right_ref[...] = contract(tall(bca_ref), diagonals, for_right_ref, extent)


def below_top_kernel(abc_ref, bac_ref, old_ref, came_left_ref, came_right_ref, for_left_ref, for_right_ref, map_ref, me_ref,
                     field_ref, out_ref):
    position = map_ref[me_ref[0]]
    came = choose(position == 2, loads([came_left_ref, came_right_ref]))
    now = jnp.logical_or(position == 1, position == 2)
    field_ref[...] = choose(now, [lambda: old_ref[...], lambda: came])
    downward(abc_ref, bac_ref, field_ref, for_left_ref, for_right_ref, out_ref)


def down_kernel(depth, *refs):
    came, (abc_ref, bac_ref, old_ref, for_left_ref, for_right_ref, table_ref) = refs[:LOW], refs[LOW : LOW + 6]
    field_ref, out_ref = refs[LOW + 6 :]
    arrive(depth, came, old_ref, table_ref, field_ref)
    downward(abc_ref, bac_ref, field_ref, for_left_ref, for_right_ref, out_ref)


def arrive(depth, came, old_ref, table_ref, field_ref):
    arrived = choose(table_ref[FROM_PARENT], loads(came))
    field_ref[...] = choose(table_ref[DEPTH] == depth, [lambda: old_ref[...], lambda: arrived])


def downward(abc_ref, bac_ref, field_ref, for_left_ref, for_right_ref, out_ref):
    extent = bac_ref.shape[0]
    diagonals = block_diagonals(split_terms(field_ref[...], extent), extent)
    out_ref[0] = contract(tall(abc_ref.at[0]), diagonals, for_left_ref, extent)
    out_ref[1] = contract(tall(bac_ref), diagonals, for_right_ref, extent)


def weigh_kernel(bac_ref, left_ref, right_ref, out_ref, spread_ref):
    extent = bac_ref.shape[0]
    groups, _, rows_out, _ = out_ref.shape
    per = LANES // extent
    half = extent // per
    rows_apply(bac_ref, split_terms(right_ref[...], extent), spread_ref, extent)
    rows = lax.rem(iota((LANES, extent), 0), extent)
    lanes = iota((LANES, extent), 1)
    wanted = per * lax.rem(lanes, half) + lax.div(lanes, half)
    pick = jnp.where(rows == wanted, 1.0, 0.0).astype(jnp.bfloat16)
    group = lax.div(iota((half, LANES), 1), extent)
    for term, mat in enumerate(split_terms(left_ref[...], extent)):
        permuted = dot(mat, pick).astype(jnp.bfloat16)
        tiles = []
        for j in range(extent // per):
            given = [spread_ref[term, (per * j + q) * half : (per * j + q + 1) * half, :] for q in range(per)]
            stacked = []
            for p in range(per):
                row = None
                for q in range(per):
                    shift = (q - p) * extent % LANES
                    moved = pltpu.roll(given[q], shift, 1) if shift else given[q]
                    row = moved if row is None else jnp.where(group == q, moved, row)
                stacked.append(row)
            tiles.append(jnp.concatenate(stacked, axis=0).astype(jnp.bfloat16))
        for j in range(0, len(tiles), WIDE // LANES):
            wide = jnp.concatenate(tiles[j : j + WIDE // LANES], axis=1)
            result = dot(permuted, wide).astype(jnp.bfloat16)
            for g in range(groups):
                out_ref[g, term, :, j * LANES : j * LANES + WIDE] = result[g * rows_out : (g + 1) * rows_out]


def finish(weighed_ref, which, field):
    terms, rows, width = weighed_ref.shape[1:]
    extent = weighed_ref.shape[0] * rows
    quads = WIDE // extent
    copies = pick_rows(extent, WIDE)
    same = lax.div(iota((WIDE, WIDE), 0), extent) == lax.div(iota((WIDE, WIDE), 1), extent)
    total = None
    for term, mat in enumerate(split_terms(field, extent)):
        narrow = dot(mat, pick_rows(extent, LANES).T)
        block = dot(narrow.T.astype(jnp.bfloat16), copies)
        diagonal = jnp.where(same, jnp.concatenate([block] * quads, axis=0), 0.0).astype(jnp.bfloat16)
        stacked = jnp.concatenate([weighed_ref[which, term, :, j : j + WIDE] for j in range(0, width, WIDE)], axis=0)
        part = dot(stacked, diagonal)
        total = part if total is None else total + part
    return total


def last_kernel(depth, *refs):
    came, (old_ref, weighed_ref, which_ref, table_ref, field_ref, out_ref) = refs[:LOW], refs[LOW:]
    rows = out_ref.shape[0]
    arrive(depth, came, old_ref, table_ref, field_ref)
    total = finish(weighed_ref, which_ref[0], field_ref[...])
    for j in range(out_ref.shape[1] // WIDE):
        out_ref[:, j * WIDE : (j + 1) * WIDE] = total[j * rows : (j + 1) * rows].astype(jnp.bfloat16)


def own_kernel(field_ref, weighed_ref, which_ref, out_ref):
    rows = out_ref.shape[0]
    total = finish(weighed_ref, which_ref[0], field_ref[...])
    for j in range(out_ref.shape[1] // WIDE):
        out_ref[:, j * WIDE : (j + 1) * WIDE] = total[j * rows : (j + 1) * rows].astype(jnp.bfloat16)


def sum_kernel(own_ref, *refs):
    others, table_ref, out_ref = refs[:-2], refs[-2], refs[-1]
    total = own_ref[...].astype(jnp.float32)
    for other in others:
        total = total + other[...].astype(jnp.float32)
    out_ref[0] = jnp.where(table_ref[DEPTH] >= 0, total, 0.0).astype(jnp.bfloat16)


def pick_rows(extent, width):
    rows = iota((extent, width), 0)
    return jnp.where(rows == lax.rem(iota((extent, width), 1), extent), 1.0, 0.0).astype(jnp.bfloat16)


VMEM = pl.BlockSpec(memory_space=pltpu.VMEM)
SMEM = pl.BlockSpec(memory_space=pltpu.SMEM)


def call(kernel, out_shape, *operands, scratch=(), smem_out=()):
    shapes = out_shape if isinstance(out_shape, list) else [out_shape]
    specs = [SMEM if i in smem_out else VMEM for i in range(len(shapes))]
    return pl.pallas_call(
        kernel,
        out_shape=out_shape,
        in_specs=[SMEM if operand.dtype == jnp.int32 else VMEM for operand in operands],
        out_specs=specs if isinstance(out_shape, list) else specs[0],
        scratch_shapes=list(scratch),
        compiler_params=pltpu.CompilerParams(vmem_limit_bytes=56 * 2**20),
    )(*operands)


def exchange(value, mask, nodes):
    return lax.ppermute(value, "node", [(i, i ^ mask) for i in range(nodes)])


def high_exchange(value, nodes):
    return [value] + [exchange(value, high * LOW, nodes) for high in range(1, nodes // LOW)]


def low_exchange(values, nodes):
    return [values[0]] + [exchange(values[j], j, nodes) for j in range(1, LOW)]


def per_device(node_tensors, prim_ops, active, top_field, node_map):
    nodes = lax.axis_size("node")
    groups = lax.axis_size("term")
    depths = nodes.bit_length() - 1
    me = lax.axis_index("node").astype(jnp.int32)[None]
    slot_ids = jnp.arange(nodes, dtype=jnp.int32)
    apart = jnp.sum(jnp.where(node_map == 0, slot_ids, 0)) ^ jnp.sum(jnp.where(node_map == 2, slot_ids, 0))

    extent = node_tensors.shape[1]
    terms = prim_ops.shape[1]
    pairs = terms * extent // LANES
    flat = jax.ShapeDtypeStruct((extent, extent * extent), jnp.bfloat16)
    mats = jax.ShapeDtypeStruct((pairs * extent, LANES), jnp.bfloat16)
    two = jax.ShapeDtypeStruct((2,) + mats.shape, jnp.bfloat16)
    table_shape = jax.ShapeDtypeStruct((TABLE,), jnp.int32)
    spread = jax.ShapeDtypeStruct((terms, extent * extent * extent // LANES, LANES), jnp.bfloat16)
    space = pltpu.VMEM(spread.shape, jnp.float32)
    turn_space = pltpu.VMEM(spread.shape[1:], jnp.float32)

    def exchange_with_top(values):
        def branch(mask):
            return lambda left, right: (exchange(left, nodes // 2, nodes), exchange(right, mask, nodes))

        return lax.switch(apart - 1, [branch(mask) for mask in range(1, nodes)], *values)

    bac, cba, left, right, field, mine, table = call(
        start_kernel,
        [flat, flat, mats, mats, mats, mats, table_shape],
        node_tensors,
        prim_ops,
        active,
        top_field,
        node_map,
        me,
        scratch=[space, turn_space, pltpu.SMEM((nodes,), jnp.int32)],
        smem_out=(6,),
    )
    bca, acb, cab = call(turn_kernel, [flat, flat, flat], bac, cba, scratch=[turn_space])
    top_for_left, top_for_right = call(prepare_kernel, [spread, spread], cba, cab, field, field, scratch=[space])

    for depth in range(depths - 2, 0, -1):
        parts = high_exchange(mine, nodes)
        came = low_exchange(call(relay_up_kernel, [two] * LOW, *parts, table), nodes)
        left, right, mine = call(
            functools.partial(up_kernel, depth),
            [mats, mats, mats],
            *came,
            bac,
            cba,
            left,
            right,
            table,
            scratch=[space],
        )
    for_left, for_right = call(prepare_kernel, [spread, spread], bca, acb, right, left, scratch=[space])

    came_left, came_right = exchange_with_top((mine, mine))
    left, right, to_left, to_right = call(
        top_kernel,
        [mats] * 4,
        acb,
        bca,
        left,
        right,
        came_left,
        came_right,
        top_for_left,
        top_for_right,
        table,
    )
    weighed = call(
        weigh_kernel,
        jax.ShapeDtypeStruct((groups, terms, extent // groups, extent * extent), jnp.bfloat16),
        bac,
        left,
        right,
        scratch=[space],
    )
    came_left, came_right = exchange_with_top((to_left, to_right))
    field, fields = call(
        below_top_kernel,
        [mats, two],
        node_tensors,
        bac,
        field,
        came_left,
        came_right,
        for_left,
        for_right,
        node_map,
        me,
    )
    for depth in range(2, depths):
        parts = high_exchange(fields, nodes)
        came = low_exchange(call(relay_down_kernel, [mats] * LOW, *parts, table), nodes)
        if depth < depths - 1:
            field, fields = call(
                functools.partial(down_kernel, depth),
                [mats, two],
                *came,
                node_tensors,
                bac,
                field,
                for_left,
                for_right,
                table,
            )

    group = lax.axis_index("term").astype(jnp.int32)[None]
    piece = jax.ShapeDtypeStruct((extent // groups, extent * extent), jnp.bfloat16)
    others = []
    for shift in range(1, groups):
        which = lax.rem(group + shift, jnp.int32(groups))
        kernel = functools.partial(last_kernel, depths - 1)
        final, part = call(kernel, [mats, piece], *came, field, weighed, which, table)
        others.append(lax.ppermute(part, "term", [(i, (i + shift) % groups) for i in range(groups)]))
    own = call(own_kernel, piece, final, weighed, group)
    return call(sum_kernel, jax.ShapeDtypeStruct((1,) + piece.shape, jnp.bfloat16), own, *others, table)


def solution(mesh):
    placed = (
        P("node", None, None),
        P("node", "term", None, None, None),
        P("node", "term", None),
        P("term", None, None),
        P(),
    )
    return jax.shard_map(
        per_device, mesh=mesh, in_specs=placed, out_specs=P("node", "term", None), check_vma=False
    )
```

```python
import functools
import math

import jax
import jax.numpy as jnp
from jax import lax
from jax.experimental import pallas as pl
from jax.experimental.pallas import tpu as pltpu
from jax.sharding import PartitionSpec as P

LANES = 128
WIDE = 256


def dot(left, right):
    return jnp.dot(left, right, preferred_element_type=jnp.float32)


def iota(shape, dim):
    return lax.broadcasted_iota(jnp.int32, shape, dim)


def split_terms(packed, extent):
    per = LANES // extent
    wide = packed.astype(jnp.float32)
    out = []
    for term in range(per * packed.shape[0] // extent):
        block = wide[(term // per) * extent : (term // per + 1) * extent]
        mine = lax.div(iota(block.shape, 1), extent) == term % per
        out.append(jnp.where(mine, block, 0.0).astype(jnp.bfloat16))
    return out


def rows_spread(tensor_ref, mats, spread_ref, extent):
    per = LANES // extent
    half = extent // per
    stack = jnp.concatenate(mats, axis=0)
    for chunk in range(extent * extent // WIDE):
        piece = tensor_ref[:, chunk * WIDE : (chunk + 1) * WIDE]
        result = dot(stack, jnp.concatenate([piece] * per, axis=0))
        for part in range(WIDE // LANES):
            i = chunk * (WIDE // LANES) + part
            for term in range(len(mats)):
                spread_ref[term, pl.ds(i, extent, stride=half), :] = result[
                    term * extent : (term + 1) * extent, part * LANES : (part + 1) * LANES
                ]


SUB = 8


def rows_apply(tensor_ref, mats, mixed_ref, extent):
    per = LANES // extent
    quads = WIDE // extent
    halves = SUB // quads
    count = 2 * halves
    stack = jnp.concatenate(mats, axis=0)
    row = iota((extent // SUB, SUB, LANES), 1)
    for first in range(0, extent // per, count):
        piece = tensor_ref[:, first * LANES : (first + count) * LANES]
        result = dot(stack, jnp.concatenate([piece] * per, axis=0))
        for term in range(len(mats)):
            tiles = [
                result[term * extent : (term + 1) * extent, k * LANES : (k + 1) * LANES].reshape(row.shape)
                for k in range(count)
            ]
            for half in range(halves):
                wanted = []
                for start in range(0, count, halves):
                    block = None
                    for k in range(halves):
                        shift = (k - half) * quads % SUB
                        moved = pltpu.roll(tiles[start + k], shift, 1) if shift else tiles[start + k]
                        block = moved if block is None else jnp.where(lax.div(row, quads) == k, moved, block)
                    wanted.append(block)
                packed = jnp.concatenate(wanted, axis=1).astype(jnp.bfloat16)
                for m in range(extent // SUB):
                    base = (m * halves + half) * (extent // per) * quads + first * quads
                    mixed_ref[term, base : base + count * quads, :] = packed[m]


def block_diagonals(mats, extent):
    per = LANES // extent
    quads = WIDE // extent
    rows = lax.rem(iota((LANES, WIDE), 0), extent)
    lanes = iota((LANES, WIDE), 1)
    wanted = per * lax.div(lax.rem(lanes, WIDE // per), quads) + lax.div(lanes, WIDE // per)
    pick = jnp.where(rows == wanted, 1.0, 0.0).astype(jnp.bfloat16)
    spread = dot(jnp.concatenate(mats, axis=0), pick)
    lanes = iota((WIDE, WIDE), 1)
    same = lax.div(iota((WIDE, WIDE), 0), extent) == lax.rem(lanes, quads)
    out = []
    for term in range(len(mats)):
        block = spread[term * extent : (term + 1) * extent]
        out.append(jnp.where(same, jnp.concatenate([block] * quads, axis=0), 0.0).astype(jnp.bfloat16))
    return out


def tall(tensor_ref):
    width = tensor_ref.shape[1]
    return jnp.concatenate([tensor_ref[:, j : j + WIDE] for j in range(0, width, WIDE)], axis=0)


def pair_up(accs, extent):
    per = LANES // extent
    out = []
    for first in range(0, len(accs), per):
        packed = None
        for lo in range(per):
            acc = accs[first + lo]
            group = lax.div(iota((extent, LANES), 1), extent)
            kept = jnp.zeros((extent, LANES), jnp.float32)
            for p in range(per):
                kept = jnp.where(group == p, acc[p * extent : (p + 1) * extent], kept)
            total = kept
            for p in range(1, per):
                total = total + pltpu.roll(kept, p * extent, 1)
            packed = total if packed is None else jnp.where(group == lo, total, packed)
        out.append(packed.astype(jnp.bfloat16))
    return jnp.concatenate(out, axis=0)


def contract(stacked, diagonals, mixed, extent):
    per = LANES // extent
    groups = stacked.shape[0] // extent
    accs = []
    for term, diagonal in enumerate(diagonals):
        moved = dot(stacked, diagonal).astype(jnp.bfloat16)
        left = jnp.concatenate(
            [
                jnp.concatenate(
                    [
                        moved[j * extent : (j + 1) * extent, p * (WIDE // per) : (p + 1) * (WIDE // per)]
                        for j in range(groups)
                    ],
                    axis=1,
                )
                for p in range(per)
            ],
            axis=0,
        )
        accs.append(dot(left, mixed[term]))
    return pair_up(accs, extent)


def swap(value, turn_ref, out_ref, extent):
    per = LANES // extent
    half = extent // per
    rows = iota((extent, extent), 0)
    wanted = per * lax.rem(rows, half) + lax.div(rows, half)
    order = jnp.where(iota((extent, extent), 1) == wanted, 1.0, 0.0).astype(jnp.bfloat16)
    sorted_rows = dot(order, value)
    group = lax.div(iota((half, LANES), 1), extent)
    for j in range(extent // per):
        given = [sorted_rows[p * half : (p + 1) * half, j * LANES : (j + 1) * LANES] for p in range(per)]
        for q in range(per):
            row = None
            for p in range(per):
                shift = (p - q) * extent % LANES
                moved = pltpu.roll(given[p], shift, 1) if shift else given[p]
                row = moved if row is None else jnp.where(group == p, moved, row)
            turn_ref[pl.ds(per * j + q, half, stride=extent), :] = row
    for i in range(half):
        out_ref[:, i * LANES : (i + 1) * LANES] = turn_ref[i * extent : (i + 1) * extent, :].astype(jnp.bfloat16)


def flip(value, extent):
    per = LANES // extent
    wide = value.astype(jnp.float32)
    tiles = []
    for j in range(extent // per):
        turned = wide[:, j * LANES : (j + 1) * LANES].T
        tiles.append(jnp.concatenate([turned[p * extent : (p + 1) * extent] for p in range(per)], axis=1))
    return jnp.concatenate(tiles, axis=1).astype(jnp.bfloat16)


DEPTH, FROM_LEFT, FROM_RIGHT, FROM_PARENT, UP_RELAY, DOWN_RELAY, TABLE = 0, 1, 2, 3, 8, 16, 24
LOW = 4


def fill_table(map_ref, me, inverse_ref, table_ref):
    nodes = map_ref.shape[0]

    def note(slot, carry):
        inverse_ref[map_ref[slot]] = slot
        return carry

    lax.fori_loop(0, nodes, note, 0)
    low = lax.rem(me, LOW)
    high = lax.div(me, LOW)

    def routes(slot):
        position = map_ref[slot]
        last = jnp.int32(nodes - 1)
        left = inverse_ref[jnp.minimum(2 * position + 1, last)]
        right = inverse_ref[jnp.minimum(2 * position + 2, last)]
        parent = inverse_ref[lax.div(jnp.maximum(position - 1, 0), 2)]
        return position, left, right, parent

    position, left, right, parent = routes(me)
    depth = jnp.int32(0)
    for power in range(1, nodes.bit_length() - 1):
        depth = depth + jnp.where(position + 1 >= 2**power, 1, 0)
    table_ref[DEPTH] = jnp.where(position >= nodes - 1, -1, depth)
    table_ref[FROM_LEFT] = lax.rem(left, LOW) ^ low
    table_ref[FROM_RIGHT] = lax.rem(right, LOW) ^ low
    table_ref[FROM_PARENT] = lax.rem(parent, LOW) ^ low
    for j in range(LOW):
        position, left, right, parent = routes(high * LOW + (low ^ j))
        table_ref[UP_RELAY + 2 * j] = lax.div(left, LOW) ^ high
        table_ref[UP_RELAY + 2 * j + 1] = lax.div(right, LOW) ^ high
        table_ref[DOWN_RELAY + j] = 2 * (lax.div(parent, LOW) ^ high) + lax.rem(position + 1, 2)


def choose(index, choices):
    out = choices[0]().astype(jnp.float32)
    for k in range(1, len(choices)):
        out = jnp.where(index == k, choices[k]().astype(jnp.float32), out)
    return out.astype(jnp.bfloat16)


def loads(refs, *where):
    return [lambda ref=ref: ref[where] if where else ref[...] for ref in refs]


def start_kernel(
    tensor_hbm, prim_hbm, active_hbm, top_hbm, map_hbm, me_ref,
    bac_ref, cba_ref, left_ref, right_ref, field_ref, out_ref, table_ref,
    tensor_ref, prim_ref, active_ref, top_ref, map_ref, mixed_ref, turn_ref, inverse_ref, sems,
):
    given = (tensor_hbm, prim_hbm, top_hbm, active_hbm, map_hbm)
    held = (tensor_ref, prim_ref, top_ref, active_ref, map_ref)
    copies = [pltpu.make_async_copy(*pair, sems.at[i]) for i, pair in enumerate(zip(given, held))]
    for copy in copies:
        copy.start()
    extent = tensor_ref.shape[1]
    per = LANES // extent
    terms = prim_ref.shape[1]
    for copy in copies[::-1]:
        copy.wait()
        if copy is copies[-1]:
            fill_table(map_ref, me_ref[0], inverse_ref, table_ref)
    eye = jnp.where(iota((extent, extent), 0) == iota((extent, extent), 1), 1.0, 0.0)

    def operator(term, side):
        return jnp.where(active_ref[0, term, side] == 1, prim_ref[0, term, side].astype(jnp.float32), eye)

    for first in range(0, terms, per):
        rows = pl.ds(first // per * extent, extent)
        for side, ref in ((0, left_ref), (1, right_ref)):
            side_by_side = [operator(first + lo, side) for lo in range(per)]
            ref[rows, :] = jnp.concatenate(side_by_side, axis=1).astype(jnp.bfloat16)
        fields = [top_ref[first + lo].astype(jnp.float32) for lo in range(per)]
        field_ref[rows, :] = jnp.concatenate(fields, axis=1).astype(jnp.bfloat16)
    swap(tensor_ref[0], turn_ref, bac_ref, extent)
    cba_ref[...] = flip(tensor_ref[0], extent)
    rows_apply(bac_ref, split_terms(right_ref[...], extent), mixed_ref, extent)
    diagonals = block_diagonals(split_terms(left_ref[...], extent), extent)
    out_ref[...] = contract(tall(cba_ref), diagonals, mixed_ref, extent)


def turn_kernel(bac_ref, cba_ref, bca_ref, acb_ref, turn_ref):
    extent = bac_ref.shape[0]
    swap(cba_ref[...], turn_ref, bca_ref, extent)
    swap(flip(bac_ref[...], extent), turn_ref, acb_ref, extent)


def relay_up_kernel(*refs):
    parts, table_ref, outs = refs[:-5], refs[-5], refs[-4:]
    for j, out in enumerate(outs):
        for side in range(2):
            out[side] = choose(table_ref[UP_RELAY + 2 * j + side], loads(parts))


def relay_down_kernel(*refs):
    parts, table_ref, outs = refs[:-5], refs[-5], refs[-4:]
    choices = [f for part in parts for side in range(2) for f in loads([part], side)]
    for j, out in enumerate(outs):
        out[...] = choose(table_ref[DOWN_RELAY + j], choices)


def up_kernel(depth, *refs):
    came, (bac_ref, cba_ref, old_left_ref, old_right_ref, table_ref) = refs[:LOW], refs[LOW : LOW + 5]
    left_ref, right_ref, out_ref, mixed_ref = refs[LOW + 5 :]
    extent = bac_ref.shape[0]
    now = table_ref[DEPTH] == depth
    left = choose(table_ref[FROM_LEFT], loads(came, 0))
    right = choose(table_ref[FROM_RIGHT], loads(came, 1))
    left_ref[...] = choose(now, [lambda: old_left_ref[...], lambda: left])
    right_ref[...] = choose(now, [lambda: old_right_ref[...], lambda: right])
    rows_apply(bac_ref, split_terms(right_ref[...], extent), mixed_ref, extent)
    diagonals = block_diagonals(split_terms(left_ref[...], extent), extent)
    out_ref[...] = contract(tall(cba_ref), diagonals, mixed_ref, extent)


def top_kernel(
    abc_ref, bac_ref, bca_ref, acb_ref, field_ref, old_left_ref, old_right_ref, came_left_ref, came_right_ref, table_ref,
    sides_ref, to_left_ref, to_right_ref, for_left_ref, for_right_ref,
):
    extent = bac_ref.shape[0]
    now = table_ref[DEPTH] == 0
    sides_ref[0] = choose(now, loads([old_left_ref, came_left_ref]))
    sides_ref[1] = choose(now, loads([old_right_ref, came_right_ref]))
    diagonals = block_diagonals(split_terms(field_ref[...], extent), extent)
    rows_apply(bca_ref, split_terms(sides_ref[1], extent), for_left_ref, extent)
    to_left_ref[...] = contract(tall(abc_ref.at[0]), diagonals, for_left_ref, extent)
    rows_apply(acb_ref, split_terms(sides_ref[0], extent), for_right_ref, extent)
    to_right_ref[...] = contract(tall(bac_ref), diagonals, for_right_ref, extent)


def below_top_kernel(abc_ref, bac_ref, old_ref, came_left_ref, came_right_ref, for_left_ref, for_right_ref, map_ref, me_ref,
                     field_ref, out_ref):
    position = map_ref[me_ref[0]]
    came = choose(position == 2, loads([came_left_ref, came_right_ref]))
    now = jnp.logical_or(position == 1, position == 2)
    field_ref[...] = choose(now, [lambda: old_ref[...], lambda: came])
    downward(abc_ref, bac_ref, field_ref, for_left_ref, for_right_ref, out_ref)


def down_kernel(depth, *refs):
    came, (abc_ref, bac_ref, old_ref, for_left_ref, for_right_ref, table_ref) = refs[:LOW], refs[LOW : LOW + 6]
    field_ref, out_ref = refs[LOW + 6 :]
    arrive(depth, came, old_ref, table_ref, field_ref)
    downward(abc_ref, bac_ref, field_ref, for_left_ref, for_right_ref, out_ref)


def arrive(depth, came, old_ref, table_ref, field_ref):
    arrived = choose(table_ref[FROM_PARENT], loads(came))
    field_ref[...] = choose(table_ref[DEPTH] == depth, [lambda: old_ref[...], lambda: arrived])


def downward(abc_ref, bac_ref, field_ref, for_left_ref, for_right_ref, out_ref):
    extent = bac_ref.shape[0]
    diagonals = block_diagonals(split_terms(field_ref[...], extent), extent)
    out_ref[0] = contract(tall(abc_ref.at[0]), diagonals, for_left_ref, extent)
    out_ref[1] = contract(tall(bac_ref), diagonals, for_right_ref, extent)


def weigh_kernel(bac_ref, sides_ref, group_ref, out_ref, spread_ref):
    extent = bac_ref.shape[0]
    rows_out = out_ref.shape[1]
    per = LANES // extent
    half = extent // per
    rows_spread(bac_ref, split_terms(sides_ref[1], extent), spread_ref, extent)
    rows = lax.rem(iota((LANES, extent), 0), extent)
    lanes = iota((LANES, extent), 1)
    wanted = per * lax.rem(lanes, half) + lax.div(lanes, half)
    pick = jnp.where(rows == wanted, 1.0, 0.0).astype(jnp.bfloat16)
    group = lax.div(iota((half, LANES), 1), extent)
    for term, mat in enumerate(split_terms(sides_ref[0], extent)):
        permuted = dot(mat, pick)
        mine = permuted[:rows_out]
        for g in range(1, extent // rows_out):
            mine = jnp.where(group_ref[0] == g, permuted[g * rows_out : (g + 1) * rows_out], mine)
        mine = mine.astype(jnp.bfloat16)
        tiles = []
        for j in range(extent // per):
            given = [spread_ref[term, (per * j + q) * half : (per * j + q + 1) * half, :] for q in range(per)]
            stacked = []
            for p in range(per):
                row = None
                for q in range(per):
                    shift = (q - p) * extent % LANES
                    moved = pltpu.roll(given[q], shift, 1) if shift else given[q]
                    row = moved if row is None else jnp.where(group == q, moved, row)
                stacked.append(row)
            tiles.append(jnp.concatenate(stacked, axis=0).astype(jnp.bfloat16))
        for j in range(0, len(tiles), WIDE // LANES):
            wide = jnp.concatenate(tiles[j : j + WIDE // LANES], axis=1)
            out_ref[term, :, j * LANES : j * LANES + WIDE] = dot(mine, wide).astype(jnp.bfloat16)


def last_kernel(depth, *refs):
    came, (old_ref, table_ref, field_ref) = refs[:LOW], refs[LOW:]
    arrive(depth, came, old_ref, table_ref, field_ref)


def finish_kernel(*refs):
    table_ref, out_ref = refs[-2:]
    count = (len(refs) - 2) // 2
    rows, width = out_ref.shape[1:]
    extent = math.isqrt(width)
    total = None
    for field_ref, weighed_ref in zip(refs[:count], refs[count:-2]):
        part = weighted_sum(weighed_ref, field_ref[...], extent).astype(jnp.bfloat16).astype(jnp.float32)
        total = part if total is None else total + part
    total = jnp.where(table_ref[DEPTH] >= 0, total, 0.0).astype(jnp.bfloat16)
    for j in range(width // WIDE):
        out_ref[0, :, j * WIDE : (j + 1) * WIDE] = total[j * rows : (j + 1) * rows]


def weighted_sum(weighed_ref, field, extent):
    width = weighed_ref.shape[2]
    quads = WIDE // extent
    copies = pick_rows(extent, WIDE)
    same = lax.div(iota((WIDE, WIDE), 0), extent) == lax.div(iota((WIDE, WIDE), 1), extent)
    total = None
    for term, mat in enumerate(split_terms(field, extent)):
        narrow = dot(mat, pick_rows(extent, LANES).T)
        block = dot(narrow.T.astype(jnp.bfloat16), copies)
        diagonal = jnp.where(same, jnp.concatenate([block] * quads, axis=0), 0.0).astype(jnp.bfloat16)
        stacked = jnp.concatenate([weighed_ref[term, :, j : j + WIDE] for j in range(0, width, WIDE)], axis=0)
        part = dot(stacked, diagonal)
        total = part if total is None else total + part
    return total


def pick_rows(extent, width):
    rows = iota((extent, width), 0)
    return jnp.where(rows == lax.rem(iota((extent, width), 1), extent), 1.0, 0.0).astype(jnp.bfloat16)


VMEM = pl.BlockSpec(memory_space=pltpu.VMEM)
SMEM = pl.BlockSpec(memory_space=pltpu.SMEM)
HBM = pl.BlockSpec(memory_space=pltpu.HBM)


def call(kernel, out_shape, *operands, scratch=(), smem_out=(), in_hbm=()):
    shapes = out_shape if isinstance(out_shape, list) else [out_shape]
    specs = [SMEM if i in smem_out else VMEM for i in range(len(shapes))]
    taken = [SMEM if operand.dtype == jnp.int32 else VMEM for operand in operands]
    for i in in_hbm:
        taken[i] = HBM
    return pl.pallas_call(
        kernel,
        out_shape=out_shape,
        in_specs=taken,
        out_specs=specs if isinstance(out_shape, list) else specs[0],
        scratch_shapes=list(scratch),
        compiler_params=pltpu.CompilerParams(vmem_limit_bytes=16 * 2**20),
    )(*operands)


def exchange(value, mask, nodes):
    return lax.ppermute(value, "node", [(i, i ^ mask) for i in range(nodes)])


def high_exchange(value, nodes):
    return [value] + [exchange(value, high * LOW, nodes) for high in range(1, nodes // LOW)]


def low_exchange(values, nodes):
    return [values[0]] + [exchange(values[j], j, nodes) for j in range(1, LOW)]


def per_device(node_tensors, prim_ops, active, top_field, node_map):
    nodes = lax.axis_size("node")
    groups = lax.axis_size("term")
    depths = nodes.bit_length() - 1
    me = lax.axis_index("node").astype(jnp.int32)[None]
    slot_ids = jnp.arange(nodes, dtype=jnp.int32)
    apart = jnp.sum(jnp.where(node_map == 0, slot_ids, 0)) ^ jnp.sum(jnp.where(node_map == 2, slot_ids, 0))

    extent = node_tensors.shape[1]
    terms = prim_ops.shape[1]
    pairs = terms * extent // LANES
    flat = jax.ShapeDtypeStruct((extent, extent * extent), jnp.bfloat16)
    mats = jax.ShapeDtypeStruct((pairs * extent, LANES), jnp.bfloat16)
    two = jax.ShapeDtypeStruct((2,) + mats.shape, jnp.bfloat16)
    table_shape = jax.ShapeDtypeStruct((TABLE,), jnp.int32)
    spread = jax.ShapeDtypeStruct((terms, extent * extent * extent // LANES, LANES), jnp.bfloat16)
    part = jax.ShapeDtypeStruct((terms, extent // groups, extent * extent), jnp.bfloat16)
    space = pltpu.VMEM(spread.shape, jnp.float32)
    mixed = pltpu.VMEM(spread.shape, jnp.bfloat16)
    turn_space = pltpu.VMEM(spread.shape[1:], jnp.float32)
    group = lax.axis_index("term").astype(jnp.int32)[None]

    def others(value):
        return [
            lax.ppermute(value, "term", [(i, (i + shift) % groups) for i in range(groups)]) for shift in range(1, groups)
        ]

    def weigh(sides):
        return call(weigh_kernel, part, bac, sides, group, scratch=[space])

    def with_top(first, second):
        def branch(mask):
            return lambda first, second: (exchange(first, nodes // 2, nodes), exchange(second, mask, nodes))

        return lax.switch(apart - 1, [branch(mask) for mask in range(1, nodes)], first, second)

    bac, cba, left, right, field, mine, table = call(
        start_kernel,
        [flat, flat, mats, mats, mats, mats, table_shape],
        node_tensors,
        prim_ops,
        active,
        top_field,
        node_map,
        me,
        scratch=[
            pltpu.VMEM(node_tensors.shape, jnp.bfloat16),
            pltpu.VMEM(prim_ops.shape, jnp.bfloat16),
            pltpu.SMEM(active.shape, jnp.int32),
            pltpu.VMEM(top_field.shape, jnp.bfloat16),
            pltpu.SMEM(node_map.shape, jnp.int32),
            mixed,
            turn_space,
            pltpu.SMEM((nodes,), jnp.int32),
            pltpu.SemaphoreType.DMA((5,)),
        ],
        smem_out=(6,),
        in_hbm=(0, 1, 2, 3, 4),
    )
    bca, acb = call(turn_kernel, [flat, flat], bac, cba, scratch=[turn_space])

    for depth in range(depths - 2, 0, -1):
        parts = high_exchange(mine, nodes)
        came = low_exchange(call(relay_up_kernel, [two] * LOW, *parts, table), nodes)
        left, right, mine = call(
            functools.partial(up_kernel, depth),
            [mats, mats, mats],
            *came,
            bac,
            cba,
            left,
            right,
            table,
            scratch=[mixed],
        )

    came_left, came_right = with_top(mine, mine)
    sides, to_left, to_right, for_left, for_right = call(
        top_kernel,
        [two, mats, mats, spread, spread],
        node_tensors,
        bac,
        bca,
        acb,
        field,
        left,
        right,
        came_left,
        came_right,
        table,
    )
    came_left, came_right = with_top(to_left, to_right)
    all_sides = [sides] + others(sides)
    field, fields = call(
        below_top_kernel,
        [mats, two],
        node_tensors,
        bac,
        field,
        came_left,
        came_right,
        for_left,
        for_right,
        node_map,
        me,
    )
    weighed = []
    for depth in range(2, depths):
        parts = high_exchange(fields, nodes)
        share = -(-groups // (depths - 2))
        weighed += [weigh(sides) for sides in all_sides[(depth - 2) * share : (depth - 1) * share]]
        parts, weighed = lax.optimization_barrier((parts, weighed))
        came = low_exchange(call(relay_down_kernel, [mats] * LOW, *parts, table), nodes)
        if depth < depths - 1:
            field, fields = call(
                functools.partial(down_kernel, depth),
                [mats, two],
                *came,
                node_tensors,
                bac,
                field,
                for_left,
                for_right,
                table,
            )
    field = call(functools.partial(last_kernel, depths - 1), mats, *came, field, table)
    out = jax.ShapeDtypeStruct((1, extent // groups, extent * extent), jnp.bfloat16)
    return call(finish_kernel, out, field, *others(field), *weighed, table)


def solution(mesh):
    placed = (
        P("node", None, None),
        P("node", "term", None, None, None),
        P("node", "term", None),
        P("term", None, None),
        P(),
    )
    return jax.shard_map(
        per_device, mesh=mesh, in_specs=placed, out_specs=P("node", "term", None), check_vma=False
    )
```

```python
import functools
import math

import jax
import jax.numpy as jnp
from jax import lax
from jax.experimental import pallas as pl
from jax.experimental.pallas import tpu as pltpu
from jax.sharding import PartitionSpec as P

LANES = 128
WIDE = 256
BATCH = 2
PAD = 16
KEPT = 2**18


def dot(left, right):
    return jnp.dot(left, right, preferred_element_type=jnp.float32)


def iota(shape, dim):
    return lax.broadcasted_iota(jnp.int32, shape, dim)


def split_terms(packed, extent):
    per = LANES // extent
    wide = packed.astype(jnp.float32)
    out = []
    for term in range(per * packed.shape[0] // extent):
        block = wide[(term // per) * extent : (term // per + 1) * extent]
        mine = lax.div(iota(block.shape, 1), extent) == term % per
        out.append(jnp.where(mine, block, 0.0).astype(jnp.bfloat16))
    return out


def rows_spread(tensor_ref, mats, spread_ref, extent):
    per = LANES // extent
    half = extent // per
    stack = jnp.concatenate(mats, axis=0)
    for chunk in range(extent * extent // WIDE):
        piece = tensor_ref[:, chunk * WIDE : (chunk + 1) * WIDE]
        result = dot(stack, jnp.concatenate([piece] * per, axis=0))
        for part in range(WIDE // LANES):
            i = chunk * (WIDE // LANES) + part
            for term in range(len(mats)):
                spread_ref[term, pl.ds(i, extent, stride=half), :] = result[
                    term * extent : (term + 1) * extent, part * LANES : (part + 1) * LANES
                ]


SUB = 8


def rows_apply(tensor_ref, mats, mixed_ref, extent):
    per = LANES // extent
    quads = WIDE // extent
    halves = SUB // quads
    count = 2 * halves
    stack = jnp.concatenate(mats, axis=0)
    row = iota((extent // SUB, SUB, LANES), 1)
    for first in range(0, extent // per, count):
        piece = tensor_ref[:, first * LANES : (first + count) * LANES]
        result = dot(stack, jnp.concatenate([piece] * per, axis=0))
        for term in range(len(mats)):
            tiles = [
                result[term * extent : (term + 1) * extent, k * LANES : (k + 1) * LANES].reshape(row.shape)
                for k in range(count)
            ]
            for half in range(halves):
                wanted = []
                for start in range(0, count, halves):
                    block = None
                    for k in range(halves):
                        shift = (k - half) * quads % SUB
                        moved = pltpu.roll(tiles[start + k], shift, 1) if shift else tiles[start + k]
                        block = moved if block is None else jnp.where(lax.div(row, quads) == k, moved, block)
                    wanted.append(block)
                packed = jnp.concatenate(wanted, axis=1).astype(jnp.bfloat16)
                for m in range(extent // SUB):
                    base = (m * halves + half) * (extent // per) * quads + first * quads
                    mixed_ref[term, base : base + count * quads, :] = packed[m]


def block_diagonals(mats, extent):
    per = LANES // extent
    quads = WIDE // extent
    rows = lax.rem(iota((LANES, WIDE), 0), extent)
    lanes = iota((LANES, WIDE), 1)
    wanted = per * lax.div(lax.rem(lanes, WIDE // per), quads) + lax.div(lanes, WIDE // per)
    pick = jnp.where(rows == wanted, 1.0, 0.0).astype(jnp.bfloat16)
    spread = dot(jnp.concatenate(mats, axis=0), pick)
    lanes = iota((WIDE, WIDE), 1)
    same = lax.div(iota((WIDE, WIDE), 0), extent) == lax.rem(lanes, quads)
    out = []
    for term in range(len(mats)):
        block = spread[term * extent : (term + 1) * extent]
        out.append(jnp.where(same, jnp.concatenate([block] * quads, axis=0), 0.0).astype(jnp.bfloat16))
    return out


def tall(tensor_ref):
    width = tensor_ref.shape[1]
    return jnp.concatenate([tensor_ref[:, j : j + WIDE] for j in range(0, width, WIDE)], axis=0)


def pair_up(accs, extent):
    per = LANES // extent
    out = []
    for first in range(0, len(accs), per):
        blocks = None
        for lo in range(per):
            acc = accs[first + lo]
            group = lax.div(iota((extent, LANES), 1), extent)
            kept = jnp.zeros((extent, LANES), jnp.float32)
            for p in range(per):
                kept = jnp.where(group == p, acc[p * extent : (p + 1) * extent], kept)
            total = kept
            for p in range(1, per):
                total = total + pltpu.roll(kept, p * extent, 1)
            blocks = total if blocks is None else jnp.where(group == lo, total, blocks)
        out.append(blocks)
    return out


def below_diagonal(shape, extent):
    rows, lanes = iota(shape, 0), lax.rem(iota(shape, 1), extent)
    return rows > lanes, rows == lanes


def fold(blocks):
    extent = blocks[0].shape[0]
    below, on = below_diagonal(blocks[0].shape, extent)
    out = []
    for first in range(0, len(blocks), 2):
        lower, upper = blocks[first], blocks[min(first + 1, len(blocks) - 1)]
        out.append(jnp.where(jnp.logical_or(below, on), lower, upper))
        row = jnp.sum(jnp.where(on, upper, 0.0), axis=0, keepdims=True)
        out.append(jnp.broadcast_to(row, (PAD, LANES)))
    return jnp.concatenate(out, axis=0).astype(jnp.bfloat16)


def unfold(message, pairs):
    height = message.shape[0] // (-(-pairs // 2))
    extent = height - PAD
    wide = message.astype(jnp.float32)
    out = []
    for base in range(0, message.shape[0], height):
        body, row = wide[base : base + extent], wide[base + extent : base + extent + 1]
        below, on = below_diagonal(body.shape, extent)
        turned = body.T
        parts = [turned[k : k + extent] for k in range(0, LANES, extent)]
        turned = jnp.concatenate(parts, axis=1)
        out.append(jnp.where(jnp.logical_or(below, on), body, turned))
        out.append(jnp.where(below, turned, jnp.where(on, row, body)))
    return jnp.concatenate(out[:pairs], axis=0).astype(jnp.bfloat16)


def contract(stacked, diagonals, mixed, extent):
    per = LANES // extent
    groups = stacked.shape[0] // extent
    lefts = []
    for diagonal in diagonals:
        moved = dot(stacked, diagonal).astype(jnp.bfloat16)
        for p in range(per):
            lanes = slice(p * (WIDE // per), (p + 1) * (WIDE // per))
            lefts.append(jnp.concatenate([moved[j * extent : (j + 1) * extent, lanes] for j in range(groups)], axis=1))
    accs = []
    for first in range(0, len(diagonals), BATCH):
        left = jnp.concatenate(lefts[first * per : (first + BATCH) * per], axis=0)
        right = jnp.concatenate([mixed[term] for term in range(first, first + BATCH)], axis=1)
        result = dot(left, right)
        for k in range(BATCH):
            accs.append(result[k * LANES : (k + 1) * LANES, k * LANES : (k + 1) * LANES])
    return fold(pair_up(accs, extent))


def swap(value, turn_ref, out_ref, extent):
    per = LANES // extent
    half = extent // per
    rows = iota((extent, extent), 0)
    wanted = per * lax.rem(rows, half) + lax.div(rows, half)
    order = jnp.where(iota((extent, extent), 1) == wanted, 1.0, 0.0).astype(jnp.bfloat16)
    sorted_rows = dot(order, value)
    group = lax.div(iota((half, LANES), 1), extent)
    for j in range(extent // per):
        given = [sorted_rows[p * half : (p + 1) * half, j * LANES : (j + 1) * LANES] for p in range(per)]
        for q in range(per):
            row = None
            for p in range(per):
                shift = (p - q) * extent % LANES
                moved = pltpu.roll(given[p], shift, 1) if shift else given[p]
                row = moved if row is None else jnp.where(group == p, moved, row)
            turn_ref[pl.ds(per * j + q, half, stride=extent), :] = row
    for i in range(half):
        out_ref[:, i * LANES : (i + 1) * LANES] = turn_ref[i * extent : (i + 1) * extent, :].astype(jnp.bfloat16)


def flip(value, extent):
    per = LANES // extent
    wide = value.astype(jnp.float32)
    tiles = []
    for j in range(extent // per):
        turned = wide[:, j * LANES : (j + 1) * LANES].T
        tiles.append(jnp.concatenate([turned[p * extent : (p + 1) * extent] for p in range(per)], axis=1))
    return jnp.concatenate(tiles, axis=1).astype(jnp.bfloat16)


DEPTH, FROM_LEFT, FROM_RIGHT, FROM_PARENT, UP_RELAY, DOWN_RELAY, TABLE = 0, 1, 2, 3, 8, 16, 24
LOW = 4


def fill_table(map_ref, me, inverse_ref, table_ref):
    nodes = map_ref.shape[0]

    def note(slot, carry):
        inverse_ref[map_ref[slot]] = slot
        return carry

    lax.fori_loop(0, nodes, note, 0)
    low = lax.rem(me, LOW)
    high = lax.div(me, LOW)

    def routes(slot):
        position = map_ref[slot]
        last = jnp.int32(nodes - 1)
        left = inverse_ref[jnp.minimum(2 * position + 1, last)]
        right = inverse_ref[jnp.minimum(2 * position + 2, last)]
        parent = inverse_ref[lax.div(jnp.maximum(position - 1, 0), 2)]
        return position, left, right, parent

    position, left, right, parent = routes(me)
    depth = jnp.int32(0)
    for power in range(1, nodes.bit_length() - 1):
        depth = depth + jnp.where(position + 1 >= 2**power, 1, 0)
    table_ref[DEPTH] = jnp.where(position >= nodes - 1, -1, depth)
    table_ref[FROM_LEFT] = lax.rem(left, LOW) ^ low
    table_ref[FROM_RIGHT] = lax.rem(right, LOW) ^ low
    table_ref[FROM_PARENT] = lax.rem(parent, LOW) ^ low
    for j in range(LOW):
        position, left, right, parent = routes(high * LOW + (low ^ j))
        table_ref[UP_RELAY + 2 * j] = lax.div(left, LOW) ^ high
        table_ref[UP_RELAY + 2 * j + 1] = lax.div(right, LOW) ^ high
        table_ref[DOWN_RELAY + j] = 2 * (lax.div(parent, LOW) ^ high) + lax.rem(position + 1, 2)


def choose(index, choices):
    out = choices[0]().astype(jnp.float32)
    for k in range(1, len(choices)):
        out = jnp.where(index == k, choices[k]().astype(jnp.float32), out)
    return out.astype(jnp.bfloat16)


def loads(refs, *where):
    return [lambda ref=ref: ref[where] if where else ref[...] for ref in refs]


def start_kernel(
    tensor_hbm, prim_hbm, active_hbm, top_hbm, map_hbm, me_ref,
    abc_ref, bac_ref, cba_ref, left_ref, right_ref, field_ref, out_ref, table_ref,
    prim_ref, active_ref, top_ref, map_ref, mixed_ref, turn_ref, inverse_ref, sems,
):
    given = (tensor_hbm.at[0], prim_hbm, top_hbm, active_hbm, map_hbm)
    held = (abc_ref, prim_ref, top_ref, active_ref, map_ref)
    copies = [pltpu.make_async_copy(*pair, sems.at[i]) for i, pair in enumerate(zip(given, held))]
    for copy in copies:
        copy.start()
    extent = abc_ref.shape[0]
    per = LANES // extent
    terms = prim_ref.shape[1]
    for copy in copies[::-1]:
        copy.wait()
        if copy is copies[-1]:
            fill_table(map_ref, me_ref[0], inverse_ref, table_ref)
    eye = jnp.where(iota((extent, extent), 0) == iota((extent, extent), 1), 1.0, 0.0)

    def operator(term, side):
        return jnp.where(active_ref[0, term, side] == 1, prim_ref[0, term, side].astype(jnp.float32), eye)

    for first in range(0, terms, per):
        rows = pl.ds(first // per * extent, extent)
        for side, ref in ((0, left_ref), (1, right_ref)):
            side_by_side = [operator(first + lo, side) for lo in range(per)]
            ref[rows, :] = jnp.concatenate(side_by_side, axis=1).astype(jnp.bfloat16)
        fields = [top_ref[first + lo].astype(jnp.float32) for lo in range(per)]
        field_ref[rows, :] = jnp.concatenate(fields, axis=1).astype(jnp.bfloat16)
    swap(abc_ref[...], turn_ref, bac_ref, extent)
    cba_ref[...] = flip(abc_ref[...], extent)
    rows_apply(bac_ref, split_terms(right_ref[...], extent), mixed_ref, extent)
    diagonals = block_diagonals(split_terms(left_ref[...], extent), extent)
    out_ref[...] = contract(tall(cba_ref), diagonals, mixed_ref, extent)


def turn_kernel(bac_ref, cba_ref, turned_ref, turn_ref):
    extent = bac_ref.shape[0]
    swap(cba_ref[...], turn_ref, turned_ref.at[0], extent)
    swap(flip(bac_ref[...], extent), turn_ref, turned_ref.at[1], extent)


def relay_up_kernel(*refs):
    parts, table_ref, outs = refs[:-5], refs[-5], refs[-4:]
    for j, out in enumerate(outs):
        for side in range(2):
            out[side] = choose(table_ref[UP_RELAY + 2 * j + side], loads(parts))


def relay_down_kernel(*refs):
    parts, table_ref, outs = refs[:-5], refs[-5], refs[-4:]
    choices = [f for part in parts for side in range(2) for f in loads([part], side)]
    for j, out in enumerate(outs):
        out[...] = choose(table_ref[DOWN_RELAY + j], choices)


def up_kernel(depth, *refs):
    came, (bac_ref, cba_ref, old_left_ref, old_right_ref, table_ref) = refs[:LOW], refs[LOW : LOW + 5]
    left_ref, right_ref, out_ref, mixed_ref = refs[LOW + 5 :]
    extent = bac_ref.shape[0]
    now = table_ref[DEPTH] == depth
    pairs = old_left_ref.shape[0] // extent
    left = unfold(choose(table_ref[FROM_LEFT], loads(came, 0)), pairs)
    right = unfold(choose(table_ref[FROM_RIGHT], loads(came, 1)), pairs)
    left_ref[...] = choose(now, [lambda: old_left_ref[...], lambda: left])
    right_ref[...] = choose(now, [lambda: old_right_ref[...], lambda: right])
    rows_apply(bac_ref, split_terms(right_ref[...], extent), mixed_ref, extent)
    diagonals = block_diagonals(split_terms(left_ref[...], extent), extent)
    out_ref[...] = contract(tall(cba_ref), diagonals, mixed_ref, extent)


def top_kernel(
    abc_ref, bac_ref, turned_ref, field_ref, old_left_ref, old_right_ref, came_left_ref, came_right_ref, table_ref,
    sides_ref, out_ref, mixed_ref,
):
    now = table_ref[DEPTH] == 0
    pairs = old_left_ref.shape[0] // abc_ref.shape[0]
    sides_ref[0] = choose(now, [lambda: old_left_ref[...], lambda: unfold(came_left_ref[...], pairs)])
    sides_ref[1] = choose(now, [lambda: old_right_ref[...], lambda: unfold(came_right_ref[...], pairs)])
    downward(abc_ref, bac_ref, turned_ref, field_ref, sides_ref, out_ref, mixed_ref)


def below_top_kernel(
    abc_ref, bac_ref, turned_ref, old_ref, came_left_ref, came_right_ref, sides_ref, map_ref, me_ref,
    field_ref, out_ref, mixed_ref,
):
    position = map_ref[me_ref[0]]
    came = unfold(choose(position == 2, loads([came_left_ref, came_right_ref])), old_ref.shape[0] // abc_ref.shape[0])
    now = jnp.logical_or(position == 1, position == 2)
    field_ref[...] = choose(now, [lambda: old_ref[...], lambda: came])
    downward(abc_ref, bac_ref, turned_ref, field_ref, sides_ref, out_ref, mixed_ref)


def down_kernel(depth, *refs):
    came, (abc_ref, bac_ref, turned_ref, old_ref, sides_ref, table_ref) = refs[:LOW], refs[LOW : LOW + 6]
    field_ref, out_ref, mixed_ref = refs[LOW + 6 :]
    arrive(depth, old_ref.shape[0] // abc_ref.shape[0], came, old_ref, table_ref, field_ref)
    downward(abc_ref, bac_ref, turned_ref, field_ref, sides_ref, out_ref, mixed_ref)


def arrive(depth, pairs, came, old_ref, table_ref, field_ref):
    arrived = choose(table_ref[FROM_PARENT], loads(came))
    arrived = unfold(arrived, pairs)
    field_ref[...] = choose(table_ref[DEPTH] == depth, [lambda: old_ref[...], lambda: arrived])


def downward(abc_ref, bac_ref, turned_ref, field_ref, sides_ref, out_ref, mixed_ref):
    extent = bac_ref.shape[0]
    diagonals = block_diagonals(split_terms(field_ref[...], extent), extent)
    rows_apply(turned_ref.at[0], split_terms(sides_ref[1], extent), mixed_ref.at[0], extent)
    rows_apply(turned_ref.at[1], split_terms(sides_ref[0], extent), mixed_ref.at[1], extent)
    out_ref[0] = contract(tall(abc_ref), diagonals, mixed_ref.at[0], extent)
    out_ref[1] = contract(tall(bac_ref), diagonals, mixed_ref.at[1], extent)


def weigh_kernel(pair, bac_ref, sides_ref, group_ref, out_ref, spread_ref):
    extent = bac_ref.shape[0]
    mine = slice(pair * extent, (pair + 1) * extent)
    rows_out = out_ref.shape[1]
    per = LANES // extent
    half = extent // per
    rows_spread(bac_ref, split_terms(sides_ref[1, mine], extent), spread_ref, extent)
    rows = lax.rem(iota((LANES, extent), 0), extent)
    lanes = iota((LANES, extent), 1)
    wanted = per * lax.rem(lanes, half) + lax.div(lanes, half)
    pick = jnp.where(rows == wanted, 1.0, 0.0).astype(jnp.bfloat16)
    group = lax.div(iota((half, LANES), 1), extent)
    for term, mat in enumerate(split_terms(sides_ref[0, mine], extent)):
        permuted = dot(mat, pick)
        kept = permuted[:rows_out]
        for g in range(1, extent // rows_out):
            kept = jnp.where(group_ref[0] == g, permuted[g * rows_out : (g + 1) * rows_out], kept)
        kept = kept.astype(jnp.bfloat16)
        tiles = []
        for j in range(extent // per):
            given = [spread_ref[term, (per * j + q) * half : (per * j + q + 1) * half, :] for q in range(per)]
            stacked = []
            for p in range(per):
                row = None
                for q in range(per):
                    shift = (q - p) * extent % LANES
                    moved = pltpu.roll(given[q], shift, 1) if shift else given[q]
                    row = moved if row is None else jnp.where(group == q, moved, row)
                stacked.append(row)
            tiles.append(jnp.concatenate(stacked, axis=0).astype(jnp.bfloat16))
        for j in range(0, len(tiles), WIDE // LANES):
            wide = jnp.concatenate(tiles[j : j + WIDE // LANES], axis=1)
            out_ref[term, :, j * LANES : j * LANES + WIDE] = dot(kept, wide).astype(jnp.bfloat16)


def last_kernel(depth, pairs, *refs):
    came, (old_ref, table_ref, field_ref) = refs[:LOW], refs[LOW:]
    arrive(depth, pairs, came, old_ref, table_ref, field_ref)


def finish_kernel(groups, *refs):
    table_ref, out_ref = refs[-2:]
    rows, width = out_ref.shape[1:]
    pairs = (len(refs) - 2 - groups) // groups
    total = None
    for g in range(groups):
        weighed = refs[groups + g * pairs : groups + (g + 1) * pairs]
        part = weighted_sum(weighed, refs[g][...], math.isqrt(width)).astype(jnp.bfloat16).astype(jnp.float32)
        total = part if total is None else total + part
    total = jnp.where(table_ref[DEPTH] >= 0, total, 0.0).astype(jnp.bfloat16)
    for j in range(width // WIDE):
        out_ref[0, :, j * WIDE : (j + 1) * WIDE] = total[j * rows : (j + 1) * rows]


def weighted_sum(weighed_refs, field, extent):
    per, _, width = weighed_refs[0].shape
    quads = WIDE // extent
    copies = pick_rows(LANES, WIDE, extent)
    spread = dot(jnp.concatenate(split_terms(field, extent), axis=0), copies)
    same = lax.div(iota((WIDE, WIDE), 0), extent) == lax.div(iota((WIDE, WIDE), 1), extent)
    total = None
    for term in range(per * len(weighed_refs)):
        weighed_ref = weighed_refs[term // per]
        block = spread[term * extent : (term + 1) * extent]
        diagonal = jnp.where(same, jnp.concatenate([block] * quads, axis=0), 0.0).astype(jnp.bfloat16)
        pieces = [weighed_ref[term % per, :, j : j + WIDE] for j in range(0, width, WIDE)]
        part = dot(jnp.concatenate(pieces, axis=0), diagonal)
        total = part if total is None else total + part
    return total


def pick_rows(rows, lanes, extent):
    same = lax.rem(iota((rows, lanes), 0), extent) == lax.rem(iota((rows, lanes), 1), extent)
    return jnp.where(same, 1.0, 0.0).astype(jnp.bfloat16)


VMEM = pl.BlockSpec(memory_space=pltpu.VMEM)
SMEM = pl.BlockSpec(memory_space=pltpu.SMEM)
HBM = pl.BlockSpec(memory_space=pltpu.HBM)


def call(kernel, out_shape, *operands, scratch=(), smem_out=(), in_hbm=(), kept=True, beside=()):
    shapes = out_shape if isinstance(out_shape, list) else [out_shape]
    specs = [SMEM if i in smem_out else VMEM for i in range(len(shapes))]
    taken = [SMEM if operand.dtype == jnp.int32 else VMEM for operand in operands]
    operands = list(operands)
    for i, operand in enumerate(operands):
        if i in in_hbm:
            taken[i] = HBM
            operands[i] = pltpu.with_memory_space_constraint(operand, pltpu.HBM)
        elif operand.size >= KEPT:
            operands[i] = pltpu.with_memory_space_constraint(operand, pltpu.VMEM)
    shapes = [pltpu.VMEM(x.shape, x.dtype) if kept and x.size >= KEPT else x for x in shapes]
    given = len(operands)
    operands += [pltpu.with_memory_space_constraint(x, pltpu.VMEM) for x in beside]

    def without(*refs):
        kernel(*refs[:given], *refs[len(operands) :])

    return pl.pallas_call(
        without,
        out_shape=shapes if isinstance(out_shape, list) else shapes[0],
        in_specs=taken + [VMEM] * len(beside),
        out_specs=specs if isinstance(out_shape, list) else specs[0],
        scratch_shapes=list(scratch),
        compiler_params=pltpu.CompilerParams(vmem_limit_bytes=16 * 2**20),
    )(*operands)


def exchange(value, mask, nodes):
    return lax.ppermute(value, "node", [(i, i ^ mask) for i in range(nodes)])


def high_exchange(value, nodes):
    return [value] + [exchange(value, high * LOW, nodes) for high in range(1, nodes // LOW)]


def low_exchange(values, nodes):
    return [values[0]] + [exchange(values[j], j, nodes) for j in range(1, LOW)]


def per_device(node_tensors, prim_ops, active, top_field, node_map):
    nodes = lax.axis_size("node")
    groups = lax.axis_size("term")
    depths = nodes.bit_length() - 1
    me = lax.axis_index("node").astype(jnp.int32)[None]
    slot_ids = jnp.arange(nodes, dtype=jnp.int32)
    apart = jnp.sum(jnp.where(node_map == 0, slot_ids, 0)) ^ jnp.sum(jnp.where(node_map == 2, slot_ids, 0))

    extent = node_tensors.shape[1]
    terms = prim_ops.shape[1]
    pairs = terms * extent // LANES
    flat = jax.ShapeDtypeStruct((extent, extent * extent), jnp.bfloat16)
    mats = jax.ShapeDtypeStruct((pairs * extent, LANES), jnp.bfloat16)
    two = jax.ShapeDtypeStruct((2,) + mats.shape, jnp.bfloat16)
    message = jax.ShapeDtypeStruct((-(-pairs // 2) * (extent + PAD), LANES), jnp.bfloat16)
    messages = jax.ShapeDtypeStruct((2,) + message.shape, jnp.bfloat16)
    table_shape = jax.ShapeDtypeStruct((TABLE,), jnp.int32)
    spread = jax.ShapeDtypeStruct((terms, extent * extent * extent // LANES, LANES), jnp.bfloat16)
    part = jax.ShapeDtypeStruct((LANES // extent, extent // groups, extent * extent), jnp.bfloat16)
    space = pltpu.VMEM((LANES // extent,) + spread.shape[1:], jnp.float32)
    both = [pltpu.VMEM((2,) + spread.shape, jnp.bfloat16)]
    mixed_space = pltpu.VMEM(spread.shape, jnp.bfloat16)
    turn_space = pltpu.VMEM(spread.shape[1:], jnp.float32)
    group = lax.axis_index("term").astype(jnp.int32)[None]

    def others(value):
        return [
            lax.ppermute(value, "term", [(i, (i + shift) % groups) for i in range(groups)]) for shift in range(1, groups)
        ]

    def weigh_beside(count, values):
        for sides, pair in to_weigh[len(weighed) : len(weighed) + count]:
            weighed.append(call(functools.partial(weigh_kernel, pair), part, bac, sides, group, scratch=[space]))
        return lax.optimization_barrier((values, weighed[-count:]))

    def with_top(first, second):
        def branch(mask):
            return lambda first, second: (exchange(first, nodes // 2, nodes), exchange(second, mask, nodes))

        return lax.switch(apart - 1, [branch(mask) for mask in range(1, nodes)], first, second)

    abc, bac, cba, left, right, field, mine, table = call(
        start_kernel,
        [flat, flat, flat, mats, mats, mats, message, table_shape],
        node_tensors,
        prim_ops,
        active,
        top_field,
        node_map,
        me,
        scratch=[
            pltpu.VMEM(prim_ops.shape, jnp.bfloat16),
            pltpu.SMEM(active.shape, jnp.int32),
            pltpu.VMEM(top_field.shape, jnp.bfloat16),
            pltpu.SMEM(node_map.shape, jnp.int32),
            mixed_space,
            turn_space,
            pltpu.SMEM((nodes,), jnp.int32),
            pltpu.SemaphoreType.DMA((5,)),
        ],
        smem_out=(7,),
        in_hbm=(0, 1, 2, 3, 4),
    )
    turned = call(turn_kernel, jax.ShapeDtypeStruct((2,) + flat.shape, flat.dtype), bac, cba, scratch=[turn_space])

    for depth in range(depths - 2, 0, -1):
        parts = high_exchange(mine, nodes)
        came = low_exchange(call(relay_up_kernel, [messages] * LOW, *parts, table), nodes)
        left, right, mine = call(
            functools.partial(up_kernel, depth),
            [mats, mats, message],
            *came,
            bac,
            cba,
            left,
            right,
            table,
            scratch=[mixed_space],
        )

    came_left, came_right = with_top(mine, mine)
    sides, fields = call(
        top_kernel,
        [two, messages],
        abc,
        bac,
        turned,
        field,
        left,
        right,
        came_left,
        came_right,
        table,
        scratch=both,
    )
    came_left, came_right = with_top(fields[0], fields[1])
    to_weigh = [(each, pair) for each in [sides] + others(sides) for pair in range(pairs)]
    share = -(-len(to_weigh) // (2 * (depths - 2)))
    field, fields = call(
        below_top_kernel,
        [mats, messages],
        abc,
        bac,
        turned,
        field,
        came_left,
        came_right,
        sides,
        node_map,
        me,
        scratch=both,
    )
    weighed = []
    for depth in range(2, depths):
        parts = high_exchange(fields, nodes)
        parts, weighed[-share:] = weigh_beside(share, parts)
        came = low_exchange(call(relay_down_kernel, [message] * LOW, *parts, table), nodes)
        came, weighed[-share:] = weigh_beside(share, came)
        if depth < depths - 1:
            field, fields = call(
                functools.partial(down_kernel, depth),
                [mats, messages],
                *came,
                abc,
                bac,
                turned,
                field,
                sides,
                table,
                scratch=both,
            )
    field = call(functools.partial(last_kernel, depths - 1, pairs), mats, *came, field, table)
    out = jax.ShapeDtypeStruct((1, extent // groups, extent * extent), jnp.bfloat16)
    return call(functools.partial(finish_kernel, groups), out, field, *others(field), *weighed, table, kept=False)


def solution(mesh):
    placed = (
        P("node", None, None),
        P("node", "term", None, None, None),
        P("node", "term", None),
        P("term", None, None),
        P(),
    )
    return jax.shard_map(
        per_device, mesh=mesh, in_specs=placed, out_specs=P("node", "term", None), check_vma=False
    )
```

```python
import functools
import math

import jax
import jax.numpy as jnp
from jax import lax
from jax.experimental import pallas as pl
from jax.experimental.pallas import tpu as pltpu
from jax.sharding import PartitionSpec as P

LANES = 128
WIDE = 256
BATCH = 2
PAD = 16
KEPT = 2**18


def dot(left, right):
    return jnp.dot(left, right, preferred_element_type=jnp.float32)


def iota(shape, dim):
    return lax.broadcasted_iota(jnp.int32, shape, dim)


def split_terms(packed, extent):
    per = LANES // extent
    wide = packed.astype(jnp.float32)
    out = []
    for term in range(per * packed.shape[0] // extent):
        block = wide[(term // per) * extent : (term // per + 1) * extent]
        mine = lax.div(iota(block.shape, 1), extent) == term % per
        out.append(jnp.where(mine, block, 0.0).astype(jnp.bfloat16))
    return out


def rows_spread(tensor_ref, mats, spread_ref, extent):
    per = LANES // extent
    half = extent // per
    stack = jnp.concatenate(mats, axis=0)
    for chunk in range(extent * extent // WIDE):
        piece = tensor_ref[:, chunk * WIDE : (chunk + 1) * WIDE]
        result = dot(stack, jnp.concatenate([piece] * per, axis=0))
        for part in range(WIDE // LANES):
            i = chunk * (WIDE // LANES) + part
            for term in range(len(mats)):
                spread_ref[term, pl.ds(i, extent, stride=half), :] = result[
                    term * extent : (term + 1) * extent, part * LANES : (part + 1) * LANES
                ]


SUB = 8


def rows_apply(tensor_ref, mats, mixed_ref, extent):
    per = LANES // extent
    quads = WIDE // extent
    halves = SUB // quads
    count = 2 * halves
    stack = jnp.concatenate(mats, axis=0)
    row = iota((extent // SUB, SUB, LANES), 1)
    for first in range(0, extent // per, count):
        piece = tensor_ref[:, first * LANES : (first + count) * LANES]
        result = dot(stack, jnp.concatenate([piece] * per, axis=0))
        for term in range(len(mats)):
            tiles = [
                result[term * extent : (term + 1) * extent, k * LANES : (k + 1) * LANES].reshape(row.shape)
                for k in range(count)
            ]
            for half in range(halves):
                wanted = []
                for start in range(0, count, halves):
                    block = None
                    for k in range(halves):
                        shift = (k - half) * quads % SUB
                        moved = pltpu.roll(tiles[start + k], shift, 1) if shift else tiles[start + k]
                        block = moved if block is None else jnp.where(lax.div(row, quads) == k, moved, block)
                    wanted.append(block)
                packed = jnp.concatenate(wanted, axis=1).astype(jnp.bfloat16)
                for m in range(extent // SUB):
                    base = (m * halves + half) * (extent // per) * quads + first * quads
                    mixed_ref[term, base : base + count * quads, :] = packed[m]


def block_diagonals(mats, extent):
    per = LANES // extent
    quads = WIDE // extent
    rows = lax.rem(iota((LANES, WIDE), 0), extent)
    lanes = iota((LANES, WIDE), 1)
    wanted = per * lax.div(lax.rem(lanes, WIDE // per), quads) + lax.div(lanes, WIDE // per)
    pick = jnp.where(rows == wanted, 1.0, 0.0).astype(jnp.bfloat16)
    spread = dot(jnp.concatenate(mats, axis=0), pick)
    lanes = iota((WIDE, WIDE), 1)
    same = lax.div(iota((WIDE, WIDE), 0), extent) == lax.rem(lanes, quads)
    out = []
    for term in range(len(mats)):
        block = spread[term * extent : (term + 1) * extent]
        out.append(jnp.where(same, jnp.concatenate([block] * quads, axis=0), 0.0).astype(jnp.bfloat16))
    return out


def tall(tensor_ref):
    width = tensor_ref.shape[1]
    return jnp.concatenate([tensor_ref[:, j : j + WIDE] for j in range(0, width, WIDE)], axis=0)


def pair_up(accs, extent):
    per = LANES // extent
    out = []
    for first in range(0, len(accs), per):
        blocks = None
        for lo in range(per):
            acc = accs[first + lo]
            group = lax.div(iota((extent, LANES), 1), extent)
            kept = jnp.zeros((extent, LANES), jnp.float32)
            for p in range(per):
                kept = jnp.where(group == p, acc[p * extent : (p + 1) * extent], kept)
            total = kept
            for p in range(1, per):
                total = total + pltpu.roll(kept, p * extent, 1)
            blocks = total if blocks is None else jnp.where(group == lo, total, blocks)
        out.append(blocks)
    return out


def below_diagonal(shape, extent):
    rows, lanes = iota(shape, 0), lax.rem(iota(shape, 1), extent)
    return rows > lanes, rows == lanes


def fold(blocks):
    extent = blocks[0].shape[0]
    below, on = below_diagonal(blocks[0].shape, extent)
    out = []
    for first in range(0, len(blocks), 2):
        lower, upper = blocks[first], blocks[min(first + 1, len(blocks) - 1)]
        out.append(jnp.where(jnp.logical_or(below, on), lower, upper))
        row = jnp.sum(jnp.where(on, upper, 0.0), axis=0, keepdims=True)
        out.append(jnp.broadcast_to(row, (PAD, LANES)))
    return jnp.concatenate(out, axis=0).astype(jnp.bfloat16)


def unfold(message, pairs):
    height = message.shape[0] // (-(-pairs // 2))
    extent = height - PAD
    wide = message.astype(jnp.float32)
    out = []
    for base in range(0, message.shape[0], height):
        body, row = wide[base : base + extent], wide[base + extent : base + extent + 1]
        below, on = below_diagonal(body.shape, extent)
        turned = body.T
        parts = [turned[k : k + extent] for k in range(0, LANES, extent)]
        turned = jnp.concatenate(parts, axis=1)
        out.append(jnp.where(jnp.logical_or(below, on), body, turned))
        out.append(jnp.where(below, turned, jnp.where(on, row, body)))
    return jnp.concatenate(out[:pairs], axis=0).astype(jnp.bfloat16)


def apply_lanes(stacked, diagonals, extent):
    per = LANES // extent
    groups = stacked.shape[0] // extent
    lefts = []
    for diagonal in diagonals:
        moved = dot(stacked, diagonal).astype(jnp.bfloat16)
        for p in range(per):
            lanes = slice(p * (WIDE // per), (p + 1) * (WIDE // per))
            lefts.append(jnp.concatenate([moved[j * extent : (j + 1) * extent, lanes] for j in range(groups)], axis=1))
    return lefts


def contract(lefts, mixed, extent):
    per = LANES // extent
    accs = []
    for first in range(0, len(lefts) // per, BATCH):
        left = jnp.concatenate(lefts[first * per : (first + BATCH) * per], axis=0)
        right = jnp.concatenate([mixed[term] for term in range(first, first + BATCH)], axis=1)
        result = dot(left, right)
        for k in range(BATCH):
            accs.append(result[k * LANES : (k + 1) * LANES, k * LANES : (k + 1) * LANES])
    return fold(pair_up(accs, extent))


def swap(value, turn_ref, out_ref, extent):
    per = LANES // extent
    half = extent // per
    rows = iota((extent, extent), 0)
    wanted = per * lax.rem(rows, half) + lax.div(rows, half)
    order = jnp.where(iota((extent, extent), 1) == wanted, 1.0, 0.0).astype(jnp.bfloat16)
    sorted_rows = dot(order, value)
    group = lax.div(iota((half, LANES), 1), extent)
    for j in range(extent // per):
        given = [sorted_rows[p * half : (p + 1) * half, j * LANES : (j + 1) * LANES] for p in range(per)]
        for q in range(per):
            row = None
            for p in range(per):
                shift = (p - q) * extent % LANES
                moved = pltpu.roll(given[p], shift, 1) if shift else given[p]
                row = moved if row is None else jnp.where(group == p, moved, row)
            turn_ref[pl.ds(per * j + q, half, stride=extent), :] = row
    for i in range(half):
        out_ref[:, i * LANES : (i + 1) * LANES] = turn_ref[i * extent : (i + 1) * extent, :].astype(jnp.bfloat16)


def flip(value, extent):
    per = LANES // extent
    wide = value.astype(jnp.float32)
    tiles = []
    for j in range(extent // per):
        turned = wide[:, j * LANES : (j + 1) * LANES].T
        tiles.append(jnp.concatenate([turned[p * extent : (p + 1) * extent] for p in range(per)], axis=1))
    return jnp.concatenate(tiles, axis=1).astype(jnp.bfloat16)


DEPTH, FROM_LEFT, FROM_RIGHT, FROM_PARENT, POSITION, GROUP, APART, UP_RELAY, DOWN_RELAY, TABLE = *range(7), 8, 16, 24
LOW = 4


def entry(table_ref, row):
    return table_ref[row : row + 1, :]


def fill_table(map_ref, me, inverse_ref, table_ref):
    def put(row, value):
        table_ref[row : row + 1, :] = jnp.full((1, LANES), value, jnp.int32)

    nodes = map_ref.shape[0]

    def note(slot, carry):
        inverse_ref[map_ref[slot]] = slot
        return carry

    lax.fori_loop(0, nodes, note, 0)
    low = lax.rem(me, LOW)
    high = lax.div(me, LOW)

    def routes(slot):
        position = map_ref[slot]
        last = jnp.int32(nodes - 1)
        left = inverse_ref[jnp.minimum(2 * position + 1, last)]
        right = inverse_ref[jnp.minimum(2 * position + 2, last)]
        parent = inverse_ref[lax.div(jnp.maximum(position - 1, 0), 2)]
        return position, left, right, parent

    position, left, right, parent = routes(me)
    depth = jnp.int32(0)
    for power in range(1, nodes.bit_length() - 1):
        depth = depth + jnp.where(position + 1 >= 2**power, 1, 0)
    put(DEPTH, jnp.where(position >= nodes - 1, -1, depth))
    put(POSITION, position)
    put(GROUP, lax.axis_index("term"))
    put(APART, inverse_ref[0] ^ inverse_ref[2])
    put(FROM_LEFT, lax.rem(left, LOW) ^ low)
    put(FROM_RIGHT, lax.rem(right, LOW) ^ low)
    put(FROM_PARENT, lax.rem(parent, LOW) ^ low)
    for j in range(LOW):
        position, left, right, parent = routes(high * LOW + (low ^ j))
        put(UP_RELAY + 2 * j, lax.div(left, LOW) ^ high)
        put(UP_RELAY + 2 * j + 1, lax.div(right, LOW) ^ high)
        put(DOWN_RELAY + j, 2 * (lax.div(parent, LOW) ^ high) + lax.rem(position + 1, 2))


def choose(index, choices):
    out = choices[0]().astype(jnp.float32)
    for k in range(1, len(choices)):
        out = jnp.where(index == k, choices[k]().astype(jnp.float32), out)
    return out.astype(jnp.bfloat16)


def either(mask, old, new):
    return choose(jnp.where(mask, 1, 0), [old, new])


def loads(refs, *where):
    return [lambda ref=ref: ref[where] if where else ref[...] for ref in refs]


def start_kernel(
    tensor_hbm, prim_hbm, active_hbm, top_hbm, map_hbm,
    abc_ref, bac_ref, cba_ref, left_ref, right_ref, field_ref, out_ref, table_ref,
    prim_ref, active_ref, top_ref, map_ref, mixed_ref, turn_ref, inverse_ref, sems,
):
    given = (tensor_hbm.at[0], prim_hbm, top_hbm, active_hbm, map_hbm)
    held = (abc_ref, prim_ref, top_ref, active_ref, map_ref)
    copies = [pltpu.make_async_copy(*pair, sems.at[i]) for i, pair in enumerate(zip(given, held))]
    for copy in copies:
        copy.start()
    extent = abc_ref.shape[0]
    per = LANES // extent
    terms = prim_ref.shape[1]
    for copy in copies[:0:-1]:
        copy.wait()
        if copy is copies[-1]:
            fill_table(map_ref, lax.axis_index("node"), inverse_ref, table_ref)
    eye = jnp.where(iota((extent, extent), 0) == iota((extent, extent), 1), 1.0, 0.0)

    def operator(term, side):
        return jnp.where(active_ref[0, side, term] == 1, prim_ref[0, term, side].astype(jnp.float32), eye)

    for first in range(0, terms, per):
        rows = pl.ds(first // per * extent, extent)
        for side, ref in ((0, left_ref), (1, right_ref)):
            side_by_side = [operator(first + lo, side) for lo in range(per)]
            ref[rows, :] = jnp.concatenate(side_by_side, axis=1).astype(jnp.bfloat16)
        fields = [top_ref[first + lo].astype(jnp.float32) for lo in range(per)]
        field_ref[rows, :] = jnp.concatenate(fields, axis=1).astype(jnp.bfloat16)
    diagonals = block_diagonals(split_terms(left_ref[...], extent), extent)
    copies[0].wait()
    swap(abc_ref[...], turn_ref, bac_ref, extent)
    cba_ref[...] = flip(abc_ref[...], extent)
    rows_apply(bac_ref, split_terms(right_ref[...], extent), mixed_ref, extent)
    out_ref[...] = contract(apply_lanes(tall(cba_ref), diagonals, extent), mixed_ref, extent)


def turn_kernel(bac_ref, cba_ref, table_ref, turned_ref, apart_ref, turn_ref):
    extent = bac_ref.shape[0]
    apart_ref[0] = jnp.max(entry(table_ref, APART)) - 1
    swap(cba_ref[...], turn_ref, turned_ref.at[0], extent)
    swap(flip(bac_ref[...], extent), turn_ref, turned_ref.at[1], extent)


def relay_up_kernel(*refs):
    parts, table_ref, outs = refs[:-5], refs[-5], refs[-4:]
    for j, out in enumerate(outs):
        for side in range(2):
            out[side] = choose(entry(table_ref, UP_RELAY + 2 * j + side), loads(parts))


def relay_down_kernel(*refs):
    parts, table_ref, outs = refs[:-5], refs[-5], refs[-4:]
    choices = [f for part in parts for side in range(2) for f in loads([part], side)]
    for j, out in enumerate(outs):
        out[...] = choose(entry(table_ref, DOWN_RELAY + j), choices)


def up_kernel(depth, *refs):
    came, (bac_ref, cba_ref, old_left_ref, old_right_ref, table_ref) = refs[:LOW], refs[LOW : LOW + 5]
    left_ref, right_ref, out_ref, mixed_ref = refs[LOW + 5 :]
    extent = bac_ref.shape[0]
    now = entry(table_ref, DEPTH) == depth
    pairs = old_left_ref.shape[0] // extent
    left = unfold(choose(entry(table_ref, FROM_LEFT), loads(came, 0)), pairs)
    right = unfold(choose(entry(table_ref, FROM_RIGHT), loads(came, 1)), pairs)
    left_ref[...] = either(now, lambda: old_left_ref[...], lambda: left)
    right_ref[...] = either(now, lambda: old_right_ref[...], lambda: right)
    rows_apply(bac_ref, split_terms(right_ref[...], extent), mixed_ref, extent)
    diagonals = block_diagonals(split_terms(left_ref[...], extent), extent)
    out_ref[...] = contract(apply_lanes(tall(cba_ref), diagonals, extent), mixed_ref, extent)


def fetch(came, held, sems):
    copies = [pltpu.make_async_copy(*pair, sems.at[k]) for k, pair in enumerate(zip(came, held))]
    for copy in copies:
        copy.start()
    return copies


def top_kernel(
    came_left_hbm, came_right_hbm, abc_ref, bac_ref, turned_ref, field_ref, old_left_ref, old_right_ref, table_ref,
    sides_ref, out_ref, mixed_ref, came_left_ref, came_right_ref, sems,
):
    copies = fetch((came_left_hbm, came_right_hbm), (came_left_ref, came_right_ref), sems)
    extent = bac_ref.shape[0]
    now = entry(table_ref, DEPTH) == 0
    diagonals = block_diagonals(split_terms(field_ref[...], extent), extent)
    left_lanes = apply_lanes(tall(abc_ref), diagonals, extent)
    for copy in copies:
        copy.wait()
    pairs = old_left_ref.shape[0] // extent
    sides_ref[0] = either(now, lambda: old_left_ref[...], lambda: unfold(came_left_ref[...], pairs))
    sides_ref[1] = either(now, lambda: old_right_ref[...], lambda: unfold(came_right_ref[...], pairs))
    mix(turned_ref, sides_ref, mixed_ref)
    out_ref[0] = contract(left_lanes, mixed_ref.at[0], extent)
    out_ref[1] = contract(apply_lanes(tall(bac_ref), diagonals, extent), mixed_ref.at[1], extent)


def below_top_kernel(
    came_left_ref, came_right_ref, abc_ref, bac_ref, turned_ref, old_ref, sides_ref, table_ref,
    field_ref, out_ref, mixed_ref,
):
    position = entry(table_ref, POSITION)
    came = unfold(either(position == 2, *loads([came_left_ref, came_right_ref])), old_ref.shape[0] // abc_ref.shape[0])
    now = jnp.logical_or(position == 1, position == 2)
    field_ref[...] = either(now, lambda: old_ref[...], lambda: came)
    mix(turned_ref, sides_ref, mixed_ref)
    spread_down(abc_ref, bac_ref, field_ref, out_ref, mixed_ref)


def down_kernel(depth, *refs):
    came, (abc_ref, bac_ref, turned_ref, old_ref, sides_ref, table_ref) = refs[:LOW], refs[LOW : LOW + 6]
    field_ref, out_ref, mixed_ref = refs[LOW + 6 :]
    arrive(depth, old_ref.shape[0] // abc_ref.shape[0], came, old_ref, table_ref, field_ref)
    mix(turned_ref, sides_ref, mixed_ref)
    spread_down(abc_ref, bac_ref, field_ref, out_ref, mixed_ref)


def arrive(depth, pairs, came, old_ref, table_ref, field_ref):
    arrived = choose(entry(table_ref, FROM_PARENT), loads(came))
    arrived = unfold(arrived, pairs)
    field_ref[...] = either(entry(table_ref, DEPTH) == depth, lambda: old_ref[...], lambda: arrived)


def mix(turned_ref, sides_ref, mixed_ref):
    extent = turned_ref.shape[1]
    rows_apply(turned_ref.at[0], split_terms(sides_ref[1], extent), mixed_ref.at[0], extent)
    rows_apply(turned_ref.at[1], split_terms(sides_ref[0], extent), mixed_ref.at[1], extent)


def spread_down(abc_ref, bac_ref, field_ref, out_ref, mixed_ref):
    extent = bac_ref.shape[0]
    diagonals = block_diagonals(split_terms(field_ref[...], extent), extent)
    out_ref[0] = contract(apply_lanes(tall(abc_ref), diagonals, extent), mixed_ref.at[0], extent)
    out_ref[1] = contract(apply_lanes(tall(bac_ref), diagonals, extent), mixed_ref.at[1], extent)


def weigh_kernel(pair, bac_ref, sides_ref, table_ref, out_ref, spread_ref):
    extent = bac_ref.shape[0]
    mine = slice(pair * extent, (pair + 1) * extent)
    rows_out = out_ref.shape[1]
    per = LANES // extent
    half = extent // per
    rows_spread(bac_ref, split_terms(sides_ref[1, mine], extent), spread_ref, extent)
    rows = lax.rem(iota((LANES, extent), 0), extent)
    lanes = iota((LANES, extent), 1)
    wanted = per * lax.rem(lanes, half) + lax.div(lanes, half)
    pick = jnp.where(rows == wanted, 1.0, 0.0).astype(jnp.bfloat16)
    group = lax.div(iota((half, LANES), 1), extent)
    for term, mat in enumerate(split_terms(sides_ref[0, mine], extent)):
        permuted = dot(mat, pick)
        kept = permuted[:rows_out]
        for g in range(1, extent // rows_out):
            kept = jnp.where(entry(table_ref, GROUP)[:, :extent] == g, permuted[g * rows_out : (g + 1) * rows_out], kept)
        kept = kept.astype(jnp.bfloat16)
        tiles = []
        for j in range(extent // per):
            given = [spread_ref[term, (per * j + q) * half : (per * j + q + 1) * half, :] for q in range(per)]
            stacked = []
            for p in range(per):
                row = None
                for q in range(per):
                    shift = (q - p) * extent % LANES
                    moved = pltpu.roll(given[q], shift, 1) if shift else given[q]
                    row = moved if row is None else jnp.where(group == q, moved, row)
                stacked.append(row)
            tiles.append(jnp.concatenate(stacked, axis=0).astype(jnp.bfloat16))
        for j in range(0, len(tiles), WIDE // LANES):
            wide = jnp.concatenate(tiles[j : j + WIDE // LANES], axis=1)
            out_ref[term, :, j * LANES : j * LANES + WIDE] = dot(kept, wide).astype(jnp.bfloat16)


def last_kernel(depth, pairs, *refs):
    came, (old_ref, table_ref, field_ref) = refs[:LOW], refs[LOW:]
    arrive(depth, pairs, came, old_ref, table_ref, field_ref)


def part_kernel(field_ref, *refs):
    out_ref = refs[-1]
    width = refs[0].shape[2]
    out_ref[...] = weighted_sum(refs[:-1], field_ref[...], math.isqrt(width)).astype(jnp.bfloat16)


def finish_kernel(groups, own_ref, *refs):
    table_ref, out_ref = refs[-2:]
    rows, width = out_ref.shape[1:]
    total = own_ref[...].astype(jnp.float32)
    fields, weighed = refs[: groups - 1], refs[groups - 1 : -2]
    for g, field_ref in enumerate(fields):
        pairs = len(weighed) // len(fields)
        part = weighted_sum(weighed[g * pairs : (g + 1) * pairs], field_ref[...], math.isqrt(width))
        total = total + part.astype(jnp.bfloat16).astype(jnp.float32)
    real = jnp.concatenate([entry(table_ref, DEPTH)] * (WIDE // LANES), axis=1) >= 0
    total = jnp.where(real, total, 0.0).astype(jnp.bfloat16)
    for j in range(width // WIDE):
        out_ref[0, :, j * WIDE : (j + 1) * WIDE] = total[j * rows : (j + 1) * rows]


def weighted_sum(weighed_refs, field, extent):
    per, _, width = weighed_refs[0].shape
    quads = WIDE // extent
    copies = pick_rows(LANES, WIDE, extent)
    spread = dot(jnp.concatenate(split_terms(field, extent), axis=0), copies)
    same = lax.div(iota((WIDE, WIDE), 0), extent) == lax.div(iota((WIDE, WIDE), 1), extent)
    total = None
    for term in range(per * len(weighed_refs)):
        weighed_ref = weighed_refs[term // per]
        block = spread[term * extent : (term + 1) * extent]
        diagonal = jnp.where(same, jnp.concatenate([block] * quads, axis=0), 0.0).astype(jnp.bfloat16)
        pieces = [weighed_ref[term % per, :, j : j + WIDE] for j in range(0, width, WIDE)]
        part = dot(jnp.concatenate(pieces, axis=0), diagonal)
        total = part if total is None else total + part
    return total


def pick_rows(rows, lanes, extent):
    same = lax.rem(iota((rows, lanes), 0), extent) == lax.rem(iota((rows, lanes), 1), extent)
    return jnp.where(same, 1.0, 0.0).astype(jnp.bfloat16)


VMEM = pl.BlockSpec(memory_space=pltpu.VMEM)
SMEM = pl.BlockSpec(memory_space=pltpu.SMEM)
HBM = pl.BlockSpec(memory_space=pltpu.HBM)


def call(kernel, out_shape, *operands, scratch=(), smem_out=(), in_hbm=(), kept=True, beside=()):
    shapes = out_shape if isinstance(out_shape, list) else [out_shape]
    specs = [SMEM if i in smem_out else VMEM for i in range(len(shapes))]
    taken = [VMEM] * len(operands)
    operands = list(operands)
    for i, operand in enumerate(operands):
        if i in in_hbm:
            taken[i] = HBM
            operands[i] = pltpu.with_memory_space_constraint(operand, pltpu.HBM)
        elif operand.size >= KEPT:
            operands[i] = pltpu.with_memory_space_constraint(operand, pltpu.VMEM)
    shapes = [pltpu.VMEM(x.shape, x.dtype) if kept and x.size >= KEPT else x for x in shapes]
    given = len(operands)
    operands += [pltpu.with_memory_space_constraint(x, pltpu.VMEM) for x in beside]

    def without(*refs):
        kernel(*refs[:given], *refs[len(operands) :])

    return pl.pallas_call(
        without,
        out_shape=shapes if isinstance(out_shape, list) else shapes[0],
        in_specs=taken + [VMEM] * len(beside),
        out_specs=specs if isinstance(out_shape, list) else specs[0],
        scratch_shapes=list(scratch),
        compiler_params=pltpu.CompilerParams(vmem_limit_bytes=16 * 2**20),
    )(*operands)


def exchange(value, mask, nodes):
    return lax.ppermute(value, "node", [(i, i ^ mask) for i in range(nodes)])


def high_exchange(value, nodes):
    return [value] + [exchange(value, high * LOW, nodes) for high in range(1, nodes // LOW)]


def low_exchange(values, nodes):
    return [values[0]] + [exchange(values[j], j, nodes) for j in range(1, LOW)]


def per_device(node_tensors, prim_ops, active, top_field, node_map):
    nodes = lax.axis_size("node")
    groups = lax.axis_size("term")
    depths = nodes.bit_length() - 1
    turned_active = jnp.swapaxes(active, 1, 2)

    extent = node_tensors.shape[1]
    terms = prim_ops.shape[1]
    pairs = terms * extent // LANES
    flat = jax.ShapeDtypeStruct((extent, extent * extent), jnp.bfloat16)
    mats = jax.ShapeDtypeStruct((pairs * extent, LANES), jnp.bfloat16)
    two = jax.ShapeDtypeStruct((2,) + mats.shape, jnp.bfloat16)
    message = jax.ShapeDtypeStruct((-(-pairs // 2) * (extent + PAD), LANES), jnp.bfloat16)
    messages = jax.ShapeDtypeStruct((2,) + message.shape, jnp.bfloat16)
    table_shape = jax.ShapeDtypeStruct((TABLE, LANES), jnp.int32)
    spread = jax.ShapeDtypeStruct((terms, extent * extent * extent // LANES, LANES), jnp.bfloat16)
    part = jax.ShapeDtypeStruct((LANES // extent, extent // groups, extent * extent), jnp.bfloat16)
    space = pltpu.VMEM((LANES // extent,) + spread.shape[1:], jnp.float32)
    both = [pltpu.VMEM((2,) + spread.shape, jnp.bfloat16)]
    mixed_space = pltpu.VMEM(spread.shape, jnp.bfloat16)
    turn_space = pltpu.VMEM(spread.shape[1:], jnp.float32)

    def others(value):
        return [
            lax.ppermute(value, "term", [(i, (i + shift) % groups) for i in range(groups)]) for shift in range(1, groups)
        ]

    def weigh_beside(count, values):
        for sides, pair in to_weigh[len(weighed) : len(weighed) + count]:
            weighed.append(call(functools.partial(weigh_kernel, pair), part, bac, sides, table, scratch=[space]))
        return lax.optimization_barrier((values, weighed[-count:]))

    def with_top(first, second):
        def branch(mask):
            return lambda first, second: (exchange(first, nodes // 2, nodes), exchange(second, mask, nodes))

        return lax.switch(apart[0], [branch(mask) for mask in range(1, nodes)], first, second)

    abc, bac, cba, left, right, field, mine, table = call(
        start_kernel,
        [flat, flat, flat, mats, mats, mats, message, table_shape],
        node_tensors,
        prim_ops,
        turned_active,
        top_field,
        node_map,
        scratch=[
            pltpu.VMEM(prim_ops.shape, jnp.bfloat16),
            pltpu.SMEM(turned_active.shape, jnp.int32),
            pltpu.VMEM(top_field.shape, jnp.bfloat16),
            pltpu.SMEM(node_map.shape, jnp.int32),
            mixed_space,
            turn_space,
            pltpu.SMEM((nodes,), jnp.int32),
            pltpu.SemaphoreType.DMA((5,)),
        ],
        in_hbm=(0, 1, 2, 3, 4),
    )
    for depth in range(depths - 2, 0, -1):
        parts = high_exchange(mine, nodes)
        came = low_exchange(call(relay_up_kernel, [messages] * LOW, *parts, table), nodes)
        if depth == depths - 2:
            turned, apart = call(
                turn_kernel,
                [jax.ShapeDtypeStruct((2,) + flat.shape, flat.dtype), jax.ShapeDtypeStruct((1,), jnp.int32)],
                bac,
                cba,
                table,
                scratch=[turn_space],
                smem_out=(1,),
            )
            came, turned, apart = lax.optimization_barrier((came, turned, apart))
        left, right, mine = call(
            functools.partial(up_kernel, depth),
            [mats, mats, message],
            *came,
            bac,
            cba,
            left,
            right,
            table,
            scratch=[mixed_space],
        )

    came_left, came_right = with_top(mine, mine)
    landing = both + [pltpu.VMEM(message.shape, jnp.bfloat16)] * 2 + [pltpu.SemaphoreType.DMA((2,))]
    sides, fields = call(
        top_kernel,
        [two, messages],
        came_left,
        came_right,
        abc,
        bac,
        turned,
        field,
        left,
        right,
        table,
        scratch=landing,
        in_hbm=(0, 1),
    )
    came_left, came_right = with_top(fields[0], fields[1])
    to_weigh = [(each, pair) for each in [sides] + others(sides) for pair in range(pairs)]
    share = -(-len(to_weigh) // (2 * (depths - 2)))
    field, fields = call(
        below_top_kernel,
        [mats, messages],
        came_left,
        came_right,
        abc,
        bac,
        turned,
        field,
        sides,
        table,
        scratch=both,
    )
    weighed = []
    for depth in range(2, depths):
        parts = high_exchange(fields, nodes)
        parts, weighed[-share:] = weigh_beside(share, parts)
        came = low_exchange(call(relay_down_kernel, [message] * LOW, *parts, table), nodes)
        came, weighed[-share:] = weigh_beside(share, came)
        if depth < depths - 1:
            field, fields = call(
                functools.partial(down_kernel, depth),
                [mats, messages],
                *came,
                abc,
                bac,
                turned,
                field,
                sides,
                table,
                scratch=both,
            )
    field = call(functools.partial(last_kernel, depths - 1, pairs), mats, *came, field, table)
    out = jax.ShapeDtypeStruct((1, extent // groups, extent * extent), jnp.bfloat16)
    tall_part = jax.ShapeDtypeStruct((extent * extent * extent // groups // WIDE, WIDE), jnp.bfloat16)
    fields = others(field)
    own = call(part_kernel, tall_part, field, *weighed[:pairs], kept=False)
    own, fields = lax.optimization_barrier((own, fields))
    rest = weighed[pairs:]
    return call(functools.partial(finish_kernel, groups), out, own, *fields, *rest, table, kept=False)


def solution(mesh):
    placed = (
        P("node", None, None),
        P("node", "term", None, None, None),
        P("node", "term", None),
        P("term", None, None),
        P(),
    )
    return jax.shard_map(
        per_device, mesh=mesh, in_specs=placed, out_specs=P("node", "term", None), check_vma=False
    )
```

```python
import functools
import math

import jax
import jax.numpy as jnp
from jax import lax
from jax.experimental import pallas as pl
from jax.experimental.pallas import tpu as pltpu
from jax.sharding import PartitionSpec as P

LANES = 128
WIDE = 256
BATCH = 2
PAD = 16
KEPT = 2**18


def dot(left, right):
    return jnp.dot(left, right, preferred_element_type=jnp.float32)


def iota(shape, dim):
    return lax.broadcasted_iota(jnp.int32, shape, dim)


def split_terms(packed, extent):
    per = LANES // extent
    wide = packed.astype(jnp.float32)
    out = []
    for term in range(per * packed.shape[0] // extent):
        block = wide[(term // per) * extent : (term // per + 1) * extent]
        mine = lax.div(iota(block.shape, 1), extent) == term % per
        out.append(jnp.where(mine, block, 0.0).astype(jnp.bfloat16))
    return out


def rows_spread(tensor_ref, mats, spread_ref, extent):
    per = LANES // extent
    half = extent // per
    stack = jnp.concatenate(mats, axis=0)
    for chunk in range(extent * extent // WIDE):
        piece = tensor_ref[:, chunk * WIDE : (chunk + 1) * WIDE]
        result = dot(stack, jnp.concatenate([piece] * per, axis=0))
        for part in range(WIDE // LANES):
            i = chunk * (WIDE // LANES) + part
            for term in range(len(mats)):
                spread_ref[term, pl.ds(i, extent, stride=half), :] = result[
                    term * extent : (term + 1) * extent, part * LANES : (part + 1) * LANES
                ]


SUB = 8


def rows_apply(tensor_ref, mats, mixed_ref, extent):
    per = LANES // extent
    quads = WIDE // extent
    halves = SUB // quads
    count = 2 * halves
    stack = jnp.concatenate(mats, axis=0)
    row = iota((extent // SUB, SUB, LANES), 1)
    for first in range(0, extent // per, count):
        piece = tensor_ref[:, first * LANES : (first + count) * LANES]
        result = dot(stack, jnp.concatenate([piece] * per, axis=0))
        for term in range(len(mats)):
            tiles = [
                result[term * extent : (term + 1) * extent, k * LANES : (k + 1) * LANES].reshape(row.shape)
                for k in range(count)
            ]
            for half in range(halves):
                wanted = []
                for start in range(0, count, halves):
                    block = None
                    for k in range(halves):
                        shift = (k - half) * quads % SUB
                        moved = pltpu.roll(tiles[start + k], shift, 1) if shift else tiles[start + k]
                        block = moved if block is None else jnp.where(lax.div(row, quads) == k, moved, block)
                    wanted.append(block)
                packed = jnp.concatenate(wanted, axis=1).astype(jnp.bfloat16)
                for m in range(extent // SUB):
                    base = (m * halves + half) * (extent // per) * quads + first * quads
                    mixed_ref[term, base : base + count * quads, :] = packed[m]


def block_diagonals(mats, extent):
    per = LANES // extent
    quads = WIDE // extent
    rows = lax.rem(iota((LANES, WIDE), 0), extent)
    lanes = iota((LANES, WIDE), 1)
    wanted = per * lax.div(lax.rem(lanes, WIDE // per), quads) + lax.div(lanes, WIDE // per)
    pick = jnp.where(rows == wanted, 1.0, 0.0).astype(jnp.bfloat16)
    spread = dot(jnp.concatenate(mats, axis=0), pick)
    lanes = iota((WIDE, WIDE), 1)
    same = lax.div(iota((WIDE, WIDE), 0), extent) == lax.rem(lanes, quads)
    out = []
    for term in range(len(mats)):
        block = spread[term * extent : (term + 1) * extent]
        out.append(jnp.where(same, jnp.concatenate([block] * quads, axis=0), 0.0).astype(jnp.bfloat16))
    return out


def tall(tensor_ref):
    width = tensor_ref.shape[1]
    return jnp.concatenate([tensor_ref[:, j : j + WIDE] for j in range(0, width, WIDE)], axis=0)


def pair_up(accs, extent):
    per = LANES // extent
    out = []
    for first in range(0, len(accs), per):
        blocks = None
        for lo in range(per):
            acc = accs[first + lo]
            group = lax.div(iota((extent, LANES), 1), extent)
            kept = jnp.zeros((extent, LANES), jnp.float32)
            for p in range(per):
                kept = jnp.where(group == p, acc[p * extent : (p + 1) * extent], kept)
            total = kept
            for p in range(1, per):
                total = total + pltpu.roll(kept, p * extent, 1)
            blocks = total if blocks is None else jnp.where(group == lo, total, blocks)
        out.append(blocks)
    return out


def below_diagonal(shape, extent):
    rows, lanes = iota(shape, 0), lax.rem(iota(shape, 1), extent)
    return rows > lanes, rows == lanes


def fold(blocks):
    extent = blocks[0].shape[0]
    below, on = below_diagonal(blocks[0].shape, extent)
    out = []
    for first in range(0, len(blocks), 2):
        lower, upper = blocks[first], blocks[min(first + 1, len(blocks) - 1)]
        out.append(jnp.where(jnp.logical_or(below, on), lower, upper))
        row = jnp.sum(jnp.where(on, upper, 0.0), axis=0, keepdims=True)
        out.append(jnp.broadcast_to(row, (PAD, LANES)))
    return jnp.concatenate(out, axis=0).astype(jnp.bfloat16)


def unfold(message, pairs):
    height = message.shape[0] // (-(-pairs // 2))
    extent = height - PAD
    wide = message.astype(jnp.float32)
    out = []
    for base in range(0, message.shape[0], height):
        body, row = wide[base : base + extent], wide[base + extent : base + extent + 1]
        below, on = below_diagonal(body.shape, extent)
        turned = body.T
        parts = [turned[k : k + extent] for k in range(0, LANES, extent)]
        turned = jnp.concatenate(parts, axis=1)
        out.append(jnp.where(jnp.logical_or(below, on), body, turned))
        out.append(jnp.where(below, turned, jnp.where(on, row, body)))
    return jnp.concatenate(out[:pairs], axis=0).astype(jnp.bfloat16)


def apply_lanes(stacked, diagonals, extent):
    per = LANES // extent
    groups = stacked.shape[0] // extent
    lefts = []
    for diagonal in diagonals:
        moved = dot(stacked, diagonal).astype(jnp.bfloat16)
        for p in range(per):
            lanes = slice(p * (WIDE // per), (p + 1) * (WIDE // per))
            lefts.append(jnp.concatenate([moved[j * extent : (j + 1) * extent, lanes] for j in range(groups)], axis=1))
    return lefts


def contract(lefts, mixed, extent):
    per = LANES // extent
    accs = []
    for first in range(0, len(lefts) // per, BATCH):
        left = jnp.concatenate(lefts[first * per : (first + BATCH) * per], axis=0)
        right = jnp.concatenate([mixed[term] for term in range(first, first + BATCH)], axis=1)
        result = dot(left, right)
        for k in range(BATCH):
            accs.append(result[k * LANES : (k + 1) * LANES, k * LANES : (k + 1) * LANES])
    return fold(pair_up(accs, extent))


def swap(value, turn_ref, out_ref, extent):
    per = LANES // extent
    half = extent // per
    rows = iota((extent, extent), 0)
    wanted = per * lax.rem(rows, half) + lax.div(rows, half)
    order = jnp.where(iota((extent, extent), 1) == wanted, 1.0, 0.0).astype(jnp.bfloat16)
    sorted_rows = dot(order, value)
    group = lax.div(iota((half, LANES), 1), extent)
    for j in range(extent // per):
        given = [sorted_rows[p * half : (p + 1) * half, j * LANES : (j + 1) * LANES] for p in range(per)]
        for q in range(per):
            row = None
            for p in range(per):
                shift = (p - q) * extent % LANES
                moved = pltpu.roll(given[p], shift, 1) if shift else given[p]
                row = moved if row is None else jnp.where(group == p, moved, row)
            turn_ref[pl.ds(per * j + q, half, stride=extent), :] = row
    for i in range(half):
        out_ref[:, i * LANES : (i + 1) * LANES] = turn_ref[i * extent : (i + 1) * extent, :].astype(jnp.bfloat16)


def flip(value, extent):
    per = LANES // extent
    wide = value.astype(jnp.float32)
    tiles = []
    for j in range(extent // per):
        turned = wide[:, j * LANES : (j + 1) * LANES].T
        tiles.append(jnp.concatenate([turned[p * extent : (p + 1) * extent] for p in range(per)], axis=1))
    return jnp.concatenate(tiles, axis=1).astype(jnp.bfloat16)


DEPTH, FROM_LEFT, FROM_RIGHT, FROM_PARENT, POSITION, GROUP, APART, UP_RELAY, DOWN_RELAY, TABLE = *range(7), 8, 16, 24
LOW = 4


def entry(table_ref, row):
    return table_ref[row : row + 1, :]


def fill_table(map_ref, me, inverse_ref, table_ref):
    def put(row, value):
        table_ref[row : row + 1, :] = jnp.full((1, LANES), value, jnp.int32)

    nodes = map_ref.shape[0]

    def note(slot, carry):
        inverse_ref[map_ref[slot]] = slot
        return carry

    lax.fori_loop(0, nodes, note, 0)
    low = lax.rem(me, LOW)
    high = lax.div(me, LOW)

    def routes(slot):
        position = map_ref[slot]
        last = jnp.int32(nodes - 1)
        left = inverse_ref[jnp.minimum(2 * position + 1, last)]
        right = inverse_ref[jnp.minimum(2 * position + 2, last)]
        parent = inverse_ref[lax.div(jnp.maximum(position - 1, 0), 2)]
        return position, left, right, parent

    position, left, right, parent = routes(me)
    depth = jnp.int32(0)
    for power in range(1, nodes.bit_length() - 1):
        depth = depth + jnp.where(position + 1 >= 2**power, 1, 0)
    put(DEPTH, jnp.where(position >= nodes - 1, -1, depth))
    put(POSITION, position)
    put(GROUP, lax.axis_index("term"))
    put(APART, inverse_ref[0] ^ inverse_ref[2])
    put(FROM_LEFT, lax.rem(left, LOW) ^ low)
    put(FROM_RIGHT, lax.rem(right, LOW) ^ low)
    put(FROM_PARENT, lax.rem(parent, LOW) ^ low)
    for j in range(LOW):
        position, left, right, parent = routes(high * LOW + (low ^ j))
        put(UP_RELAY + 2 * j, lax.div(left, LOW) ^ high)
        put(UP_RELAY + 2 * j + 1, lax.div(right, LOW) ^ high)
        put(DOWN_RELAY + j, 2 * (lax.div(parent, LOW) ^ high) + lax.rem(position + 1, 2))


def choose(index, choices):
    out = choices[0]().astype(jnp.float32)
    for k in range(1, len(choices)):
        out = jnp.where(index == k, choices[k]().astype(jnp.float32), out)
    return out.astype(jnp.bfloat16)


def either(mask, old, new):
    return choose(jnp.where(mask, 1, 0), [old, new])


def loads(refs, *where):
    return [lambda ref=ref: ref[where] if where else ref[...] for ref in refs]


def start_kernel(
    tensor_hbm, prim_hbm, active_hbm, top_hbm, map_hbm,
    abc_ref, bac_ref, cba_ref, left_ref, right_ref, field_ref, out_ref, table_ref,
    prim_ref, active_ref, top_ref, map_ref, mixed_ref, turn_ref, inverse_ref, sems,
):
    given = (tensor_hbm.at[0], prim_hbm, top_hbm, active_hbm, map_hbm)
    held = (abc_ref, prim_ref, top_ref, active_ref, map_ref)
    copies = [pltpu.make_async_copy(*pair, sems.at[i]) for i, pair in enumerate(zip(given, held))]
    for copy in copies:
        copy.start()
    extent = abc_ref.shape[0]
    per = LANES // extent
    terms = prim_ref.shape[1]
    for copy in copies[:0:-1]:
        copy.wait()
        if copy is copies[-1]:
            fill_table(map_ref, lax.axis_index("node"), inverse_ref, table_ref)
    eye = jnp.where(iota((extent, extent), 0) == iota((extent, extent), 1), 1.0, 0.0)

    def operator(term, side):
        return jnp.where(active_ref[0, side, term] == 1, prim_ref[0, term, side].astype(jnp.float32), eye)

    for first in range(0, terms, per):
        rows = pl.ds(first // per * extent, extent)
        for side, ref in ((0, left_ref), (1, right_ref)):
            side_by_side = [operator(first + lo, side) for lo in range(per)]
            ref[rows, :] = jnp.concatenate(side_by_side, axis=1).astype(jnp.bfloat16)
        fields = [top_ref[first + lo].astype(jnp.float32) for lo in range(per)]
        field_ref[rows, :] = jnp.concatenate(fields, axis=1).astype(jnp.bfloat16)
    diagonals = block_diagonals(split_terms(left_ref[...], extent), extent)
    copies[0].wait()
    swap(abc_ref[...], turn_ref, bac_ref, extent)
    cba_ref[...] = flip(abc_ref[...], extent)
    rows_apply(bac_ref, split_terms(right_ref[...], extent), mixed_ref, extent)
    out_ref[...] = contract(apply_lanes(tall(cba_ref), diagonals, extent), mixed_ref, extent)


def turn_kernel(bac_ref, cba_ref, table_ref, turned_ref, apart_ref, turn_ref):
    extent = bac_ref.shape[0]
    apart_ref[0] = jnp.max(entry(table_ref, APART)) - 1
    swap(cba_ref[...], turn_ref, turned_ref.at[0], extent)
    swap(flip(bac_ref[...], extent), turn_ref, turned_ref.at[1], extent)


def both_kernel(first_ref, second_ref, out_ref):
    out_ref[0] = first_ref[...]
    out_ref[1] = second_ref[...]


def relay_up_kernel(*refs):
    parts, table_ref, outs = refs[:-5], refs[-5], refs[-4:]
    for j, out in enumerate(outs):
        for side in range(2):
            out[side] = choose(entry(table_ref, UP_RELAY + 2 * j + side), loads(parts))


def relay_down_kernel(*refs):
    parts, table_ref, outs = refs[:-5], refs[-5], refs[-4:]
    choices = [f for part in parts for side in range(2) for f in loads([part], side)]
    for j, out in enumerate(outs):
        out[...] = choose(entry(table_ref, DOWN_RELAY + j), choices)


def up_kernel(depth, *refs):
    came, (bac_ref, cba_ref, old_left_ref, old_right_ref, table_ref) = refs[:LOW], refs[LOW : LOW + 5]
    left_ref, right_ref, out_ref, mixed_ref = refs[LOW + 5 :]
    extent = bac_ref.shape[0]
    now = entry(table_ref, DEPTH) == depth
    pairs = old_left_ref.shape[0] // extent
    left = unfold(choose(entry(table_ref, FROM_LEFT), loads(came, 0)), pairs)
    right = unfold(choose(entry(table_ref, FROM_RIGHT), loads(came, 1)), pairs)
    left_ref[...] = either(now, lambda: old_left_ref[...], lambda: left)
    right_ref[...] = either(now, lambda: old_right_ref[...], lambda: right)
    rows_apply(bac_ref, split_terms(right_ref[...], extent), mixed_ref, extent)
    diagonals = block_diagonals(split_terms(left_ref[...], extent), extent)
    out_ref[...] = contract(apply_lanes(tall(cba_ref), diagonals, extent), mixed_ref, extent)


def top_kernel(
    came_ref, abc_ref, bac_ref, turned_ref, field_ref, old_left_ref, old_right_ref, table_ref,
    sides_ref, out_ref, mixed_ref,
):
    extent = bac_ref.shape[0]
    now = entry(table_ref, DEPTH) == 0
    diagonals = block_diagonals(split_terms(field_ref[...], extent), extent)
    left_lanes = apply_lanes(tall(abc_ref), diagonals, extent)
    pairs = old_left_ref.shape[0] // extent
    sides_ref[0] = either(now, lambda: old_left_ref[...], lambda: unfold(came_ref[0], pairs))
    sides_ref[1] = either(now, lambda: old_right_ref[...], lambda: unfold(came_ref[1], pairs))
    mix(turned_ref, sides_ref, mixed_ref)
    out_ref[0] = contract(left_lanes, mixed_ref.at[0], extent)
    out_ref[1] = contract(apply_lanes(tall(bac_ref), diagonals, extent), mixed_ref.at[1], extent)


def below_top_kernel(
    came_ref, abc_ref, bac_ref, turned_ref, old_ref, sides_ref, table_ref,
    field_ref, out_ref, mixed_ref,
):
    position = entry(table_ref, POSITION)
    came = unfold(either(position == 2, *[f for side in range(2) for f in loads([came_ref], side)]), old_ref.shape[0] // abc_ref.shape[0])
    now = jnp.logical_or(position == 1, position == 2)
    field_ref[...] = either(now, lambda: old_ref[...], lambda: came)
    mix(turned_ref, sides_ref, mixed_ref)
    spread_down(abc_ref, bac_ref, field_ref, out_ref, mixed_ref)


def down_kernel(depth, *refs):
    came, (abc_ref, bac_ref, old_ref, mixed_ref, table_ref) = refs[:LOW], refs[LOW : LOW + 5]
    field_ref, out_ref = refs[LOW + 5 :]
    arrive(depth, old_ref.shape[0] // abc_ref.shape[0], came, old_ref, table_ref, field_ref)
    spread_down(abc_ref, bac_ref, field_ref, out_ref, mixed_ref)


def arrive(depth, pairs, came, old_ref, table_ref, field_ref):
    arrived = choose(entry(table_ref, FROM_PARENT), loads(came))
    arrived = unfold(arrived, pairs)
    field_ref[...] = either(entry(table_ref, DEPTH) == depth, lambda: old_ref[...], lambda: arrived)


def mix(turned_ref, sides_ref, mixed_ref):
    extent = turned_ref.shape[1]
    rows_apply(turned_ref.at[0], split_terms(sides_ref[1], extent), mixed_ref.at[0], extent)
    rows_apply(turned_ref.at[1], split_terms(sides_ref[0], extent), mixed_ref.at[1], extent)


def spread_down(abc_ref, bac_ref, field_ref, out_ref, mixed_ref):
    extent = bac_ref.shape[0]
    diagonals = block_diagonals(split_terms(field_ref[...], extent), extent)
    out_ref[0] = contract(apply_lanes(tall(abc_ref), diagonals, extent), mixed_ref.at[0], extent)
    out_ref[1] = contract(apply_lanes(tall(bac_ref), diagonals, extent), mixed_ref.at[1], extent)


def weigh_kernel(pair, bac_ref, sides_ref, table_ref, out_ref, spread_ref):
    extent = bac_ref.shape[0]
    mine = slice(pair * extent, (pair + 1) * extent)
    rows_out = out_ref.shape[1]
    per = LANES // extent
    half = extent // per
    rows_spread(bac_ref, split_terms(sides_ref[1, mine], extent), spread_ref, extent)
    rows = lax.rem(iota((LANES, extent), 0), extent)
    lanes = iota((LANES, extent), 1)
    wanted = per * lax.rem(lanes, half) + lax.div(lanes, half)
    pick = jnp.where(rows == wanted, 1.0, 0.0).astype(jnp.bfloat16)
    group = lax.div(iota((half, LANES), 1), extent)
    for term, mat in enumerate(split_terms(sides_ref[0, mine], extent)):
        permuted = dot(mat, pick)
        kept = permuted[:rows_out]
        for g in range(1, extent // rows_out):
            kept = jnp.where(entry(table_ref, GROUP)[:, :extent] == g, permuted[g * rows_out : (g + 1) * rows_out], kept)
        kept = kept.astype(jnp.bfloat16)
        tiles = []
        for j in range(extent // per):
            given = [spread_ref[term, (per * j + q) * half : (per * j + q + 1) * half, :] for q in range(per)]
            stacked = []
            for p in range(per):
                row = None
                for q in range(per):
                    shift = (q - p) * extent % LANES
                    moved = pltpu.roll(given[q], shift, 1) if shift else given[q]
                    row = moved if row is None else jnp.where(group == q, moved, row)
                stacked.append(row)
            tiles.append(jnp.concatenate(stacked, axis=0).astype(jnp.bfloat16))
        for j in range(0, len(tiles), WIDE // LANES):
            wide = jnp.concatenate(tiles[j : j + WIDE // LANES], axis=1)
            out_ref[term, :, j * LANES : j * LANES + WIDE] = dot(kept, wide).astype(jnp.bfloat16)


def last_kernel(depth, pairs, *refs):
    came, (old_ref, table_ref, field_ref) = refs[:LOW], refs[LOW:]
    arrive(depth, pairs, came, old_ref, table_ref, field_ref)


def part_kernel(field_ref, *refs):
    out_ref = refs[-1]
    width = refs[0].shape[2]
    out_ref[...] = weighted_sum(refs[:-1], field_ref[...], math.isqrt(width)).astype(jnp.bfloat16)


def finish_kernel(groups, own_ref, *refs):
    table_ref, out_ref = refs[-2:]
    rows, width = out_ref.shape[1:]
    total = own_ref[...].astype(jnp.float32)
    fields, weighed = refs[: groups - 1], refs[groups - 1 : -2]
    for g, field_ref in enumerate(fields):
        pairs = len(weighed) // len(fields)
        part = weighted_sum(weighed[g * pairs : (g + 1) * pairs], field_ref[...], math.isqrt(width))
        total = total + part.astype(jnp.bfloat16).astype(jnp.float32)
    real = jnp.concatenate([entry(table_ref, DEPTH)] * (WIDE // LANES), axis=1) >= 0
    total = jnp.where(real, total, 0.0).astype(jnp.bfloat16)
    for j in range(width // WIDE):
        out_ref[0, :, j * WIDE : (j + 1) * WIDE] = total[j * rows : (j + 1) * rows]


def weighted_sum(weighed_refs, field, extent):
    per, _, width = weighed_refs[0].shape
    quads = WIDE // extent
    copies = pick_rows(LANES, WIDE, extent)
    spread = dot(jnp.concatenate(split_terms(field, extent), axis=0), copies)
    same = lax.div(iota((WIDE, WIDE), 0), extent) == lax.div(iota((WIDE, WIDE), 1), extent)
    total = None
    for term in range(per * len(weighed_refs)):
        weighed_ref = weighed_refs[term // per]
        block = spread[term * extent : (term + 1) * extent]
        diagonal = jnp.where(same, jnp.concatenate([block] * quads, axis=0), 0.0).astype(jnp.bfloat16)
        pieces = [weighed_ref[term % per, :, j : j + WIDE] for j in range(0, width, WIDE)]
        part = dot(jnp.concatenate(pieces, axis=0), diagonal)
        total = part if total is None else total + part
    return total


def pick_rows(rows, lanes, extent):
    same = lax.rem(iota((rows, lanes), 0), extent) == lax.rem(iota((rows, lanes), 1), extent)
    return jnp.where(same, 1.0, 0.0).astype(jnp.bfloat16)


VMEM = pl.BlockSpec(memory_space=pltpu.VMEM)
SMEM = pl.BlockSpec(memory_space=pltpu.SMEM)
HBM = pl.BlockSpec(memory_space=pltpu.HBM)


def call(kernel, out_shape, *operands, scratch=(), smem_out=(), in_hbm=(), kept=True, in_vmem=False, beside=()):
    shapes = out_shape if isinstance(out_shape, list) else [out_shape]
    specs = [SMEM if i in smem_out else VMEM for i in range(len(shapes))]
    taken = [VMEM] * len(operands)
    operands = list(operands)
    for i, operand in enumerate(operands):
        if i in in_hbm:
            taken[i] = HBM
            operands[i] = pltpu.with_memory_space_constraint(operand, pltpu.HBM)
        elif operand.size >= KEPT:
            operands[i] = pltpu.with_memory_space_constraint(operand, pltpu.VMEM)
    shapes = [pltpu.VMEM(x.shape, x.dtype) if in_vmem or (kept and x.size >= KEPT) else x for x in shapes]
    given = len(operands)
    operands += [pltpu.with_memory_space_constraint(x, pltpu.VMEM) for x in beside]

    def without(*refs):
        kernel(*refs[:given], *refs[len(operands) :])

    return pl.pallas_call(
        without,
        out_shape=shapes if isinstance(out_shape, list) else shapes[0],
        in_specs=taken + [VMEM] * len(beside),
        out_specs=specs if isinstance(out_shape, list) else specs[0],
        scratch_shapes=list(scratch),
        compiler_params=pltpu.CompilerParams(vmem_limit_bytes=16 * 2**20),
    )(*operands)


def exchange(value, mask, nodes):
    return lax.ppermute(value, "node", [(i, i ^ mask) for i in range(nodes)])


def high_exchange(value, nodes):
    return [value] + [exchange(value, high * LOW, nodes) for high in range(1, nodes // LOW)]


def low_exchange(values, nodes):
    return [values[0]] + [exchange(values[j], j, nodes) for j in range(1, LOW)]


def per_device(node_tensors, prim_ops, active, top_field, node_map):
    nodes = lax.axis_size("node")
    groups = lax.axis_size("term")
    depths = nodes.bit_length() - 1
    turned_active = jnp.swapaxes(active, 1, 2)

    extent = node_tensors.shape[1]
    terms = prim_ops.shape[1]
    pairs = terms * extent // LANES
    flat = jax.ShapeDtypeStruct((extent, extent * extent), jnp.bfloat16)
    mats = jax.ShapeDtypeStruct((pairs * extent, LANES), jnp.bfloat16)
    two = jax.ShapeDtypeStruct((2,) + mats.shape, jnp.bfloat16)
    message = jax.ShapeDtypeStruct((-(-pairs // 2) * (extent + PAD), LANES), jnp.bfloat16)
    messages = jax.ShapeDtypeStruct((2,) + message.shape, jnp.bfloat16)
    table_shape = jax.ShapeDtypeStruct((TABLE, LANES), jnp.int32)
    spread = jax.ShapeDtypeStruct((terms, extent * extent * extent // LANES, LANES), jnp.bfloat16)
    part = jax.ShapeDtypeStruct((LANES // extent, extent // groups, extent * extent), jnp.bfloat16)
    space = pltpu.VMEM((LANES // extent,) + spread.shape[1:], jnp.float32)
    both = [pltpu.VMEM((2,) + spread.shape, jnp.bfloat16)]
    mixed_space = pltpu.VMEM(spread.shape, jnp.bfloat16)
    turn_space = pltpu.VMEM(spread.shape[1:], jnp.float32)

    def others(value):
        return [
            lax.ppermute(value, "term", [(i, (i + shift) % groups) for i in range(groups)]) for shift in range(1, groups)
        ]

    def weigh_beside(count, values):
        first = len(weighed)
        for sides, pair in to_weigh[first : first + count]:
            weighed.append(call(functools.partial(weigh_kernel, pair), part, bac, sides, table, scratch=[space]))
        values, weighed[first:] = lax.optimization_barrier((values, weighed[first:]))
        return values

    def with_top(first, second):
        def branch(mask):
            def go(first, second):
                came = exchange(first, nodes // 2, nodes), exchange(second, mask, nodes)
                return call(both_kernel, messages, *came, in_vmem=True)

            return go

        return lax.switch(apart[0], [branch(mask) for mask in range(1, nodes)], first, second)

    abc, bac, cba, left, right, field, mine, table = call(
        start_kernel,
        [flat, flat, flat, mats, mats, mats, message, table_shape],
        node_tensors,
        prim_ops,
        turned_active,
        top_field,
        node_map,
        scratch=[
            pltpu.VMEM(prim_ops.shape, jnp.bfloat16),
            pltpu.SMEM(turned_active.shape, jnp.int32),
            pltpu.VMEM(top_field.shape, jnp.bfloat16),
            pltpu.SMEM(node_map.shape, jnp.int32),
            mixed_space,
            turn_space,
            pltpu.SMEM((nodes,), jnp.int32),
            pltpu.SemaphoreType.DMA((5,)),
        ],
        in_hbm=(0, 1, 2, 3, 4),
    )
    for depth in range(depths - 2, 0, -1):
        parts = high_exchange(mine, nodes)
        came = low_exchange(call(relay_up_kernel, [messages] * LOW, *parts, table), nodes)
        if depth == depths - 2:
            turned, apart = call(
                turn_kernel,
                [jax.ShapeDtypeStruct((2,) + flat.shape, flat.dtype), jax.ShapeDtypeStruct((1,), jnp.int32)],
                bac,
                cba,
                table,
                scratch=[turn_space],
                smem_out=(1,),
            )
            came, turned, apart = lax.optimization_barrier((came, turned, apart))
        left, right, mine = call(
            functools.partial(up_kernel, depth),
            [mats, mats, message],
            *came,
            bac,
            cba,
            left,
            right,
            table,
            scratch=[mixed_space],
        )

    came = pltpu.with_memory_space_constraint(with_top(mine, mine), pltpu.VMEM)
    sides, fields = call(
        top_kernel,
        [two, messages],
        came,
        abc,
        bac,
        turned,
        field,
        left,
        right,
        table,
        scratch=both,
    )
    came = pltpu.with_memory_space_constraint(with_top(fields[0], fields[1]), pltpu.VMEM)
    to_weigh = [(each, pair) for each in [sides] + others(sides) for pair in range(pairs)]
    share = -(-len(to_weigh) // (1 + 3 * (depths - 3)))
    field, fields = call(
        below_top_kernel,
        [mats, messages],
        came,
        abc,
        bac,
        turned,
        field,
        sides,
        table,
        scratch=both,
    )
    weighed = []
    for depth in range(2, depths):
        parts = high_exchange(fields, nodes)
        if depth == 2:
            ahead = jax.ShapeDtypeStruct((2,) + spread.shape, spread.dtype)
            parts, mixed = lax.optimization_barrier((parts, call(mix, ahead, turned, sides)))
        else:
            parts = weigh_beside(2 * share, parts)
        came = low_exchange(call(relay_down_kernel, [message] * LOW, *parts, table), nodes)
        came = weigh_beside(share, came)
        if depth < depths - 1:
            field, fields = call(
                functools.partial(down_kernel, depth),
                [mats, messages],
                *came,
                abc,
                bac,
                field,
                mixed,
                table,
            )
    field = call(functools.partial(last_kernel, depths - 1, pairs), mats, *came, field, table)
    out = jax.ShapeDtypeStruct((1, extent // groups, extent * extent), jnp.bfloat16)
    tall_part = jax.ShapeDtypeStruct((extent * extent * extent // groups // WIDE, WIDE), jnp.bfloat16)
    fields = others(field)
    own = call(part_kernel, tall_part, field, *weighed[:pairs], kept=False)
    own, fields = lax.optimization_barrier((own, fields))
    rest = weighed[pairs:]
    return call(functools.partial(finish_kernel, groups), out, own, *fields, *rest, table, kept=False)


def solution(mesh):
    placed = (
        P("node", None, None),
        P("node", "term", None, None, None),
        P("node", "term", None),
        P("term", None, None),
        P(),
    )
    return jax.shard_map(
        per_device, mesh=mesh, in_specs=placed, out_specs=P("node", "term", None), check_vma=False
    )
```

```python
import functools
import math

import jax
import jax.numpy as jnp
from jax import lax
from jax.experimental import pallas as pl
from jax.experimental.pallas import tpu as pltpu
from jax.sharding import PartitionSpec as P

LANES = 128
WIDE = 256
BATCH = 2
PAD = 16
SKEW = 8
KEPT = 2**18


def dot(left, right):
    return jnp.dot(left, right, preferred_element_type=jnp.float32)


def iota(shape, dim):
    return lax.broadcasted_iota(jnp.int32, shape, dim)


def split_terms(packed, extent):
    per = LANES // extent
    wide = packed.astype(jnp.float32)
    out = []
    for term in range(per * packed.shape[0] // extent):
        block = wide[(term // per) * extent : (term // per + 1) * extent]
        mine = lax.div(iota(block.shape, 1), extent) == term % per
        out.append(jnp.where(mine, block, 0.0).astype(jnp.bfloat16))
    return out


def rows_spread(tensor_ref, mats, spread_ref, extent):
    per = LANES // extent
    half = extent // per
    stack = jnp.concatenate(mats, axis=0)
    for chunk in range(extent * extent // WIDE):
        piece = tensor_ref[:, chunk * WIDE : (chunk + 1) * WIDE]
        result = dot(stack, jnp.concatenate([piece] * per, axis=0))
        for part in range(WIDE // LANES):
            i = chunk * (WIDE // LANES) + part
            for term in range(len(mats)):
                spread_ref[term, pl.ds(i, extent, stride=half + SKEW), :] = result[
                    term * extent : (term + 1) * extent, part * LANES : (part + 1) * LANES
                ]


SUB = 8


def rows_apply(tensor_ref, mats, mixed_ref, extent):
    per = LANES // extent
    quads = WIDE // extent
    halves = SUB // quads
    count = 2 * halves
    stack = jnp.concatenate(mats, axis=0)
    row = iota((extent // SUB, SUB, LANES), 1)
    for first in range(0, extent // per, count):
        piece = tensor_ref[:, first * LANES : (first + count) * LANES]
        result = dot(stack, jnp.concatenate([piece] * per, axis=0))
        for term in range(len(mats)):
            tiles = [
                result[term * extent : (term + 1) * extent, k * LANES : (k + 1) * LANES].reshape(row.shape)
                for k in range(count)
            ]
            for half in range(halves):
                wanted = []
                for start in range(0, count, halves):
                    block = None
                    for k in range(halves):
                        shift = (k - half) * quads % SUB
                        moved = pltpu.roll(tiles[start + k], shift, 1) if shift else tiles[start + k]
                        block = moved if block is None else jnp.where(lax.div(row, quads) == k, moved, block)
                    wanted.append(block)
                packed = jnp.concatenate(wanted, axis=1).astype(jnp.bfloat16)
                for m in range(extent // SUB):
                    base = (m * halves + half) * (extent // per) * quads + first * quads
                    mixed_ref[term, base : base + count * quads, :] = packed[m]


def block_diagonals(mats, extent):
    per = LANES // extent
    quads = WIDE // extent
    rows = lax.rem(iota((LANES, WIDE), 0), extent)
    lanes = iota((LANES, WIDE), 1)
    wanted = per * lax.div(lax.rem(lanes, WIDE // per), quads) + lax.div(lanes, WIDE // per)
    pick = jnp.where(rows == wanted, 1.0, 0.0).astype(jnp.bfloat16)
    spread = dot(jnp.concatenate(mats, axis=0), pick)
    lanes = iota((WIDE, WIDE), 1)
    same = lax.div(iota((WIDE, WIDE), 0), extent) == lax.rem(lanes, quads)
    out = []
    for term in range(len(mats)):
        block = spread[term * extent : (term + 1) * extent]
        out.append(jnp.where(same, jnp.concatenate([block] * quads, axis=0), 0.0).astype(jnp.bfloat16))
    return out


def tall(tensor_ref):
    width = tensor_ref.shape[1]
    return jnp.concatenate([tensor_ref[:, j : j + WIDE] for j in range(0, width, WIDE)], axis=0)


def pair_up(accs, extent):
    per = LANES // extent
    out = []
    for first in range(0, len(accs), per):
        blocks = None
        for lo in range(per):
            acc = accs[first + lo]
            group = lax.div(iota((extent, LANES), 1), extent)
            kept = jnp.zeros((extent, LANES), jnp.float32)
            for p in range(per):
                kept = jnp.where(group == p, acc[p * extent : (p + 1) * extent], kept)
            total = kept
            for p in range(1, per):
                total = total + pltpu.roll(kept, p * extent, 1)
            blocks = total if blocks is None else jnp.where(group == lo, total, blocks)
        out.append(blocks)
    return out


def below_diagonal(shape, extent):
    rows, lanes = iota(shape, 0), lax.rem(iota(shape, 1), extent)
    return rows > lanes, rows == lanes


def fold(blocks):
    extent = blocks[0].shape[0]
    below, on = below_diagonal(blocks[0].shape, extent)
    out = []
    for first in range(0, len(blocks), 2):
        lower, upper = blocks[first], blocks[min(first + 1, len(blocks) - 1)]
        out.append(jnp.where(jnp.logical_or(below, on), lower, upper))
        row = jnp.sum(jnp.where(on, upper, 0.0), axis=0, keepdims=True)
        out.append(jnp.broadcast_to(row, (PAD, LANES)))
    return jnp.concatenate(out, axis=0).astype(jnp.bfloat16)


def unfold(message, pairs):
    height = message.shape[0] // (-(-pairs // 2))
    extent = height - PAD
    wide = message.astype(jnp.float32)
    out = []
    for base in range(0, message.shape[0], height):
        body, row = wide[base : base + extent], wide[base + extent : base + extent + 1]
        below, on = below_diagonal(body.shape, extent)
        turned = body.T
        parts = [turned[k : k + extent] for k in range(0, LANES, extent)]
        turned = jnp.concatenate(parts, axis=1)
        out.append(jnp.where(jnp.logical_or(below, on), body, turned))
        out.append(jnp.where(below, turned, jnp.where(on, row, body)))
    return jnp.concatenate(out[:pairs], axis=0).astype(jnp.bfloat16)


def apply_lanes(stacked, diagonals, extent):
    per = LANES // extent
    groups = stacked.shape[0] // extent
    lefts = []
    for diagonal in diagonals:
        moved = dot(stacked, diagonal).astype(jnp.bfloat16)
        for p in range(per):
            lanes = slice(p * (WIDE // per), (p + 1) * (WIDE // per))
            lefts.append(jnp.concatenate([moved[j * extent : (j + 1) * extent, lanes] for j in range(groups)], axis=1))
    return lefts


def contract(lefts, mixed, extent):
    per = LANES // extent
    accs = []
    for first in range(0, len(lefts) // per, BATCH):
        left = jnp.concatenate(lefts[first * per : (first + BATCH) * per], axis=0)
        right = jnp.concatenate([mixed[term] for term in range(first, first + BATCH)], axis=1)
        result = dot(left, right)
        for k in range(BATCH):
            accs.append(result[k * LANES : (k + 1) * LANES, k * LANES : (k + 1) * LANES])
    return fold(pair_up(accs, extent))


def swap(value, turn_ref, out_ref, extent):
    per = LANES // extent
    half = extent // per
    rows = iota((extent, extent), 0)
    wanted = per * lax.rem(rows, half) + lax.div(rows, half)
    order = jnp.where(iota((extent, extent), 1) == wanted, 1.0, 0.0).astype(jnp.bfloat16)
    sorted_rows = dot(order, value)
    group = lax.div(iota((half, LANES), 1), extent)
    for j in range(extent // per):
        given = [sorted_rows[p * half : (p + 1) * half, j * LANES : (j + 1) * LANES] for p in range(per)]
        for q in range(per):
            row = None
            for p in range(per):
                shift = (p - q) * extent % LANES
                moved = pltpu.roll(given[p], shift, 1) if shift else given[p]
                row = moved if row is None else jnp.where(group == p, moved, row)
            turn_ref[pl.ds(per * j + q, half, stride=extent + SKEW), :] = row
    for i in range(half):
        out_ref[:, i * LANES : (i + 1) * LANES] = turn_ref[pl.ds(i * (extent + SKEW), extent), :].astype(jnp.bfloat16)


def flip(value, extent):
    per = LANES // extent
    wide = value.astype(jnp.float32)
    tiles = []
    for j in range(extent // per):
        turned = wide[:, j * LANES : (j + 1) * LANES].T
        tiles.append(jnp.concatenate([turned[p * extent : (p + 1) * extent] for p in range(per)], axis=1))
    return jnp.concatenate(tiles, axis=1).astype(jnp.bfloat16)


DEPTH, FROM_LEFT, FROM_RIGHT, FROM_PARENT, POSITION, GROUP, APART, UP_RELAY, DOWN_RELAY, TABLE = *range(7), 8, 16, 24
LOW = 4


def entry(table_ref, row):
    return table_ref[row : row + 1, :]


def fill_table(map_ref, me, inverse_ref, table_ref):
    def put(row, value):
        table_ref[row : row + 1, :] = jnp.full((1, LANES), value, jnp.int32)

    nodes = map_ref.shape[0]

    def note(slot, carry):
        inverse_ref[map_ref[slot]] = slot
        return carry

    lax.fori_loop(0, nodes, note, 0)
    low = lax.rem(me, LOW)
    high = lax.div(me, LOW)

    def routes(slot):
        position = map_ref[slot]
        last = jnp.int32(nodes - 1)
        left = inverse_ref[jnp.minimum(2 * position + 1, last)]
        right = inverse_ref[jnp.minimum(2 * position + 2, last)]
        parent = inverse_ref[lax.div(jnp.maximum(position - 1, 0), 2)]
        return position, left, right, parent

    position, left, right, parent = routes(me)
    depth = jnp.int32(0)
    for power in range(1, nodes.bit_length() - 1):
        depth = depth + jnp.where(position + 1 >= 2**power, 1, 0)
    put(DEPTH, jnp.where(position >= nodes - 1, -1, depth))
    put(POSITION, position)
    put(GROUP, lax.axis_index("term"))
    put(APART, inverse_ref[0] ^ inverse_ref[2])
    put(FROM_LEFT, lax.rem(left, LOW) ^ low)
    put(FROM_RIGHT, lax.rem(right, LOW) ^ low)
    put(FROM_PARENT, lax.rem(parent, LOW) ^ low)
    for j in range(LOW):
        position, left, right, parent = routes(high * LOW + (low ^ j))
        put(UP_RELAY + 2 * j, lax.div(left, LOW) ^ high)
        put(UP_RELAY + 2 * j + 1, lax.div(right, LOW) ^ high)
        put(DOWN_RELAY + j, 2 * (lax.div(parent, LOW) ^ high) + lax.rem(position + 1, 2))


def choose(index, choices):
    out = choices[0]().astype(jnp.float32)
    for k in range(1, len(choices)):
        out = jnp.where(index == k, choices[k]().astype(jnp.float32), out)
    return out.astype(jnp.bfloat16)


def either(mask, old, new):
    return choose(jnp.where(mask, 1, 0), [old, new])


def loads(refs, *where):
    return [lambda ref=ref: ref[where] if where else ref[...] for ref in refs]


def start_kernel(
    tensor_hbm, prim_hbm, active_hbm, top_hbm, map_hbm,
    abc_ref, bac_ref, cba_ref, left_ref, right_ref, field_ref, out_ref, table_ref,
    prim_ref, active_ref, top_ref, map_ref, mixed_ref, turn_ref, inverse_ref, sems,
):
    given = (tensor_hbm.at[0], prim_hbm, top_hbm, active_hbm, map_hbm)
    held = (abc_ref, prim_ref, top_ref, active_ref, map_ref)
    copies = [pltpu.make_async_copy(*pair, sems.at[i]) for i, pair in enumerate(zip(given, held))]
    for copy in copies:
        copy.start()
    extent = abc_ref.shape[0]
    per = LANES // extent
    terms = prim_ref.shape[1]
    for copy in copies[:0:-1]:
        copy.wait()
        if copy is copies[-1]:
            fill_table(map_ref, lax.axis_index("node"), inverse_ref, table_ref)
    eye = jnp.where(iota((extent, extent), 0) == iota((extent, extent), 1), 1.0, 0.0)

    def operator(term, side):
        return jnp.where(active_ref[0, side, term] == 1, prim_ref[0, term, side].astype(jnp.float32), eye)

    for first in range(0, terms, per):
        rows = pl.ds(first // per * extent, extent)
        for side, ref in ((0, left_ref), (1, right_ref)):
            side_by_side = [operator(first + lo, side) for lo in range(per)]
            ref[rows, :] = jnp.concatenate(side_by_side, axis=1).astype(jnp.bfloat16)
        fields = [top_ref[first + lo].astype(jnp.float32) for lo in range(per)]
        field_ref[rows, :] = jnp.concatenate(fields, axis=1).astype(jnp.bfloat16)
    diagonals = block_diagonals(split_terms(left_ref[...], extent), extent)
    copies[0].wait()
    swap(abc_ref[...], turn_ref, bac_ref, extent)
    cba_ref[...] = flip(abc_ref[...], extent)
    rows_apply(bac_ref, split_terms(right_ref[...], extent), mixed_ref, extent)
    out_ref[...] = contract(apply_lanes(tall(cba_ref), diagonals, extent), mixed_ref, extent)


def turn_kernel(bac_ref, cba_ref, table_ref, turned_ref, apart_ref, turn_ref):
    extent = bac_ref.shape[0]
    apart_ref[0] = jnp.max(entry(table_ref, APART)) - 1
    swap(cba_ref[...], turn_ref, turned_ref.at[0], extent)
    swap(flip(bac_ref[...], extent), turn_ref, turned_ref.at[1], extent)


def both_kernel(first_ref, second_ref, out_ref):
    out_ref[0] = first_ref[...]
    out_ref[1] = second_ref[...]


def relay_up_kernel(*refs):
    parts, table_ref, outs = refs[:-5], refs[-5], refs[-4:]
    for j, out in enumerate(outs):
        for side in range(2):
            out[side] = choose(entry(table_ref, UP_RELAY + 2 * j + side), loads(parts))


def relay_down_kernel(*refs):
    parts, table_ref, outs = refs[:-5], refs[-5], refs[-4:]
    choices = [f for part in parts for side in range(2) for f in loads([part], side)]
    for j, out in enumerate(outs):
        out[...] = choose(entry(table_ref, DOWN_RELAY + j), choices)


def up_kernel(depth, *refs):
    came, (bac_ref, cba_ref, old_left_ref, old_right_ref, table_ref) = refs[:LOW], refs[LOW : LOW + 5]
    left_ref, right_ref, out_ref, mixed_ref = refs[LOW + 5 :]
    extent = bac_ref.shape[0]
    now = entry(table_ref, DEPTH) == depth
    pairs = old_left_ref.shape[0] // extent
    left = unfold(choose(entry(table_ref, FROM_LEFT), loads(came, 0)), pairs)
    right = unfold(choose(entry(table_ref, FROM_RIGHT), loads(came, 1)), pairs)
    left_ref[...] = either(now, lambda: old_left_ref[...], lambda: left)
    right_ref[...] = either(now, lambda: old_right_ref[...], lambda: right)
    rows_apply(bac_ref, split_terms(right_ref[...], extent), mixed_ref, extent)
    diagonals = block_diagonals(split_terms(left_ref[...], extent), extent)
    out_ref[...] = contract(apply_lanes(tall(cba_ref), diagonals, extent), mixed_ref, extent)


def top_kernel(
    came_ref, abc_ref, bac_ref, turned_ref, field_ref, old_left_ref, old_right_ref, table_ref,
    sides_ref, out_ref, mixed_ref,
):
    extent = bac_ref.shape[0]
    now = entry(table_ref, DEPTH) == 0
    diagonals = block_diagonals(split_terms(field_ref[...], extent), extent)
    left_lanes = apply_lanes(tall(abc_ref), diagonals, extent)
    pairs = old_left_ref.shape[0] // extent
    sides_ref[0] = either(now, lambda: old_left_ref[...], lambda: unfold(came_ref[0], pairs))
    sides_ref[1] = either(now, lambda: old_right_ref[...], lambda: unfold(came_ref[1], pairs))
    mix(turned_ref, sides_ref, mixed_ref)
    out_ref[0] = contract(left_lanes, mixed_ref.at[0], extent)
    out_ref[1] = contract(apply_lanes(tall(bac_ref), diagonals, extent), mixed_ref.at[1], extent)


def below_top_kernel(
    came_ref, abc_ref, bac_ref, turned_ref, old_ref, sides_ref, table_ref,
    field_ref, out_ref, mixed_ref,
):
    position = entry(table_ref, POSITION)
    came = unfold(either(position == 2, *[f for side in range(2) for f in loads([came_ref], side)]), old_ref.shape[0] // abc_ref.shape[0])
    now = jnp.logical_or(position == 1, position == 2)
    field_ref[...] = either(now, lambda: old_ref[...], lambda: came)
    mix(turned_ref, sides_ref, mixed_ref)
    spread_down(abc_ref, bac_ref, field_ref, out_ref, mixed_ref)


def down_kernel(depth, *refs):
    came, (abc_ref, bac_ref, old_ref, mixed_ref, table_ref) = refs[:LOW], refs[LOW : LOW + 5]
    field_ref, out_ref = refs[LOW + 5 :]
    arrive(depth, old_ref.shape[0] // abc_ref.shape[0], came, old_ref, table_ref, field_ref)
    spread_down(abc_ref, bac_ref, field_ref, out_ref, mixed_ref)


def arrive(depth, pairs, came, old_ref, table_ref, field_ref):
    arrived = choose(entry(table_ref, FROM_PARENT), loads(came))
    arrived = unfold(arrived, pairs)
    field_ref[...] = either(entry(table_ref, DEPTH) == depth, lambda: old_ref[...], lambda: arrived)


def mix(turned_ref, sides_ref, mixed_ref):
    extent = turned_ref.shape[1]
    rows_apply(turned_ref.at[0], split_terms(sides_ref[1], extent), mixed_ref.at[0], extent)
    rows_apply(turned_ref.at[1], split_terms(sides_ref[0], extent), mixed_ref.at[1], extent)


def spread_down(abc_ref, bac_ref, field_ref, out_ref, mixed_ref):
    extent = bac_ref.shape[0]
    diagonals = block_diagonals(split_terms(field_ref[...], extent), extent)
    out_ref[0] = contract(apply_lanes(tall(abc_ref), diagonals, extent), mixed_ref.at[0], extent)
    out_ref[1] = contract(apply_lanes(tall(bac_ref), diagonals, extent), mixed_ref.at[1], extent)


def weigh_kernel(pair, bac_ref, sides_ref, table_ref, out_ref, spread_ref):
    extent = bac_ref.shape[0]
    mine = slice(pair * extent, (pair + 1) * extent)
    rows_out = out_ref.shape[1]
    per = LANES // extent
    half = extent // per
    rows_spread(bac_ref, split_terms(sides_ref[1, mine], extent), spread_ref, extent)
    rows = lax.rem(iota((LANES, extent), 0), extent)
    lanes = iota((LANES, extent), 1)
    wanted = per * lax.rem(lanes, half) + lax.div(lanes, half)
    pick = jnp.where(rows == wanted, 1.0, 0.0).astype(jnp.bfloat16)
    group = lax.div(iota((half, LANES), 1), extent)
    for term, mat in enumerate(split_terms(sides_ref[0, mine], extent)):
        permuted = dot(mat, pick)
        kept = permuted[:rows_out]
        for g in range(1, extent // rows_out):
            kept = jnp.where(entry(table_ref, GROUP)[:, :extent] == g, permuted[g * rows_out : (g + 1) * rows_out], kept)
        kept = kept.astype(jnp.bfloat16)
        tiles = []
        for j in range(extent // per):
            given = [spread_ref[term, pl.ds((per * j + q) * (half + SKEW), half), :] for q in range(per)]
            stacked = []
            for p in range(per):
                row = None
                for q in range(per):
                    shift = (q - p) * extent % LANES
                    moved = pltpu.roll(given[q], shift, 1) if shift else given[q]
                    row = moved if row is None else jnp.where(group == q, moved, row)
                stacked.append(row)
            tiles.append(jnp.concatenate(stacked, axis=0).astype(jnp.bfloat16))
        for j in range(0, len(tiles), WIDE // LANES):
            wide = jnp.concatenate(tiles[j : j + WIDE // LANES], axis=1)
            out_ref[term, :, j * LANES : j * LANES + WIDE] = dot(kept, wide).astype(jnp.bfloat16)


def last_kernel(depth, pairs, *refs):
    came, (old_ref, table_ref, field_ref) = refs[:LOW], refs[LOW:]
    arrive(depth, pairs, came, old_ref, table_ref, field_ref)


def part_kernel(field_ref, *refs):
    out_ref = refs[-1]
    width = refs[0].shape[2]
    out_ref[...] = weighted_sum(refs[:-1], field_ref[...], math.isqrt(width)).astype(jnp.bfloat16)


def finish_kernel(groups, own_ref, *refs):
    table_ref, out_ref = refs[-2:]
    rows, width = out_ref.shape[1:]
    total = own_ref[...].astype(jnp.float32)
    fields, weighed = refs[: groups - 1], refs[groups - 1 : -2]
    for g, field_ref in enumerate(fields):
        pairs = len(weighed) // len(fields)
        part = weighted_sum(weighed[g * pairs : (g + 1) * pairs], field_ref[...], math.isqrt(width))
        total = total + part.astype(jnp.bfloat16).astype(jnp.float32)
    real = jnp.concatenate([entry(table_ref, DEPTH)] * (WIDE // LANES), axis=1) >= 0
    total = jnp.where(real, total, 0.0).astype(jnp.bfloat16)
    for j in range(width // WIDE):
        out_ref[0, :, j * WIDE : (j + 1) * WIDE] = total[j * rows : (j + 1) * rows]


def weighted_sum(weighed_refs, field, extent):
    per, _, width = weighed_refs[0].shape
    quads = WIDE // extent
    copies = pick_rows(LANES, WIDE, extent)
    spread = dot(jnp.concatenate(split_terms(field, extent), axis=0), copies)
    same = lax.div(iota((WIDE, WIDE), 0), extent) == lax.div(iota((WIDE, WIDE), 1), extent)
    total = None
    for term in range(per * len(weighed_refs)):
        weighed_ref = weighed_refs[term // per]
        block = spread[term * extent : (term + 1) * extent]
        diagonal = jnp.where(same, jnp.concatenate([block] * quads, axis=0), 0.0).astype(jnp.bfloat16)
        pieces = [weighed_ref[term % per, :, j : j + WIDE] for j in range(0, width, WIDE)]
        part = dot(jnp.concatenate(pieces, axis=0), diagonal)
        total = part if total is None else total + part
    return total


def pick_rows(rows, lanes, extent):
    same = lax.rem(iota((rows, lanes), 0), extent) == lax.rem(iota((rows, lanes), 1), extent)
    return jnp.where(same, 1.0, 0.0).astype(jnp.bfloat16)


VMEM = pl.BlockSpec(memory_space=pltpu.VMEM)
SMEM = pl.BlockSpec(memory_space=pltpu.SMEM)
HBM = pl.BlockSpec(memory_space=pltpu.HBM)


def call(kernel, out_shape, *operands, scratch=(), smem_out=(), in_hbm=(), kept=True, in_vmem=False, beside=()):
    shapes = out_shape if isinstance(out_shape, list) else [out_shape]
    specs = [SMEM if i in smem_out else VMEM for i in range(len(shapes))]
    taken = [VMEM] * len(operands)
    operands = list(operands)
    for i, operand in enumerate(operands):
        if i in in_hbm:
            taken[i] = HBM
            operands[i] = pltpu.with_memory_space_constraint(operand, pltpu.HBM)
        elif operand.size >= KEPT:
            operands[i] = pltpu.with_memory_space_constraint(operand, pltpu.VMEM)
    shapes = [pltpu.VMEM(x.shape, x.dtype) if in_vmem or (kept and x.size >= KEPT) else x for x in shapes]
    given = len(operands)
    operands += [pltpu.with_memory_space_constraint(x, pltpu.VMEM) for x in beside]

    def without(*refs):
        kernel(*refs[:given], *refs[len(operands) :])

    return pl.pallas_call(
        without,
        out_shape=shapes if isinstance(out_shape, list) else shapes[0],
        in_specs=taken + [VMEM] * len(beside),
        out_specs=specs if isinstance(out_shape, list) else specs[0],
        scratch_shapes=list(scratch),
        compiler_params=pltpu.CompilerParams(vmem_limit_bytes=16 * 2**20),
    )(*operands)


def exchange(value, mask, nodes):
    return lax.ppermute(value, "node", [(i, i ^ mask) for i in range(nodes)])


def high_exchange(value, nodes):
    return [value] + [exchange(value, high * LOW, nodes) for high in range(1, nodes // LOW)]


def low_exchange(values, nodes):
    return [values[0]] + [exchange(values[j], j, nodes) for j in range(1, LOW)]


def per_device(node_tensors, prim_ops, active, top_field, node_map):
    nodes = lax.axis_size("node")
    groups = lax.axis_size("term")
    depths = nodes.bit_length() - 1
    turned_active = jnp.swapaxes(active, 1, 2)

    extent = node_tensors.shape[1]
    terms = prim_ops.shape[1]
    pairs = terms * extent // LANES
    flat = jax.ShapeDtypeStruct((extent, extent * extent), jnp.bfloat16)
    mats = jax.ShapeDtypeStruct((pairs * extent, LANES), jnp.bfloat16)
    two = jax.ShapeDtypeStruct((2,) + mats.shape, jnp.bfloat16)
    message = jax.ShapeDtypeStruct((-(-pairs // 2) * (extent + PAD), LANES), jnp.bfloat16)
    messages = jax.ShapeDtypeStruct((2,) + message.shape, jnp.bfloat16)
    table_shape = jax.ShapeDtypeStruct((TABLE, LANES), jnp.int32)
    spread = jax.ShapeDtypeStruct((terms, extent * extent * extent // LANES, LANES), jnp.bfloat16)
    part = jax.ShapeDtypeStruct((LANES // extent, extent // groups, extent * extent), jnp.bfloat16)
    per = LANES // extent
    space = pltpu.VMEM((per, extent * (extent // per + SKEW), LANES), jnp.float32)
    both = [pltpu.VMEM((2,) + spread.shape, jnp.bfloat16)]
    mixed_space = pltpu.VMEM(spread.shape, jnp.bfloat16)
    turn_space = pltpu.VMEM((extent // per * (extent + SKEW), LANES), jnp.float32)

    def others(value):
        return [
            lax.ppermute(value, "term", [(i, (i + shift) % groups) for i in range(groups)]) for shift in range(1, groups)
        ]

    def weigh_beside(count, values):
        first = len(weighed)
        for sides, pair in to_weigh[first : first + count]:
            weighed.append(call(functools.partial(weigh_kernel, pair), part, bac, sides, table, scratch=[space]))
        values, weighed[first:] = lax.optimization_barrier((values, weighed[first:]))
        return values

    def with_top(first, second):
        def branch(mask):
            def go(first, second):
                came = exchange(first, nodes // 2, nodes), exchange(second, mask, nodes)
                return call(both_kernel, messages, *came, in_vmem=True)

            return go

        return lax.switch(apart[0], [branch(mask) for mask in range(1, nodes)], first, second)

    abc, bac, cba, left, right, field, mine, table = call(
        start_kernel,
        [flat, flat, flat, mats, mats, mats, message, table_shape],
        node_tensors,
        prim_ops,
        turned_active,
        top_field,
        node_map,
        scratch=[
            pltpu.VMEM(prim_ops.shape, jnp.bfloat16),
            pltpu.SMEM(turned_active.shape, jnp.int32),
            pltpu.VMEM(top_field.shape, jnp.bfloat16),
            pltpu.SMEM(node_map.shape, jnp.int32),
            mixed_space,
            turn_space,
            pltpu.SMEM((nodes,), jnp.int32),
            pltpu.SemaphoreType.DMA((5,)),
        ],
        in_hbm=(0, 1, 2, 3, 4),
    )
    for depth in range(depths - 2, 0, -1):
        parts = high_exchange(mine, nodes)
        came = low_exchange(call(relay_up_kernel, [messages] * LOW, *parts, table), nodes)
        if depth == depths - 2:
            turned, apart = call(
                turn_kernel,
                [jax.ShapeDtypeStruct((2,) + flat.shape, flat.dtype), jax.ShapeDtypeStruct((1,), jnp.int32)],
                bac,
                cba,
                table,
                scratch=[turn_space],
                smem_out=(1,),
            )
            came, turned, apart = lax.optimization_barrier((came, turned, apart))
        left, right, mine = call(
            functools.partial(up_kernel, depth),
            [mats, mats, message],
            *came,
            bac,
            cba,
            left,
            right,
            table,
            scratch=[mixed_space],
        )

    came = pltpu.with_memory_space_constraint(with_top(mine, mine), pltpu.VMEM)
    sides, fields = call(
        top_kernel,
        [two, messages],
        came,
        abc,
        bac,
        turned,
        field,
        left,
        right,
        table,
        scratch=both,
    )
    came = pltpu.with_memory_space_constraint(with_top(fields[0], fields[1]), pltpu.VMEM)
    to_weigh = [(each, pair) for each in [sides] + others(sides) for pair in range(pairs)]
    share = -(-len(to_weigh) // (1 + 3 * (depths - 3)))
    field, fields = call(
        below_top_kernel,
        [mats, messages],
        came,
        abc,
        bac,
        turned,
        field,
        sides,
        table,
        scratch=both,
    )
    weighed = []
    for depth in range(2, depths):
        parts = high_exchange(fields, nodes)
        if depth == 2:
            ahead = jax.ShapeDtypeStruct((2,) + spread.shape, spread.dtype)
            parts, mixed = lax.optimization_barrier((parts, call(mix, ahead, turned, sides)))
        else:
            parts = weigh_beside(2 * share, parts)
        came = low_exchange(call(relay_down_kernel, [message] * LOW, *parts, table), nodes)
        came = weigh_beside(share, came)
        if depth < depths - 1:
            field, fields = call(
                functools.partial(down_kernel, depth),
                [mats, messages],
                *came,
                abc,
                bac,
                field,
                mixed,
                table,
            )
    field = call(functools.partial(last_kernel, depths - 1, pairs), mats, *came, field, table)
    out = jax.ShapeDtypeStruct((1, extent // groups, extent * extent), jnp.bfloat16)
    tall_part = jax.ShapeDtypeStruct((extent * extent * extent // groups // WIDE, WIDE), jnp.bfloat16)
    fields = others(field)
    own = call(part_kernel, tall_part, field, *weighed[:pairs], kept=False)
    own, fields = lax.optimization_barrier((own, fields))
    rest = weighed[pairs:]
    return call(functools.partial(finish_kernel, groups), out, own, *fields, *rest, table, kept=False)


def solution(mesh):
    placed = (
        P("node", None, None),
        P("node", "term", None, None, None),
        P("node", "term", None),
        P("term", None, None),
        P(),
    )
    return jax.shard_map(
        per_device, mesh=mesh, in_specs=placed, out_specs=P("node", "term", None), check_vma=False
    )
```

```python
import functools
import math

import jax
import jax.numpy as jnp
from jax import lax
from jax.experimental import pallas as pl
from jax.experimental.pallas import tpu as pltpu
from jax.sharding import PartitionSpec as P

LANES = 128
WIDE = 256
BATCH = 2
PAD = 16
SKEW = 8
KEPT = 2**18


def dot(left, right):
    return jnp.dot(left, right, preferred_element_type=jnp.float32)


def iota(shape, dim):
    return lax.broadcasted_iota(jnp.int32, shape, dim)


def split_terms(packed, extent):
    per = LANES // extent
    wide = packed.astype(jnp.float32)
    out = []
    for term in range(per * packed.shape[0] // extent):
        block = wide[(term // per) * extent : (term // per + 1) * extent]
        mine = lax.div(iota(block.shape, 1), extent) == term % per
        out.append(jnp.where(mine, block, 0.0).astype(jnp.bfloat16))
    return out


def rows_spread(tensor_ref, mats, spread_ref, extent):
    per = LANES // extent
    half = extent // per
    stack = jnp.concatenate(mats, axis=0)
    for chunk in range(extent * extent // WIDE):
        piece = tensor_ref[:, chunk * WIDE : (chunk + 1) * WIDE]
        result = dot(stack, jnp.concatenate([piece] * per, axis=0))
        for part in range(WIDE // LANES):
            i = chunk * (WIDE // LANES) + part
            for term in range(len(mats)):
                spread_ref[term, pl.ds(i, extent, stride=half + SKEW), :] = result[
                    term * extent : (term + 1) * extent, part * LANES : (part + 1) * LANES
                ]


SUB = 8


def rows_apply(tensor_ref, mats, mixed_ref, extent):
    per = LANES // extent
    quads = WIDE // extent
    halves = SUB // quads
    count = 2 * halves
    stack = jnp.concatenate(mats, axis=0)
    row = iota((extent // SUB, SUB, LANES), 1)
    for first in range(0, extent // per, count):
        piece = tensor_ref[:, first * LANES : (first + count) * LANES]
        result = dot(stack, jnp.concatenate([piece] * per, axis=0))
        for term in range(len(mats)):
            tiles = [
                result[term * extent : (term + 1) * extent, k * LANES : (k + 1) * LANES].reshape(row.shape)
                for k in range(count)
            ]
            for half in range(halves):
                wanted = []
                for start in range(0, count, halves):
                    block = None
                    for k in range(halves):
                        shift = (k - half) * quads % SUB
                        moved = pltpu.roll(tiles[start + k], shift, 1) if shift else tiles[start + k]
                        block = moved if block is None else jnp.where(lax.div(row, quads) == k, moved, block)
                    wanted.append(block)
                packed = jnp.concatenate(wanted, axis=1).astype(jnp.bfloat16)
                for m in range(extent // SUB):
                    base = (m * halves + half) * (extent // per) * quads + first * quads
                    mixed_ref[term, base : base + count * quads, :] = packed[m]


def block_diagonals(mats, extent):
    per = LANES // extent
    quads = WIDE // extent
    rows = lax.rem(iota((LANES, WIDE), 0), extent)
    lanes = iota((LANES, WIDE), 1)
    wanted = per * lax.div(lax.rem(lanes, WIDE // per), quads) + lax.div(lanes, WIDE // per)
    pick = jnp.where(rows == wanted, 1.0, 0.0).astype(jnp.bfloat16)
    spread = dot(jnp.concatenate(mats, axis=0), pick)
    lanes = iota((WIDE, WIDE), 1)
    same = lax.div(iota((WIDE, WIDE), 0), extent) == lax.rem(lanes, quads)
    out = []
    for term in range(len(mats)):
        block = spread[term * extent : (term + 1) * extent]
        out.append(jnp.where(same, jnp.concatenate([block] * quads, axis=0), 0.0).astype(jnp.bfloat16))
    return out


def tall(tensor_ref):
    width = tensor_ref.shape[1]
    return jnp.concatenate([tensor_ref[:, j : j + WIDE] for j in range(0, width, WIDE)], axis=0)


def pair_up(accs, extent):
    per = LANES // extent
    out = []
    for first in range(0, len(accs), per):
        blocks = None
        for lo in range(per):
            acc = accs[first + lo]
            group = lax.div(iota((extent, LANES), 1), extent)
            kept = jnp.zeros((extent, LANES), jnp.float32)
            for p in range(per):
                kept = jnp.where(group == p, acc[p * extent : (p + 1) * extent], kept)
            total = kept
            for p in range(1, per):
                total = total + pltpu.roll(kept, p * extent, 1)
            blocks = total if blocks is None else jnp.where(group == lo, total, blocks)
        out.append(blocks)
    return out


def below_diagonal(shape, extent):
    rows, lanes = iota(shape, 0), lax.rem(iota(shape, 1), extent)
    return rows > lanes, rows == lanes


def fold(blocks):
    extent = blocks[0].shape[0]
    below, on = below_diagonal(blocks[0].shape, extent)
    out = []
    for first in range(0, len(blocks), 2):
        lower, upper = blocks[first], blocks[min(first + 1, len(blocks) - 1)]
        out.append(jnp.where(jnp.logical_or(below, on), lower, upper))
        row = jnp.sum(jnp.where(on, upper, 0.0), axis=0, keepdims=True)
        out.append(jnp.broadcast_to(row, (PAD, LANES)))
    return jnp.concatenate(out, axis=0).astype(jnp.bfloat16)


def unfold(message, pairs):
    height = message.shape[0] // (-(-pairs // 2))
    extent = height - PAD
    wide = message.astype(jnp.float32)
    out = []
    for base in range(0, message.shape[0], height):
        body, row = wide[base : base + extent], wide[base + extent : base + extent + 1]
        below, on = below_diagonal(body.shape, extent)
        turned = body.T
        parts = [turned[k : k + extent] for k in range(0, LANES, extent)]
        turned = jnp.concatenate(parts, axis=1)
        out.append(jnp.where(jnp.logical_or(below, on), body, turned))
        out.append(jnp.where(below, turned, jnp.where(on, row, body)))
    return jnp.concatenate(out[:pairs], axis=0).astype(jnp.bfloat16)


def apply_lanes(stacked, diagonals, extent):
    per = LANES // extent
    groups = stacked.shape[0] // extent
    lefts = []
    for diagonal in diagonals:
        moved = dot(stacked, diagonal).astype(jnp.bfloat16)
        for p in range(per):
            lanes = slice(p * (WIDE // per), (p + 1) * (WIDE // per))
            lefts.append(jnp.concatenate([moved[j * extent : (j + 1) * extent, lanes] for j in range(groups)], axis=1))
    return lefts


def contract(lefts, mixed, extent):
    per = LANES // extent
    accs = []
    for first in range(0, len(lefts) // per, BATCH):
        left = jnp.concatenate(lefts[first * per : (first + BATCH) * per], axis=0)
        right = jnp.concatenate([mixed[term] for term in range(first, first + BATCH)], axis=1)
        result = dot(left, right)
        for k in range(BATCH):
            accs.append(result[k * LANES : (k + 1) * LANES, k * LANES : (k + 1) * LANES])
    return fold(pair_up(accs, extent))


def swap(value, turn_ref, out_ref, extent):
    per = LANES // extent
    half = extent // per
    rows = iota((extent, extent), 0)
    wanted = per * lax.rem(rows, half) + lax.div(rows, half)
    order = jnp.where(iota((extent, extent), 1) == wanted, 1.0, 0.0).astype(jnp.bfloat16)
    sorted_rows = dot(order, value)
    group = lax.div(iota((half, LANES), 1), extent)
    for j in range(extent // per):
        given = [sorted_rows[p * half : (p + 1) * half, j * LANES : (j + 1) * LANES] for p in range(per)]
        for q in range(per):
            row = None
            for p in range(per):
                shift = (p - q) * extent % LANES
                moved = pltpu.roll(given[p], shift, 1) if shift else given[p]
                row = moved if row is None else jnp.where(group == p, moved, row)
            turn_ref[pl.ds(per * j + q, half, stride=extent + SKEW), :] = row
    for i in range(half):
        out_ref[:, i * LANES : (i + 1) * LANES] = turn_ref[pl.ds(i * (extent + SKEW), extent), :].astype(jnp.bfloat16)


def flip(value, extent):
    per = LANES // extent
    wide = value.astype(jnp.float32)
    tiles = []
    for j in range(extent // per):
        turned = wide[:, j * LANES : (j + 1) * LANES].T
        tiles.append(jnp.concatenate([turned[p * extent : (p + 1) * extent] for p in range(per)], axis=1))
    return jnp.concatenate(tiles, axis=1).astype(jnp.bfloat16)


DEPTH, FROM_LEFT, FROM_RIGHT, FROM_PARENT, POSITION, GROUP, APART, UP_RELAY, DOWN_RELAY, TABLE = *range(7), 8, 16, 24
LOW = 4


def entry(table_ref, row):
    return table_ref[row : row + 1, :]


def fill_table(map_ref, me, inverse_ref, table_ref):
    def put(row, value):
        table_ref[row : row + 1, :] = jnp.full((1, LANES), value, jnp.int32)

    nodes = map_ref.shape[0]

    def note(slot, carry):
        inverse_ref[map_ref[slot]] = slot
        return carry

    lax.fori_loop(0, nodes, note, 0)
    low = lax.rem(me, LOW)
    high = lax.div(me, LOW)

    def routes(slot):
        position = map_ref[slot]
        last = jnp.int32(nodes - 1)
        left = inverse_ref[jnp.minimum(2 * position + 1, last)]
        right = inverse_ref[jnp.minimum(2 * position + 2, last)]
        parent = inverse_ref[lax.div(jnp.maximum(position - 1, 0), 2)]
        return position, left, right, parent

    position, left, right, parent = routes(me)
    depth = jnp.int32(0)
    for power in range(1, nodes.bit_length() - 1):
        depth = depth + jnp.where(position + 1 >= 2**power, 1, 0)
    put(DEPTH, jnp.where(position >= nodes - 1, -1, depth))
    put(POSITION, position)
    put(GROUP, lax.axis_index("term"))
    put(APART, inverse_ref[0] ^ inverse_ref[2])
    put(FROM_LEFT, lax.rem(left, LOW) ^ low)
    put(FROM_RIGHT, lax.rem(right, LOW) ^ low)
    put(FROM_PARENT, lax.rem(parent, LOW) ^ low)
    for j in range(LOW):
        position, left, right, parent = routes(high * LOW + (low ^ j))
        put(UP_RELAY + 2 * j, lax.div(left, LOW) ^ high)
        put(UP_RELAY + 2 * j + 1, lax.div(right, LOW) ^ high)
        put(DOWN_RELAY + j, 2 * (lax.div(parent, LOW) ^ high) + lax.rem(position + 1, 2))


def choose(index, choices):
    out = choices[0]().astype(jnp.float32)
    for k in range(1, len(choices)):
        out = jnp.where(index == k, choices[k]().astype(jnp.float32), out)
    return out.astype(jnp.bfloat16)


def either(mask, old, new):
    return choose(jnp.where(mask, 1, 0), [old, new])


def loads(refs, *where):
    return [lambda ref=ref: ref[where] if where else ref[...] for ref in refs]


def start_kernel(
    tensor_hbm, prim_hbm, active_hbm, top_hbm, map_hbm,
    abc_ref, bac_ref, cba_ref, left_ref, right_ref, field_ref, out_ref, table_ref,
    prim_ref, active_ref, top_ref, map_ref, mixed_ref, turn_ref, inverse_ref, sems,
):
    given = (tensor_hbm.at[0], prim_hbm, top_hbm, active_hbm, map_hbm)
    held = (abc_ref, prim_ref, top_ref, active_ref, map_ref)
    copies = [pltpu.make_async_copy(*pair, sems.at[i]) for i, pair in enumerate(zip(given, held))]
    for copy in copies:
        copy.start()
    extent = abc_ref.shape[0]
    per = LANES // extent
    terms = prim_ref.shape[1]
    for copy in copies[:0:-1]:
        copy.wait()
        if copy is copies[-1]:
            fill_table(map_ref, lax.axis_index("node"), inverse_ref, table_ref)
    eye = jnp.where(iota((extent, extent), 0) == iota((extent, extent), 1), 1.0, 0.0)

    def operator(term, side):
        return jnp.where(active_ref[0, side, term] == 1, prim_ref[0, term, side].astype(jnp.float32), eye)

    for first in range(0, terms, per):
        rows = pl.ds(first // per * extent, extent)
        for side, ref in ((0, left_ref), (1, right_ref)):
            side_by_side = [operator(first + lo, side) for lo in range(per)]
            ref[rows, :] = jnp.concatenate(side_by_side, axis=1).astype(jnp.bfloat16)
        fields = [top_ref[first + lo].astype(jnp.float32) for lo in range(per)]
        field_ref[rows, :] = jnp.concatenate(fields, axis=1).astype(jnp.bfloat16)
    diagonals = block_diagonals(split_terms(left_ref[...], extent), extent)
    copies[0].wait()
    swap(abc_ref[...], turn_ref, bac_ref, extent)
    cba_ref[...] = flip(abc_ref[...], extent)
    rows_apply(bac_ref, split_terms(right_ref[...], extent), mixed_ref, extent)
    out_ref[...] = contract(apply_lanes(tall(cba_ref), diagonals, extent), mixed_ref, extent)


def turn_kernel(bac_ref, cba_ref, table_ref, turned_ref, apart_ref, turn_ref):
    extent = bac_ref.shape[0]
    apart_ref[0] = jnp.max(entry(table_ref, APART)) - 1
    swap(cba_ref[...], turn_ref, turned_ref.at[0], extent)
    swap(flip(bac_ref[...], extent), turn_ref, turned_ref.at[1], extent)


def both_kernel(first_ref, second_ref, out_ref):
    out_ref[0] = first_ref[...]
    out_ref[1] = second_ref[...]


def relay_up_kernel(*refs):
    parts, table_ref, outs = refs[:-5], refs[-5], refs[-4:]
    for j, out in enumerate(outs):
        for side in range(2):
            out[side] = choose(entry(table_ref, UP_RELAY + 2 * j + side), loads(parts))


def relay_down_kernel(*refs):
    parts, table_ref, outs = refs[:-5], refs[-5], refs[-4:]
    choices = [f for part in parts for side in range(2) for f in loads([part], side)]
    for j, out in enumerate(outs):
        out[...] = choose(entry(table_ref, DOWN_RELAY + j), choices)


def up_kernel(depth, *refs):
    came, (bac_ref, cba_ref, old_left_ref, old_right_ref, table_ref) = refs[:LOW], refs[LOW : LOW + 5]
    left_ref, right_ref, out_ref, mixed_ref = refs[LOW + 5 :]
    extent = bac_ref.shape[0]
    now = entry(table_ref, DEPTH) == depth
    pairs = old_left_ref.shape[0] // extent
    left = unfold(choose(entry(table_ref, FROM_LEFT), loads(came, 0)), pairs)
    right = unfold(choose(entry(table_ref, FROM_RIGHT), loads(came, 1)), pairs)
    left_ref[...] = either(now, lambda: old_left_ref[...], lambda: left)
    right_ref[...] = either(now, lambda: old_right_ref[...], lambda: right)
    rows_apply(bac_ref, split_terms(right_ref[...], extent), mixed_ref, extent)
    diagonals = block_diagonals(split_terms(left_ref[...], extent), extent)
    out_ref[...] = contract(apply_lanes(tall(cba_ref), diagonals, extent), mixed_ref, extent)


def top_kernel(
    came_ref, abc_ref, bac_ref, turned_ref, field_ref, old_left_ref, old_right_ref, table_ref,
    sides_ref, out_ref, mixed_ref,
):
    extent = bac_ref.shape[0]
    now = entry(table_ref, DEPTH) == 0
    diagonals = block_diagonals(split_terms(field_ref[...], extent), extent)
    left_lanes = apply_lanes(tall(abc_ref), diagonals, extent)
    pairs = old_left_ref.shape[0] // extent
    sides_ref[0] = either(now, lambda: old_left_ref[...], lambda: unfold(came_ref[0], pairs))
    sides_ref[1] = either(now, lambda: old_right_ref[...], lambda: unfold(came_ref[1], pairs))
    mix(turned_ref, sides_ref, mixed_ref)
    out_ref[0] = contract(left_lanes, mixed_ref.at[0], extent)
    out_ref[1] = contract(apply_lanes(tall(bac_ref), diagonals, extent), mixed_ref.at[1], extent)


def below_top_kernel(
    came_ref, abc_ref, bac_ref, turned_ref, old_ref, sides_ref, table_ref,
    field_ref, out_ref, mixed_ref,
):
    position = entry(table_ref, POSITION)
    came = unfold(either(position == 2, *[f for side in range(2) for f in loads([came_ref], side)]), old_ref.shape[0] // abc_ref.shape[0])
    now = jnp.logical_or(position == 1, position == 2)
    field_ref[...] = either(now, lambda: old_ref[...], lambda: came)
    mix(turned_ref, sides_ref, mixed_ref)
    spread_down(abc_ref, bac_ref, field_ref, out_ref, mixed_ref)


def down_kernel(depth, *refs):
    came, (abc_ref, bac_ref, old_ref, mixed_ref, table_ref) = refs[:LOW], refs[LOW : LOW + 5]
    field_ref, out_ref = refs[LOW + 5 :]
    arrive(depth, old_ref.shape[0] // abc_ref.shape[0], came, old_ref, table_ref, field_ref)
    spread_down(abc_ref, bac_ref, field_ref, out_ref, mixed_ref)


def arrive(depth, pairs, came, old_ref, table_ref, field_ref):
    arrived = choose(entry(table_ref, FROM_PARENT), loads(came))
    arrived = unfold(arrived, pairs)
    field_ref[...] = either(entry(table_ref, DEPTH) == depth, lambda: old_ref[...], lambda: arrived)


def mix(turned_ref, sides_ref, mixed_ref):
    extent = turned_ref.shape[1]
    rows_apply(turned_ref.at[0], split_terms(sides_ref[1], extent), mixed_ref.at[0], extent)
    rows_apply(turned_ref.at[1], split_terms(sides_ref[0], extent), mixed_ref.at[1], extent)


def spread_down(abc_ref, bac_ref, field_ref, out_ref, mixed_ref):
    extent = bac_ref.shape[0]
    diagonals = block_diagonals(split_terms(field_ref[...], extent), extent)
    out_ref[0] = contract(apply_lanes(tall(abc_ref), diagonals, extent), mixed_ref.at[0], extent)
    out_ref[1] = contract(apply_lanes(tall(bac_ref), diagonals, extent), mixed_ref.at[1], extent)


def weigh_kernel(pair, bac_ref, sides_ref, table_ref, out_ref, spread_ref):
    extent = bac_ref.shape[0]
    mine = slice(pair * extent, (pair + 1) * extent)
    rows_out = out_ref.shape[1]
    per = LANES // extent
    half = extent // per
    rows_spread(bac_ref, split_terms(sides_ref[1, mine], extent), spread_ref, extent)
    rows = lax.rem(iota((LANES, extent), 0), extent)
    lanes = iota((LANES, extent), 1)
    wanted = per * lax.rem(lanes, half) + lax.div(lanes, half)
    pick = jnp.where(rows == wanted, 1.0, 0.0).astype(jnp.bfloat16)
    group = lax.div(iota((half, LANES), 1), extent)
    for term, mat in enumerate(split_terms(sides_ref[0, mine], extent)):
        permuted = dot(mat, pick)
        kept = permuted[:rows_out]
        for g in range(1, extent // rows_out):
            kept = jnp.where(entry(table_ref, GROUP)[:, :extent] == g, permuted[g * rows_out : (g + 1) * rows_out], kept)
        kept = kept.astype(jnp.bfloat16)
        tiles = []
        for j in range(extent // per):
            given = [spread_ref[term, pl.ds((per * j + q) * (half + SKEW), half), :] for q in range(per)]
            stacked = []
            for p in range(per):
                row = None
                for q in range(per):
                    shift = (q - p) * extent % LANES
                    moved = pltpu.roll(given[q], shift, 1) if shift else given[q]
                    row = moved if row is None else jnp.where(group == q, moved, row)
                stacked.append(row)
            tiles.append(jnp.concatenate(stacked, axis=0).astype(jnp.bfloat16))
        for j in range(0, len(tiles), WIDE // LANES):
            wide = jnp.concatenate(tiles[j : j + WIDE // LANES], axis=1)
            out_ref[term, :, j * LANES : j * LANES + WIDE] = dot(kept, wide).astype(jnp.bfloat16)


def last_kernel(depth, pairs, *refs):
    came, (old_ref, table_ref, field_ref) = refs[:LOW], refs[LOW:]
    arrive(depth, pairs, came, old_ref, table_ref, field_ref)


def part_kernel(field_ref, *refs):
    out_ref = refs[-1]
    width = refs[0].shape[2]
    out_ref[...] = weighted_sum(refs[:-1], field_ref[...], math.isqrt(width)).astype(jnp.bfloat16)


def finish_kernel(groups, own_ref, *refs):
    table_ref, out_ref = refs[-2:]
    rows, width = out_ref.shape[1:]
    total = own_ref[...].astype(jnp.float32)
    fields, weighed = refs[: groups - 1], refs[groups - 1 : -2]
    for g, field_ref in enumerate(fields):
        pairs = len(weighed) // len(fields)
        part = weighted_sum(weighed[g * pairs : (g + 1) * pairs], field_ref[...], math.isqrt(width))
        total = total + part.astype(jnp.bfloat16).astype(jnp.float32)
    real = jnp.concatenate([entry(table_ref, DEPTH)] * (WIDE // LANES), axis=1) >= 0
    total = jnp.where(real, total, 0.0).astype(jnp.bfloat16)
    for j in range(width // WIDE):
        out_ref[0, :, j * WIDE : (j + 1) * WIDE] = total[j * rows : (j + 1) * rows]


def weighted_sum(weighed_refs, field, extent):
    per, _, width = weighed_refs[0].shape
    quads = WIDE // extent
    copies = pick_rows(LANES, WIDE, extent)
    spread = dot(jnp.concatenate(split_terms(field, extent), axis=0), copies)
    same = lax.div(iota((WIDE, WIDE), 0), extent) == lax.div(iota((WIDE, WIDE), 1), extent)
    total = None
    for term in range(per * len(weighed_refs)):
        weighed_ref = weighed_refs[term // per]
        block = spread[term * extent : (term + 1) * extent]
        diagonal = jnp.where(same, jnp.concatenate([block] * quads, axis=0), 0.0).astype(jnp.bfloat16)
        pieces = [weighed_ref[term % per, :, j : j + WIDE] for j in range(0, width, WIDE)]
        part = dot(jnp.concatenate(pieces, axis=0), diagonal)
        total = part if total is None else total + part
    return total


def pick_rows(rows, lanes, extent):
    same = lax.rem(iota((rows, lanes), 0), extent) == lax.rem(iota((rows, lanes), 1), extent)
    return jnp.where(same, 1.0, 0.0).astype(jnp.bfloat16)


VMEM = pl.BlockSpec(memory_space=pltpu.VMEM)
SMEM = pl.BlockSpec(memory_space=pltpu.SMEM)
HBM = pl.BlockSpec(memory_space=pltpu.HBM)


def call(kernel, out_shape, *operands, scratch=(), smem_out=(), in_hbm=(), kept=True, in_vmem=False, beside=()):
    shapes = out_shape if isinstance(out_shape, list) else [out_shape]
    specs = [SMEM if i in smem_out else VMEM for i in range(len(shapes))]
    taken = [VMEM] * len(operands)
    operands = list(operands)
    for i, operand in enumerate(operands):
        if i in in_hbm:
            taken[i] = HBM
            operands[i] = pltpu.with_memory_space_constraint(operand, pltpu.HBM)
        elif operand.size >= KEPT:
            operands[i] = pltpu.with_memory_space_constraint(operand, pltpu.VMEM)
    shapes = [pltpu.VMEM(x.shape, x.dtype) if in_vmem or (kept and x.size >= KEPT) else x for x in shapes]
    given = len(operands)
    operands += [pltpu.with_memory_space_constraint(x, pltpu.VMEM) for x in beside]

    def without(*refs):
        kernel(*refs[:given], *refs[len(operands) :])

    return pl.pallas_call(
        without,
        out_shape=shapes if isinstance(out_shape, list) else shapes[0],
        in_specs=taken + [VMEM] * len(beside),
        out_specs=specs if isinstance(out_shape, list) else specs[0],
        scratch_shapes=list(scratch),
        compiler_params=pltpu.CompilerParams(vmem_limit_bytes=16 * 2**20),
    )(*operands)


def exchange(value, mask, nodes):
    return lax.ppermute(value, "node", [(i, i ^ mask) for i in range(nodes)])


def high_exchange(value, nodes):
    return [value] + [exchange(value, high * LOW, nodes) for high in range(1, nodes // LOW)]


def low_exchange(values, nodes):
    return [values[0]] + [exchange(values[j], j, nodes) for j in range(1, LOW)]


def per_device(node_tensors, prim_ops, active, top_field, node_map):
    nodes = lax.axis_size("node")
    groups = lax.axis_size("term")
    depths = nodes.bit_length() - 1
    turned_active = jnp.swapaxes(active, 1, 2)

    extent = node_tensors.shape[1]
    terms = prim_ops.shape[1]
    pairs = terms * extent // LANES
    flat = jax.ShapeDtypeStruct((extent, extent * extent), jnp.bfloat16)
    mats = jax.ShapeDtypeStruct((pairs * extent, LANES), jnp.bfloat16)
    two = jax.ShapeDtypeStruct((2,) + mats.shape, jnp.bfloat16)
    message = jax.ShapeDtypeStruct((-(-pairs // 2) * (extent + PAD), LANES), jnp.bfloat16)
    messages = jax.ShapeDtypeStruct((2,) + message.shape, jnp.bfloat16)
    table_shape = jax.ShapeDtypeStruct((TABLE, LANES), jnp.int32)
    spread = jax.ShapeDtypeStruct((terms, extent * extent * extent // LANES, LANES), jnp.bfloat16)
    part = jax.ShapeDtypeStruct((LANES // extent, extent // groups, extent * extent), jnp.bfloat16)
    per = LANES // extent
    space = pltpu.VMEM((per, extent * (extent // per + SKEW) + extent, LANES), jnp.float32)
    both = [pltpu.VMEM((2,) + spread.shape, jnp.bfloat16)]
    mixed_space = pltpu.VMEM(spread.shape, jnp.bfloat16)
    turn_space = pltpu.VMEM((extent // per * (extent + SKEW) + extent, LANES), jnp.float32)

    def others(value):
        return [
            lax.ppermute(value, "term", [(i, (i + shift) % groups) for i in range(groups)]) for shift in range(1, groups)
        ]

    def weigh_beside(count, values):
        first = len(weighed)
        for sides, pair in to_weigh[first : first + count]:
            weighed.append(call(functools.partial(weigh_kernel, pair), part, bac, sides, table, scratch=[space]))
        values, weighed[first:] = lax.optimization_barrier((values, weighed[first:]))
        return values

    def with_top(first, second):
        def branch(mask):
            def go(first, second):
                came = exchange(first, nodes // 2, nodes), exchange(second, mask, nodes)
                return call(both_kernel, messages, *came, in_vmem=True)

            return go

        return lax.switch(apart[0], [branch(mask) for mask in range(1, nodes)], first, second)

    abc, bac, cba, left, right, field, mine, table = call(
        start_kernel,
        [flat, flat, flat, mats, mats, mats, message, table_shape],
        node_tensors,
        prim_ops,
        turned_active,
        top_field,
        node_map,
        scratch=[
            pltpu.VMEM(prim_ops.shape, jnp.bfloat16),
            pltpu.SMEM(turned_active.shape, jnp.int32),
            pltpu.VMEM(top_field.shape, jnp.bfloat16),
            pltpu.SMEM(node_map.shape, jnp.int32),
            mixed_space,
            turn_space,
            pltpu.SMEM((nodes,), jnp.int32),
            pltpu.SemaphoreType.DMA((5,)),
        ],
        in_hbm=(0, 1, 2, 3, 4),
    )
    for depth in range(depths - 2, 0, -1):
        parts = high_exchange(mine, nodes)
        came = low_exchange(call(relay_up_kernel, [messages] * LOW, *parts, table), nodes)
        if depth == depths - 2:
            turned, apart = call(
                turn_kernel,
                [jax.ShapeDtypeStruct((2,) + flat.shape, flat.dtype), jax.ShapeDtypeStruct((1,), jnp.int32)],
                bac,
                cba,
                table,
                scratch=[turn_space],
                smem_out=(1,),
            )
            came, turned, apart = lax.optimization_barrier((came, turned, apart))
        left, right, mine = call(
            functools.partial(up_kernel, depth),
            [mats, mats, message],
            *came,
            bac,
            cba,
            left,
            right,
            table,
            scratch=[mixed_space],
        )

    came = pltpu.with_memory_space_constraint(with_top(mine, mine), pltpu.VMEM)
    sides, fields = call(
        top_kernel,
        [two, messages],
        came,
        abc,
        bac,
        turned,
        field,
        left,
        right,
        table,
        scratch=both,
    )
    came = pltpu.with_memory_space_constraint(with_top(fields[0], fields[1]), pltpu.VMEM)
    to_weigh = [(each, pair) for each in [sides] + others(sides) for pair in range(pairs)]
    share = -(-len(to_weigh) // (1 + 3 * (depths - 3)))
    field, fields = call(
        below_top_kernel,
        [mats, messages],
        came,
        abc,
        bac,
        turned,
        field,
        sides,
        table,
        scratch=both,
    )
    weighed = []
    for depth in range(2, depths):
        parts = high_exchange(fields, nodes)
        if depth == 2:
            ahead = jax.ShapeDtypeStruct((2,) + spread.shape, spread.dtype)
            parts, mixed = lax.optimization_barrier((parts, call(mix, ahead, turned, sides)))
        else:
            parts = weigh_beside(2 * share, parts)
        came = low_exchange(call(relay_down_kernel, [message] * LOW, *parts, table), nodes)
        came = weigh_beside(share, came)
        if depth < depths - 1:
            field, fields = call(
                functools.partial(down_kernel, depth),
                [mats, messages],
                *came,
                abc,
                bac,
                field,
                mixed,
                table,
            )
    field = call(functools.partial(last_kernel, depths - 1, pairs), mats, *came, field, table)
    out = jax.ShapeDtypeStruct((1, extent // groups, extent * extent), jnp.bfloat16)
    tall_part = jax.ShapeDtypeStruct((extent * extent * extent // groups // WIDE, WIDE), jnp.bfloat16)
    fields = others(field)
    own = call(part_kernel, tall_part, field, *weighed[:pairs], kept=False)
    own, fields = lax.optimization_barrier((own, fields))
    rest = weighed[pairs:]
    return call(functools.partial(finish_kernel, groups), out, own, *fields, *rest, table, kept=False)


def solution(mesh):
    placed = (
        P("node", None, None),
        P("node", "term", None, None, None),
        P("node", "term", None),
        P("term", None, None),
        P(),
    )
    return jax.shard_map(
        per_device, mesh=mesh, in_specs=placed, out_specs=P("node", "term", None), check_vma=False
    )
```

```python
import functools
import math

import jax
import jax.numpy as jnp
from jax import lax
from jax.experimental import pallas as pl
from jax.experimental.pallas import tpu as pltpu
from jax.sharding import PartitionSpec as P

LANES = 128
WIDE = 256
BATCH = 2
PAD = 16
SKEW = 8
KEPT = 2**18


def dot(left, right):
    return jnp.dot(left, right, preferred_element_type=jnp.float32)


def iota(shape, dim):
    return lax.broadcasted_iota(jnp.int32, shape, dim)


def split_terms(packed, extent):
    per = LANES // extent
    wide = packed.astype(jnp.float32)
    out = []
    for term in range(per * packed.shape[0] // extent):
        block = wide[(term // per) * extent : (term // per + 1) * extent]
        mine = lax.div(iota(block.shape, 1), extent) == term % per
        out.append(jnp.where(mine, block, 0.0).astype(jnp.bfloat16))
    return out


def rows_spread(tensor_ref, mats, spread_ref, extent):
    per = LANES // extent
    half = extent // per
    stack = jnp.concatenate(mats, axis=0)
    for chunk in range(extent * extent // WIDE):
        piece = tensor_ref[:, chunk * WIDE : (chunk + 1) * WIDE]
        result = dot(stack, jnp.concatenate([piece] * per, axis=0))
        for part in range(WIDE // LANES):
            i = chunk * (WIDE // LANES) + part
            for term in range(len(mats)):
                spread_ref[term, pl.ds(i, extent, stride=half + SKEW), :] = result[
                    term * extent : (term + 1) * extent, part * LANES : (part + 1) * LANES
                ]


SUB = 8


def rows_apply(tensor_ref, mats, mixed_ref, extent):
    per = LANES // extent
    quads = WIDE // extent
    halves = SUB // quads
    count = 2 * halves
    stack = jnp.concatenate(mats, axis=0)
    row = iota((extent // SUB, SUB, LANES), 1)
    for first in range(0, extent // per, count):
        piece = tensor_ref[:, first * LANES : (first + count) * LANES]
        result = dot(stack, jnp.concatenate([piece] * per, axis=0))
        for term in range(len(mats)):
            tiles = [
                result[term * extent : (term + 1) * extent, k * LANES : (k + 1) * LANES].reshape(row.shape)
                for k in range(count)
            ]
            for half in range(halves):
                wanted = []
                for start in range(0, count, halves):
                    block = None
                    for k in range(halves):
                        shift = (k - half) * quads % SUB
                        moved = pltpu.roll(tiles[start + k], shift, 1) if shift else tiles[start + k]
                        block = moved if block is None else jnp.where(lax.div(row, quads) == k, moved, block)
                    wanted.append(block)
                packed = jnp.concatenate(wanted, axis=1).astype(jnp.bfloat16)
                for m in range(extent // SUB):
                    base = (m * halves + half) * (extent // per) * quads + first * quads
                    mixed_ref[term, base : base + count * quads, :] = packed[m]


def block_diagonals(mats, extent):
    per = LANES // extent
    quads = WIDE // extent
    rows = lax.rem(iota((LANES, WIDE), 0), extent)
    lanes = iota((LANES, WIDE), 1)
    wanted = per * lax.div(lax.rem(lanes, WIDE // per), quads) + lax.div(lanes, WIDE // per)
    pick = jnp.where(rows == wanted, 1.0, 0.0).astype(jnp.bfloat16)
    spread = dot(jnp.concatenate(mats, axis=0), pick)
    lanes = iota((WIDE, WIDE), 1)
    same = lax.div(iota((WIDE, WIDE), 0), extent) == lax.rem(lanes, quads)
    out = []
    for term in range(len(mats)):
        block = spread[term * extent : (term + 1) * extent]
        out.append(jnp.where(same, jnp.concatenate([block] * quads, axis=0), 0.0).astype(jnp.bfloat16))
    return out


def tall(tensor_ref):
    width = tensor_ref.shape[1]
    return jnp.concatenate([tensor_ref[:, j : j + WIDE] for j in range(0, width, WIDE)], axis=0)


def pair_up(accs, extent):
    per = LANES // extent
    out = []
    for first in range(0, len(accs), per):
        blocks = None
        for lo in range(per):
            acc = accs[first + lo]
            group = lax.div(iota((extent, LANES), 1), extent)
            kept = jnp.zeros((extent, LANES), jnp.float32)
            for p in range(per):
                kept = jnp.where(group == p, acc[p * extent : (p + 1) * extent], kept)
            total = kept
            for p in range(1, per):
                total = total + pltpu.roll(kept, p * extent, 1)
            blocks = total if blocks is None else jnp.where(group == lo, total, blocks)
        out.append(blocks)
    return out


def below_diagonal(shape, extent):
    rows, lanes = iota(shape, 0), lax.rem(iota(shape, 1), extent)
    return rows > lanes, rows == lanes


def fold(blocks):
    extent = blocks[0].shape[0]
    below, on = below_diagonal(blocks[0].shape, extent)
    out = []
    for first in range(0, len(blocks), 2):
        lower, upper = blocks[first], blocks[min(first + 1, len(blocks) - 1)]
        out.append(jnp.where(jnp.logical_or(below, on), lower, upper))
        row = jnp.sum(jnp.where(on, upper, 0.0), axis=0, keepdims=True)
        out.append(jnp.broadcast_to(row, (PAD, LANES)))
    return jnp.concatenate(out, axis=0).astype(jnp.bfloat16)


def unfold(message, pairs):
    height = message.shape[0] // (-(-pairs // 2))
    extent = height - PAD
    wide = message.astype(jnp.float32)
    out = []
    for base in range(0, message.shape[0], height):
        body, row = wide[base : base + extent], wide[base + extent : base + extent + 1]
        below, on = below_diagonal(body.shape, extent)
        turned = body.T
        parts = [turned[k : k + extent] for k in range(0, LANES, extent)]
        turned = jnp.concatenate(parts, axis=1)
        out.append(jnp.where(jnp.logical_or(below, on), body, turned))
        out.append(jnp.where(below, turned, jnp.where(on, row, body)))
    return jnp.concatenate(out[:pairs], axis=0).astype(jnp.bfloat16)


def apply_lanes(stacked, diagonals, extent):
    per = LANES // extent
    groups = stacked.shape[0] // extent
    lefts = []
    for diagonal in diagonals:
        moved = dot(stacked, diagonal).astype(jnp.bfloat16)
        for p in range(per):
            lanes = slice(p * (WIDE // per), (p + 1) * (WIDE // per))
            lefts.append(jnp.concatenate([moved[j * extent : (j + 1) * extent, lanes] for j in range(groups)], axis=1))
    return lefts


def contract(lefts, mixed, extent):
    per = LANES // extent
    accs = []
    for first in range(0, len(lefts) // per, BATCH):
        left = jnp.concatenate(lefts[first * per : (first + BATCH) * per], axis=0)
        right = jnp.concatenate([mixed[term] for term in range(first, first + BATCH)], axis=1)
        result = dot(left, right)
        for k in range(BATCH):
            accs.append(result[k * LANES : (k + 1) * LANES, k * LANES : (k + 1) * LANES])
    return fold(pair_up(accs, extent))


def swap(value, turn_ref, out_ref, extent):
    per = LANES // extent
    half = extent // per
    rows = iota((extent, extent), 0)
    wanted = per * lax.rem(rows, half) + lax.div(rows, half)
    order = jnp.where(iota((extent, extent), 1) == wanted, 1.0, 0.0).astype(jnp.bfloat16)
    sorted_rows = dot(order, value)
    group = lax.div(iota((half, LANES), 1), extent)
    for j in range(extent // per):
        given = [sorted_rows[p * half : (p + 1) * half, j * LANES : (j + 1) * LANES] for p in range(per)]
        for q in range(per):
            row = None
            for p in range(per):
                shift = (p - q) * extent % LANES
                moved = pltpu.roll(given[p], shift, 1) if shift else given[p]
                row = moved if row is None else jnp.where(group == p, moved, row)
            turn_ref[pl.ds(per * j + q, half, stride=extent + SKEW), :] = row
    for i in range(half):
        out_ref[:, i * LANES : (i + 1) * LANES] = turn_ref[pl.ds(i * (extent + SKEW), extent), :].astype(jnp.bfloat16)


def flip(value, extent):
    per = LANES // extent
    wide = value.astype(jnp.float32)
    tiles = []
    for j in range(extent // per):
        turned = wide[:, j * LANES : (j + 1) * LANES].T
        tiles.append(jnp.concatenate([turned[p * extent : (p + 1) * extent] for p in range(per)], axis=1))
    return jnp.concatenate(tiles, axis=1).astype(jnp.bfloat16)


DEPTH, FROM_LEFT, FROM_RIGHT, FROM_PARENT, POSITION, GROUP, APART, UP_RELAY, DOWN_RELAY, TABLE = *range(7), 8, 16, 24
LOW = 4


def entry(table_ref, row):
    return table_ref[row : row + 1, :]


def fill_table(map_ref, me, inverse_ref, table_ref):
    def put(row, value):
        table_ref[row : row + 1, :] = jnp.full((1, LANES), value, jnp.int32)

    nodes = map_ref.shape[0]

    def note(slot, carry):
        inverse_ref[map_ref[slot]] = slot
        return carry

    lax.fori_loop(0, nodes, note, 0)
    low = lax.rem(me, LOW)
    high = lax.div(me, LOW)

    def routes(slot):
        position = map_ref[slot]
        last = jnp.int32(nodes - 1)
        left = inverse_ref[jnp.minimum(2 * position + 1, last)]
        right = inverse_ref[jnp.minimum(2 * position + 2, last)]
        parent = inverse_ref[lax.div(jnp.maximum(position - 1, 0), 2)]
        return position, left, right, parent

    position, left, right, parent = routes(me)
    depth = jnp.int32(0)
    for power in range(1, nodes.bit_length() - 1):
        depth = depth + jnp.where(position + 1 >= 2**power, 1, 0)
    put(DEPTH, jnp.where(position >= nodes - 1, -1, depth))
    put(POSITION, position)
    put(GROUP, lax.axis_index("term"))
    put(APART, inverse_ref[0] ^ inverse_ref[2])
    put(FROM_LEFT, lax.rem(left, LOW) ^ low)
    put(FROM_RIGHT, lax.rem(right, LOW) ^ low)
    put(FROM_PARENT, lax.rem(parent, LOW) ^ low)
    for j in range(LOW):
        position, left, right, parent = routes(high * LOW + (low ^ j))
        put(UP_RELAY + 2 * j, lax.div(left, LOW) ^ high)
        put(UP_RELAY + 2 * j + 1, lax.div(right, LOW) ^ high)
        put(DOWN_RELAY + j, 2 * (lax.div(parent, LOW) ^ high) + lax.rem(position + 1, 2))


def choose(index, choices):
    out = choices[0]().astype(jnp.float32)
    for k in range(1, len(choices)):
        out = jnp.where(index == k, choices[k]().astype(jnp.float32), out)
    return out.astype(jnp.bfloat16)


def either(mask, old, new):
    return choose(jnp.where(mask, 1, 0), [old, new])


def loads(refs, *where):
    return [lambda ref=ref: ref[where] if where else ref[...] for ref in refs]


def start_kernel(
    tensor_hbm, prim_hbm, active_hbm, top_hbm, map_hbm,
    abc_ref, bac_ref, cba_ref, left_ref, right_ref, field_ref, out_ref, table_ref,
    prim_ref, active_ref, top_ref, map_ref, mixed_ref, turn_ref, inverse_ref, sems,
):
    given = (tensor_hbm.at[0], prim_hbm, top_hbm, active_hbm, map_hbm)
    held = (abc_ref, prim_ref, top_ref, active_ref, map_ref)
    copies = [pltpu.make_async_copy(*pair, sems.at[i]) for i, pair in enumerate(zip(given, held))]
    for copy in copies:
        copy.start()
    extent = abc_ref.shape[0]
    per = LANES // extent
    terms = prim_ref.shape[1]
    for copy in copies[:0:-1]:
        copy.wait()
        if copy is copies[-1]:
            fill_table(map_ref, lax.axis_index("node"), inverse_ref, table_ref)
    eye = jnp.where(iota((extent, extent), 0) == iota((extent, extent), 1), 1.0, 0.0)

    def operator(term, side):
        return jnp.where(active_ref[0, side, term] == 1, prim_ref[0, term, side].astype(jnp.float32), eye)

    for first in range(0, terms, per):
        rows = pl.ds(first // per * extent, extent)
        for side, ref in ((0, left_ref), (1, right_ref)):
            side_by_side = [operator(first + lo, side) for lo in range(per)]
            ref[rows, :] = jnp.concatenate(side_by_side, axis=1).astype(jnp.bfloat16)
        fields = [top_ref[first + lo].astype(jnp.float32) for lo in range(per)]
        field_ref[rows, :] = jnp.concatenate(fields, axis=1).astype(jnp.bfloat16)
    diagonals = block_diagonals(split_terms(left_ref[...], extent), extent)
    copies[0].wait()
    swap(abc_ref[...], turn_ref, bac_ref, extent)
    cba_ref[...] = flip(abc_ref[...], extent)
    rows_apply(bac_ref, split_terms(right_ref[...], extent), mixed_ref, extent)
    out_ref[...] = contract(apply_lanes(tall(cba_ref), diagonals, extent), mixed_ref, extent)


def turn_kernel(bac_ref, cba_ref, table_ref, turned_ref, apart_ref, turn_ref):
    extent = bac_ref.shape[0]
    apart_ref[0] = jnp.max(entry(table_ref, APART)) - 1
    swap(cba_ref[...], turn_ref, turned_ref.at[0], extent)
    swap(flip(bac_ref[...], extent), turn_ref, turned_ref.at[1], extent)


def both_kernel(first_ref, second_ref, out_ref):
    out_ref[0] = first_ref[...]
    out_ref[1] = second_ref[...]


def relay_up_kernel(*refs):
    parts, table_ref, outs = refs[:-5], refs[-5], refs[-4:]
    for j, out in enumerate(outs):
        for side in range(2):
            out[side] = choose(entry(table_ref, UP_RELAY + 2 * j + side), loads(parts))


def relay_down_kernel(*refs):
    parts, table_ref, outs = refs[:-5], refs[-5], refs[-4:]
    choices = [f for part in parts for side in range(2) for f in loads([part], side)]
    for j, out in enumerate(outs):
        out[...] = choose(entry(table_ref, DOWN_RELAY + j), choices)


def up_kernel(depth, *refs):
    came, (bac_ref, cba_ref, old_left_ref, old_right_ref, table_ref) = refs[:LOW], refs[LOW : LOW + 5]
    left_ref, right_ref, out_ref, mixed_ref = refs[LOW + 5 :]
    extent = bac_ref.shape[0]
    now = entry(table_ref, DEPTH) == depth
    pairs = old_left_ref.shape[0] // extent
    left = unfold(choose(entry(table_ref, FROM_LEFT), loads(came, 0)), pairs)
    right = unfold(choose(entry(table_ref, FROM_RIGHT), loads(came, 1)), pairs)
    left_ref[...] = either(now, lambda: old_left_ref[...], lambda: left)
    right_ref[...] = either(now, lambda: old_right_ref[...], lambda: right)
    rows_apply(bac_ref, split_terms(right_ref[...], extent), mixed_ref, extent)
    diagonals = block_diagonals(split_terms(left_ref[...], extent), extent)
    out_ref[...] = contract(apply_lanes(tall(cba_ref), diagonals, extent), mixed_ref, extent)


def top_kernel(
    came_ref, abc_ref, bac_ref, turned_ref, field_ref, old_left_ref, old_right_ref, table_ref,
    sides_ref, out_ref, mixed_ref,
):
    extent = bac_ref.shape[0]
    now = entry(table_ref, DEPTH) == 0
    diagonals = block_diagonals(split_terms(field_ref[...], extent), extent)
    left_lanes = apply_lanes(tall(abc_ref), diagonals, extent)
    pairs = old_left_ref.shape[0] // extent
    sides_ref[0] = either(now, lambda: old_left_ref[...], lambda: unfold(came_ref[0], pairs))
    sides_ref[1] = either(now, lambda: old_right_ref[...], lambda: unfold(came_ref[1], pairs))
    mix(turned_ref, sides_ref, mixed_ref)
    out_ref[0] = contract(left_lanes, mixed_ref.at[0], extent)
    out_ref[1] = contract(apply_lanes(tall(bac_ref), diagonals, extent), mixed_ref.at[1], extent)


def below_top_kernel(
    came_ref, abc_ref, bac_ref, turned_ref, old_ref, sides_ref, table_ref,
    field_ref, out_ref, mixed_ref,
):
    position = entry(table_ref, POSITION)
    came = unfold(either(position == 2, *[f for side in range(2) for f in loads([came_ref], side)]), old_ref.shape[0] // abc_ref.shape[0])
    now = jnp.logical_or(position == 1, position == 2)
    field_ref[...] = either(now, lambda: old_ref[...], lambda: came)
    mix(turned_ref, sides_ref, mixed_ref)
    spread_down(abc_ref, bac_ref, field_ref, out_ref, mixed_ref)


def down_kernel(depth, *refs):
    came, (abc_ref, bac_ref, old_ref, mixed_ref, table_ref) = refs[:LOW], refs[LOW : LOW + 5]
    field_ref, out_ref = refs[LOW + 5 :]
    arrive(depth, old_ref.shape[0] // abc_ref.shape[0], came, old_ref, table_ref, field_ref)
    spread_down(abc_ref, bac_ref, field_ref, out_ref, mixed_ref)


def arrive(depth, pairs, came, old_ref, table_ref, field_ref):
    arrived = choose(entry(table_ref, FROM_PARENT), loads(came))
    arrived = unfold(arrived, pairs)
    field_ref[...] = either(entry(table_ref, DEPTH) == depth, lambda: old_ref[...], lambda: arrived)


def mix(turned_ref, sides_ref, mixed_ref):
    extent = turned_ref.shape[1]
    rows_apply(turned_ref.at[0], split_terms(sides_ref[1], extent), mixed_ref.at[0], extent)
    rows_apply(turned_ref.at[1], split_terms(sides_ref[0], extent), mixed_ref.at[1], extent)


def spread_down(abc_ref, bac_ref, field_ref, out_ref, mixed_ref):
    extent = bac_ref.shape[0]
    diagonals = block_diagonals(split_terms(field_ref[...], extent), extent)
    out_ref[0] = contract(apply_lanes(tall(abc_ref), diagonals, extent), mixed_ref.at[0], extent)
    out_ref[1] = contract(apply_lanes(tall(bac_ref), diagonals, extent), mixed_ref.at[1], extent)


def weigh_kernel(pair, bac_ref, sides_ref, table_ref, out_ref, spread_ref):
    extent = bac_ref.shape[0]
    mine = slice(pair * extent, (pair + 1) * extent)
    rows_out = out_ref.shape[1]
    per = LANES // extent
    half = extent // per
    rows_spread(bac_ref, split_terms(sides_ref[1, mine], extent), spread_ref, extent)
    rows = lax.rem(iota((LANES, extent), 0), extent)
    lanes = iota((LANES, extent), 1)
    wanted = per * lax.rem(lanes, half) + lax.div(lanes, half)
    pick = jnp.where(rows == wanted, 1.0, 0.0).astype(jnp.bfloat16)
    group = lax.div(iota((half, LANES), 1), extent)
    for term, mat in enumerate(split_terms(sides_ref[0, mine], extent)):
        permuted = dot(mat, pick)
        kept = permuted[:rows_out]
        for g in range(1, extent // rows_out):
            kept = jnp.where(entry(table_ref, GROUP)[:, :extent] == g, permuted[g * rows_out : (g + 1) * rows_out], kept)
        kept = kept.astype(jnp.bfloat16)
        tiles = []
        for j in range(extent // per):
            given = [spread_ref[term, pl.ds((per * j + q) * (half + SKEW), half), :] for q in range(per)]
            stacked = []
            for p in range(per):
                row = None
                for q in range(per):
                    shift = (q - p) * extent % LANES
                    moved = pltpu.roll(given[q], shift, 1) if shift else given[q]
                    row = moved if row is None else jnp.where(group == q, moved, row)
                stacked.append(row)
            tiles.append(jnp.concatenate(stacked, axis=0).astype(jnp.bfloat16))
        for j in range(0, len(tiles), WIDE // LANES):
            wide = jnp.concatenate(tiles[j : j + WIDE // LANES], axis=1)
            out_ref[term, :, j * LANES : j * LANES + WIDE] = dot(kept, wide).astype(jnp.bfloat16)


def last_kernel(depth, pairs, *refs):
    came, (old_ref, table_ref, field_ref, message_ref) = refs[:LOW], refs[LOW:]
    arrive(depth, pairs, came, old_ref, table_ref, field_ref)
    wide = field_ref[...].astype(jnp.float32)
    extent = wide.shape[0] // pairs
    message_ref[...] = fold([wide[k * extent : (k + 1) * extent] for k in range(pairs)])


def part_kernel(field_ref, *refs):
    out_ref = refs[-1]
    width = refs[0].shape[2]
    out_ref[...] = weighted_sum(refs[:-1], field_ref[...], math.isqrt(width)).astype(jnp.bfloat16)


def finish_kernel(groups, own_ref, *refs):
    table_ref, out_ref = refs[-2:]
    rows, width = out_ref.shape[1:]
    total = own_ref[...].astype(jnp.float32)
    fields, weighed = refs[: groups - 1], refs[groups - 1 : -2]
    for g, field_ref in enumerate(fields):
        pairs = len(weighed) // len(fields)
        part = weighted_sum(weighed[g * pairs : (g + 1) * pairs], unfold(field_ref[...], pairs), math.isqrt(width))
        total = total + part.astype(jnp.bfloat16).astype(jnp.float32)
    real = jnp.concatenate([entry(table_ref, DEPTH)] * (WIDE // LANES), axis=1) >= 0
    total = jnp.where(real, total, 0.0).astype(jnp.bfloat16)
    for j in range(width // WIDE):
        out_ref[0, :, j * WIDE : (j + 1) * WIDE] = total[j * rows : (j + 1) * rows]


def weighted_sum(weighed_refs, field, extent):
    per, _, width = weighed_refs[0].shape
    quads = WIDE // extent
    copies = pick_rows(LANES, WIDE, extent)
    spread = dot(jnp.concatenate(split_terms(field, extent), axis=0), copies)
    same = lax.div(iota((WIDE, WIDE), 0), extent) == lax.div(iota((WIDE, WIDE), 1), extent)
    total = None
    for term in range(per * len(weighed_refs)):
        weighed_ref = weighed_refs[term // per]
        block = spread[term * extent : (term + 1) * extent]
        diagonal = jnp.where(same, jnp.concatenate([block] * quads, axis=0), 0.0).astype(jnp.bfloat16)
        pieces = [weighed_ref[term % per, :, j : j + WIDE] for j in range(0, width, WIDE)]
        part = dot(jnp.concatenate(pieces, axis=0), diagonal)
        total = part if total is None else total + part
    return total


def pick_rows(rows, lanes, extent):
    same = lax.rem(iota((rows, lanes), 0), extent) == lax.rem(iota((rows, lanes), 1), extent)
    return jnp.where(same, 1.0, 0.0).astype(jnp.bfloat16)


VMEM = pl.BlockSpec(memory_space=pltpu.VMEM)
SMEM = pl.BlockSpec(memory_space=pltpu.SMEM)
HBM = pl.BlockSpec(memory_space=pltpu.HBM)


def call(kernel, out_shape, *operands, scratch=(), smem_out=(), in_hbm=(), kept=True, in_vmem=False, beside=()):
    shapes = out_shape if isinstance(out_shape, list) else [out_shape]
    specs = [SMEM if i in smem_out else VMEM for i in range(len(shapes))]
    taken = [VMEM] * len(operands)
    operands = list(operands)
    for i, operand in enumerate(operands):
        if i in in_hbm:
            taken[i] = HBM
            operands[i] = pltpu.with_memory_space_constraint(operand, pltpu.HBM)
        elif operand.size >= KEPT:
            operands[i] = pltpu.with_memory_space_constraint(operand, pltpu.VMEM)
    shapes = [pltpu.VMEM(x.shape, x.dtype) if in_vmem or (kept and x.size >= KEPT) else x for x in shapes]
    given = len(operands)
    operands += [pltpu.with_memory_space_constraint(x, pltpu.VMEM) for x in beside]

    def without(*refs):
        kernel(*refs[:given], *refs[len(operands) :])

    return pl.pallas_call(
        without,
        out_shape=shapes if isinstance(out_shape, list) else shapes[0],
        in_specs=taken + [VMEM] * len(beside),
        out_specs=specs if isinstance(out_shape, list) else specs[0],
        scratch_shapes=list(scratch),
        compiler_params=pltpu.CompilerParams(vmem_limit_bytes=16 * 2**20),
    )(*operands)


def exchange(value, mask, nodes):
    return lax.ppermute(value, "node", [(i, i ^ mask) for i in range(nodes)])


def high_exchange(value, nodes):
    return [value] + [exchange(value, high * LOW, nodes) for high in range(1, nodes // LOW)]


def low_exchange(values, nodes):
    return [values[0]] + [exchange(values[j], j, nodes) for j in range(1, LOW)]


def per_device(node_tensors, prim_ops, active, top_field, node_map):
    nodes = lax.axis_size("node")
    groups = lax.axis_size("term")
    depths = nodes.bit_length() - 1
    turned_active = jnp.swapaxes(active, 1, 2)

    extent = node_tensors.shape[1]
    terms = prim_ops.shape[1]
    pairs = terms * extent // LANES
    flat = jax.ShapeDtypeStruct((extent, extent * extent), jnp.bfloat16)
    mats = jax.ShapeDtypeStruct((pairs * extent, LANES), jnp.bfloat16)
    two = jax.ShapeDtypeStruct((2,) + mats.shape, jnp.bfloat16)
    message = jax.ShapeDtypeStruct((-(-pairs // 2) * (extent + PAD), LANES), jnp.bfloat16)
    messages = jax.ShapeDtypeStruct((2,) + message.shape, jnp.bfloat16)
    table_shape = jax.ShapeDtypeStruct((TABLE, LANES), jnp.int32)
    spread = jax.ShapeDtypeStruct((terms, extent * extent * extent // LANES, LANES), jnp.bfloat16)
    part = jax.ShapeDtypeStruct((LANES // extent, extent // groups, extent * extent), jnp.bfloat16)
    per = LANES // extent
    space = pltpu.VMEM((per, extent * (extent // per + SKEW) + extent, LANES), jnp.float32)
    both = [pltpu.VMEM((2,) + spread.shape, jnp.bfloat16)]
    mixed_space = pltpu.VMEM(spread.shape, jnp.bfloat16)
    turn_space = pltpu.VMEM((extent // per * (extent + SKEW) + extent, LANES), jnp.float32)

    def others(value):
        return [
            lax.ppermute(value, "term", [(i, (i + shift) % groups) for i in range(groups)]) for shift in range(1, groups)
        ]

    def weigh_beside(count, values):
        first = len(weighed)
        for sides, pair in to_weigh[first : first + count]:
            weighed.append(call(functools.partial(weigh_kernel, pair), part, bac, sides, table, scratch=[space]))
        values, weighed[first:] = lax.optimization_barrier((values, weighed[first:]))
        return values

    def with_top(first, second):
        def branch(mask):
            def go(first, second):
                came = exchange(first, nodes // 2, nodes), exchange(second, mask, nodes)
                return call(both_kernel, messages, *came, in_vmem=True)

            return go

        return lax.switch(apart[0], [branch(mask) for mask in range(1, nodes)], first, second)

    abc, bac, cba, left, right, field, mine, table = call(
        start_kernel,
        [flat, flat, flat, mats, mats, mats, message, table_shape],
        node_tensors,
        prim_ops,
        turned_active,
        top_field,
        node_map,
        scratch=[
            pltpu.VMEM(prim_ops.shape, jnp.bfloat16),
            pltpu.SMEM(turned_active.shape, jnp.int32),
            pltpu.VMEM(top_field.shape, jnp.bfloat16),
            pltpu.SMEM(node_map.shape, jnp.int32),
            mixed_space,
            turn_space,
            pltpu.SMEM((nodes,), jnp.int32),
            pltpu.SemaphoreType.DMA((5,)),
        ],
        in_hbm=(0, 1, 2, 3, 4),
    )
    for depth in range(depths - 2, 0, -1):
        parts = high_exchange(mine, nodes)
        came = low_exchange(call(relay_up_kernel, [messages] * LOW, *parts, table), nodes)
        if depth == depths - 2:
            turned, apart = call(
                turn_kernel,
                [jax.ShapeDtypeStruct((2,) + flat.shape, flat.dtype), jax.ShapeDtypeStruct((1,), jnp.int32)],
                bac,
                cba,
                table,
                scratch=[turn_space],
                smem_out=(1,),
            )
            came, turned, apart = lax.optimization_barrier((came, turned, apart))
        left, right, mine = call(
            functools.partial(up_kernel, depth),
            [mats, mats, message],
            *came,
            bac,
            cba,
            left,
            right,
            table,
            scratch=[mixed_space],
        )

    came = pltpu.with_memory_space_constraint(with_top(mine, mine), pltpu.VMEM)
    sides, fields = call(
        top_kernel,
        [two, messages],
        came,
        abc,
        bac,
        turned,
        field,
        left,
        right,
        table,
        scratch=both,
    )
    came = pltpu.with_memory_space_constraint(with_top(fields[0], fields[1]), pltpu.VMEM)
    to_weigh = [(each, pair) for each in [sides] + others(sides) for pair in range(pairs)]
    share = -(-len(to_weigh) // (1 + 3 * (depths - 3)))
    field, fields = call(
        below_top_kernel,
        [mats, messages],
        came,
        abc,
        bac,
        turned,
        field,
        sides,
        table,
        scratch=both,
    )
    weighed = []
    for depth in range(2, depths):
        parts = high_exchange(fields, nodes)
        if depth == 2:
            ahead = jax.ShapeDtypeStruct((2,) + spread.shape, spread.dtype)
            parts, mixed = lax.optimization_barrier((parts, call(mix, ahead, turned, sides)))
        else:
            parts = weigh_beside(2 * share, parts)
        came = low_exchange(call(relay_down_kernel, [message] * LOW, *parts, table), nodes)
        came = weigh_beside(share, came)
        if depth < depths - 1:
            field, fields = call(
                functools.partial(down_kernel, depth),
                [mats, messages],
                *came,
                abc,
                bac,
                field,
                mixed,
                table,
            )
    field, sent = call(functools.partial(last_kernel, depths - 1, pairs), [mats, message], *came, field, table)
    out = jax.ShapeDtypeStruct((1, extent // groups, extent * extent), jnp.bfloat16)
    tall_part = jax.ShapeDtypeStruct((extent * extent * extent // groups // WIDE, WIDE), jnp.bfloat16)
    fields = others(sent)
    own = call(part_kernel, tall_part, field, *weighed[:pairs], kept=False)
    own, fields = lax.optimization_barrier((own, fields))
    rest = weighed[pairs:]
    return call(functools.partial(finish_kernel, groups), out, own, *fields, *rest, table, kept=False)


def solution(mesh):
    placed = (
        P("node", None, None),
        P("node", "term", None, None, None),
        P("node", "term", None),
        P("term", None, None),
        P(),
    )
    return jax.shard_map(
        per_device, mesh=mesh, in_specs=placed, out_specs=P("node", "term", None), check_vma=False
    )
```
